32 devices in a mesh: groups: 2 (over x), span: 16 (over z, y, core).
Axes of the slice: x: 2, y: 2, z: 4, core: 2. Of those that a mesh axis runs over, the one named last changes fastest.
Arguments:
- queries: bfloat16 [4096, 2560], P(('groups', 'span')), parts along dimension 0, may hold values from -6 to 6
- keys: bfloat16 [4096, 2560], P(('groups', 'span')), parts along dimension 0, may hold values from -6 to 6
- values: bfloat16 [4096, 2560], P(('groups', 'span')), parts along dimension 0, may hold values from -6 to 6
- lookback: int32 [32], P(('groups', 'span')), parts along dimension 0, may hold values from 0 to 3, as said below
- proj_weight: bfloat16 [2560, 768], replicated, may hold values from -0.125 to 0.125
- features: bfloat16 [64, 192, 256], P(('groups', 'span')), parts along dimension 0, may hold values from -0.29882812 to 0.29882812
- norm_gain: float32 [192], replicated, may hold values from 0.1 to 1.9
- conv_weight: bfloat16 [27, 192, 192], replicated, may hold values from -0.078125 to 0.078125
Outputs:
- attended: bfloat16 [4096, 2560], P(('groups', 'span')), parts along dimension 0
- decoded: bfloat16 [64, 192, 256], P(('groups', 'span')), parts along dimension 0
The draws below stay inside these ranges and needn't reach their ends.
There are 2 independent parts, one for each index of `groups`. The reference program is written for one: setup_inputs(seed, part) draws one part's arguments, and reference() takes and returns one part's arrays. A program takes and returns all parts, laid end to end along the dimension named above; an argument that names none is the same for every part. Nothing has to cross between parts.
Inputs may be any that keep to these rules, and one draw needn't show every extreme that they name: lookback[c] <= c for every span c; the last span's value is 3.
All inputs are finite; a program needn't handle non-finite values.
Results may differ from the reference program's by a relative error of at most 0.0069.
Values may be sent and summed in bfloat16 or wider, within the bound.
No kernel may reach another device: no remote copies, remote signals or barrier semaphores. Data moves between devices by JAX's collectives and lax.ppermute only.
A program may use at most 64 MiB of HBM per device.

```python
import jax
import jax.numpy as jnp
from jax import lax

FRAMES_DEV = 2
HEAD_DIM = 128
LOOKBACK = 3
CH = 192
SIDE = 16
PLANE = 256
TOK_DEV = 128
QKV_WIDTH = 2560
PATCH_WIDTH = 768
TOKENS = 2048
FRAMES = 32
N_SPAN = 16


def draw_queries(key, part):
    return jnp.clip(jax.random.normal(jax.random.fold_in(key, 1), (TOKENS, QKV_WIDTH), jnp.float32), -6.0, 6.0).astype(jnp.bfloat16)


def draw_keys(key, part):
    return jnp.clip(jax.random.normal(jax.random.fold_in(key, 2), (TOKENS, QKV_WIDTH), jnp.float32), -6.0, 6.0).astype(jnp.bfloat16)


def draw_lookback(key, part):
    span_ids = jnp.arange(N_SPAN, dtype=jnp.int32)
    chooser = jax.random.randint(jax.random.fold_in(key, 3), (N_SPAN,), 0, 4)
    minor_reach = jax.random.randint(jax.random.fold_in(key, 4), (N_SPAN,), 0, 2)
    reach_limit = jnp.where(chooser == 0, LOOKBACK, minor_reach)
    reach_limit = jnp.where(span_ids == N_SPAN - 1, LOOKBACK, reach_limit)
    return jnp.minimum(reach_limit, span_ids).astype(jnp.int32)


def level_of(stream_key, shape, split, low, largest):
    def one(position, parts):
        heights = jax.random.uniform(jax.random.fold_in(jax.random.fold_in(stream_key, 6), position), (parts,), jnp.float32, low / len(split), largest / len(split))
        return jnp.repeat(jnp.exp(heights), shape[position] // parts).reshape((-1,) + (1,) * (len(shape) - position - 1))

    level = one(*split[0])
    for cut in split[1:]:
        level = level * one(*cut)
    return level


def noise(rng, dims, deviation, most, cuts=(), kind=jnp.bfloat16):
    gain = level_of(rng, dims, cuts, -0.22, 0.18) if cuts else 1.0
    result = jax.random.normal(rng, dims, jnp.float32) * deviation * gain
    return jnp.minimum(jnp.maximum(result, -most), most).astype(kind)


def setup_inputs(seed: int = 0, part: int = 0) -> dict:
    streams_of = jax.random.split(jax.random.key(seed), 9)
    own_keys = jax.random.split(jax.random.fold_in(streams_of[8], part), 9)
    queries = draw_queries(jax.random.fold_in(jax.random.fold_in(streams_of[8], part), 71), part)
    keys = draw_keys(jax.random.fold_in(jax.random.fold_in(streams_of[8], part), 71), part)
    values = noise(own_keys[2], (TOKENS, QKV_WIDTH), 1.0, 6.0, ((0, 16),))
    lookback = draw_lookback(jax.random.fold_in(jax.random.fold_in(streams_of[8], part), 71), part)
    proj_weight = noise(streams_of[4], (QKV_WIDTH, PATCH_WIDTH), QKV_WIDTH ** -0.5, 0.125)
    features = noise(own_keys[5], (FRAMES, CH, PLANE), 0.05, 0.29882812, ((0, 16),))
    norm_gain = jnp.clip(1.0 + 0.18 * jax.random.normal(streams_of[6], (CH,), jnp.float32), 0.1, 1.9)
    conv_weight = noise(streams_of[7], (27, CH, CH), (27 * CH) ** -0.5, 0.078125)
    return {"queries": queries, "keys": keys, "values": values, "lookback": lookback, "proj_weight": proj_weight, "features": features, "norm_gain": norm_gain, "conv_weight": conv_weight}


eps = 1e-06

def attend(query_rows, key_rows, value_rows, reach_limit):
    row_count = query_rows.shape[0]
    head_count = query_rows.shape[1] // HEAD_DIM
    query_heads = query_rows.astype(jnp.float32).reshape(row_count, head_count, HEAD_DIM)
    key_heads = key_rows.astype(jnp.float32).reshape(key_rows.shape[0], head_count, HEAD_DIM)
    value_heads = value_rows.astype(jnp.float32).reshape(value_rows.shape[0], head_count, HEAD_DIM)
    scores = jnp.einsum('thd,khd->htk', query_heads, key_heads) * HEAD_DIM ** (-0.5)
    distance = jnp.repeat(jnp.arange(LOOKBACK + 1, dtype=jnp.int32), TOK_DEV)
    usable = distance <= reach_limit
    scores = jnp.where(usable[None, None, :], scores, -jnp.inf)
    row_max = lax.optimization_barrier(jnp.max(scores, axis=2, keepdims=True))
    weights = jnp.exp(scores - row_max)
    row_total = lax.optimization_barrier(jnp.sum(weights, axis=2))
    rounded = lax.optimization_barrier(weights.astype(jnp.bfloat16)).astype(jnp.float32)
    blended = jnp.einsum('htk,khd->thd', rounded, value_heads)
    return (blended / row_total.T[:, :, None]).reshape(row_count, -1).astype(jnp.bfloat16)

def unpatch(projected, frame_count, channels):
    shaped = projected.reshape(frame_count, SIDE // 2, SIDE // 2, channels, 2, 2)
    shaped = shaped.transpose(0, 3, 1, 4, 2, 5)
    return shaped.reshape(frame_count, channels, SIDE * SIDE)

def activate(frames_in, norm_gain):
    data = frames_in.astype(jnp.float32)
    mean_square = lax.optimization_barrier(jnp.mean(data * data, axis=1, keepdims=True))
    normed = data * lax.rsqrt(mean_square + eps) * norm_gain.astype(jnp.float32)[None, :, None]
    return jax.nn.silu(normed).astype(jnp.bfloat16)

def convolve(conv_input, conv_weight):
    frame_count = conv_input.shape[0] - 2
    plane_size = SIDE * SIDE
    padded = jnp.pad(conv_input, ((0, 0), (0, 0), (SIDE + 1, SIDE + 1)))
    column = jnp.arange(plane_size, dtype=jnp.int32) % SIDE
    summed = jnp.zeros((frame_count, conv_weight.shape[1], plane_size), jnp.float32)
    for lag_t in range(3):
        for lag_y in range(3):
            for lag_x in range(3):
                offset = SIDE + 1 + (lag_y - 1) * SIDE + (lag_x - 1)
                window = padded[lag_t:lag_t + frame_count, :, offset:offset + plane_size]
                inside = (column + lag_x - 1 >= 0) & (column + lag_x - 1 < SIDE)
                window = jnp.where(inside[None, None, :], window, jnp.zeros_like(window))
                tap_matrix = conv_weight[lag_t * 9 + lag_y * 3 + lag_x].astype(jnp.float32)
                summed = summed + jnp.einsum('oc,fcp->fop', tap_matrix, window.astype(jnp.float32))
    return summed

def reference(queries, keys, values, lookback, proj_weight, features, norm_gain, conv_weight):

    def one_span(span_index):
        first_row = (span_index * TOK_DEV).astype(jnp.int32)
        query_rows = lax.dynamic_slice_in_dim(queries, first_row, TOK_DEV, 0)
        key_parts = []
        value_parts = []
        for distance in range(LOOKBACK + 1):
            source_row = (jnp.maximum(span_index - distance, 0) * TOK_DEV).astype(jnp.int32)
            key_parts.append(lax.dynamic_slice_in_dim(keys, source_row, TOK_DEV, 0))
            value_parts.append(lax.dynamic_slice_in_dim(values, source_row, TOK_DEV, 0))
        return attend(query_rows, jnp.concatenate(key_parts, axis=0), jnp.concatenate(value_parts, axis=0), lookback[span_index])
    span_ids = jnp.arange(N_SPAN, dtype=jnp.int32)
    attended = lax.map(one_span, span_ids).reshape(TOKENS, -1)
    projected = jnp.dot(attended, proj_weight, preferred_element_type=jnp.float32)
    latent = (features.astype(jnp.float32) + unpatch(projected, FRAMES, CH)).astype(jnp.bfloat16)
    activated = activate(latent, norm_gain)
    padded_frames = jnp.concatenate([jnp.zeros((2,) + activated.shape[1:], jnp.bfloat16), activated], axis=0)

    def one_block(span_index):
        first_frame = (span_index * FRAMES_DEV).astype(jnp.int32)
        conv_input = lax.dynamic_slice_in_dim(padded_frames, first_frame, FRAMES_DEV + 2, 0)
        frames_in = lax.dynamic_slice_in_dim(latent, first_frame, FRAMES_DEV, 0)
        return (frames_in.astype(jnp.float32) + convolve(conv_input, conv_weight)).astype(jnp.bfloat16)
    decoded = lax.map(one_block, span_ids).reshape(FRAMES, CH, SIDE * SIDE)
    return (attended, decoded)
```

```python
import functools

import jax
import jax.numpy as jnp
import numpy as np
from jax import lax
from jax.experimental import pallas as pl
from jax.experimental.pallas import tpu as pltpu
from jax.sharding import PartitionSpec as P

HEAD_DIM = 128
LOOKBACK = 3
SIDE = 16
PATCH = 2
TAPS = 9
EPS = 1e-06

HBM = pl.BlockSpec(memory_space=pl.ANY)
VMEM = pl.BlockSpec(memory_space=pltpu.VMEM)
SMEM = pl.BlockSpec(memory_space=pltpu.SMEM)


def params():
    return pltpu.CompilerParams(vmem_limit_bytes=40 * 1024 * 1024)


def unpatch_matrix(frames):
    half = SIDE // PATCH
    tokens = frames * half * half
    pixels = SIDE * SIDE
    out = np.zeros((PATCH * PATCH * tokens, frames * pixels), np.float32)
    for i in range(PATCH):
        for j in range(PATCH):
            for f in range(frames):
                for row in range(half):
                    for col in range(half):
                        token = f * half * half + row * half + col
                        pixel = f * pixels + (PATCH * row + i) * SIDE + PATCH * col + j
                        out[(PATCH * i + j) * tokens + token, pixel] = 1
    return out


def shift_matrices():
    pixels = SIDE * SIDE
    out = np.zeros((pixels, TAPS * pixels), np.float32)
    for b in range(3):
        for e in range(3):
            for row in range(SIDE):
                for col in range(SIDE):
                    r, c = row + b - 1, col + e - 1
                    if 0 <= r < SIDE and 0 <= c < SIDE:
                        out[r * SIDE + c, (3 * b + e) * pixels + row * SIDE + col] = 1
    return out


OWN, S0, R1, S1, R2, S2 = range(6)
SLOTS = ((OWN, S2, R2, S1), (OWN, S0, R2, S2), (OWN, S2, R1, S1), (OWN, S0, R2, S1))


def fetch(place, refs, held, sems):
    rows = held.shape[0] // (LOOKBACK + 1)
    for slot in range(LOOKBACK + 1):
        for source in sorted({by_place[slot] for by_place in SLOTS}):
            places = [r for r in range(4) if SLOTS[r][slot] == source]
            wanted = functools.reduce(jnp.logical_or, [place == r for r in places])

            @pl.when(wanted)
            def _(slot=slot, source=source):
                pltpu.make_async_copy(
                    refs[source], held.at[pl.ds(slot * rows, rows)], sems.at[slot]
                ).start()

    def wait():
        for slot in range(LOOKBACK + 1):
            pltpu.make_async_copy(
                refs[OWN], held.at[pl.ds(slot * rows, rows)], sems.at[slot]
            ).wait()

    return wait


def scores_kernel(meta, q_ref, *rest):
    refs, (p_ref, total_ref, held, sems) = rest[:6], rest[6:]
    wait = fetch(meta[0], refs, held, sems)
    reach = meta[1]
    rows = q_ref.shape[0]
    heads = q_ref.shape[1] // HEAD_DIM
    keys = held.shape[0]
    block = lax.broadcasted_iota(jnp.int32, (rows, keys), 1) // rows
    usable = block <= reach
    wait()
    for h in range(heads):
        cols = slice(h * HEAD_DIM, (h + 1) * HEAD_DIM)
        s = lax.dot_general(
            q_ref[:, cols], held[:, cols], (((1,), (1,)), ((), ())),
            preferred_element_type=jnp.float32,
        ) * HEAD_DIM ** (-0.5)
        s = jnp.where(usable, s, -jnp.inf)
        p = jnp.exp(s - jnp.max(s, axis=1, keepdims=True))
        total_ref[:, h : h + 1] = jnp.sum(p, axis=1, keepdims=True)
        p_ref[h] = p.astype(jnp.bfloat16)


def latent_kernel(meta, p_ref, total_ref, *rest):
    refs, rest = rest[:6], rest[6:]
    w_ref, place_ref, features_ref, gain_ref, out_ref, latent_ref, act_ref, held, turned, sems = rest
    wait = fetch(meta[0], refs, held, sems)
    rows, width = out_ref.shape
    heads = width // HEAD_DIM
    frames, channels, pixels = features_ref.shape
    wait()
    for h in range(heads):
        cols = slice(h * HEAD_DIM, (h + 1) * HEAD_DIM)
        blended = jnp.dot(p_ref[h], held[:, cols], preferred_element_type=jnp.float32)
        out_ref[:, cols] = (blended / total_ref[:, h : h + 1]).astype(jnp.bfloat16)
    projected = jnp.dot(out_ref[...], w_ref[...], preferred_element_type=jnp.float32)
    turned[...] = projected.T
    parts = [turned[pl.ds(k, channels, stride=4), :] for k in range(4)]
    mixed = jnp.concatenate(parts, axis=1)
    high = mixed.astype(jnp.bfloat16)
    low = (mixed - high.astype(jnp.float32)).astype(jnp.bfloat16)
    placed = jnp.dot(high, place_ref[...], preferred_element_type=jnp.float32)
    placed += jnp.dot(low, place_ref[...], preferred_element_type=jnp.float32)
    for f in range(frames):
        latent = features_ref[f].astype(jnp.float32) + placed[:, f * pixels : (f + 1) * pixels]
        latent = latent.astype(jnp.bfloat16)
        latent_ref[f] = latent
        data = latent.astype(jnp.float32)
        mean_square = jnp.mean(data * data, axis=0, keepdims=True)
        normed = data * lax.rsqrt(mean_square + EPS) * gain_ref[...]
        act_ref[f] = (normed / (1.0 + jnp.exp(-normed))).astype(jnp.bfloat16)


def spread(act, shift_ref, moved):
    channels, pixels = act.shape
    for tap in range(TAPS):
        moved[pl.ds(tap * channels, channels), :] = jnp.dot(
            act, shift_ref[:, tap * pixels : (tap + 1) * pixels],
            preferred_element_type=jnp.float32,
        ).astype(jnp.bfloat16)


def tap_dot(w_ref, lag, moved):
    return jnp.dot(w_ref[lag], moved[...], preferred_element_type=jnp.float32)


def conv_own_kernel(act_ref, shift_ref, w_ref, part_ref, moved0, moved1):
    spread(act_ref[0], shift_ref, moved0)
    spread(act_ref[1], shift_ref, moved1)
    part_ref[0] = tap_dot(w_ref, 2, moved0)
    part_ref[1] = tap_dot(w_ref, 1, moved0) + tap_dot(w_ref, 2, moved1)


def conv_halo_kernel(halo_ref, shift_ref, w_ref, part_ref, latent_ref, out_ref, moved0, moved1):
    spread(halo_ref[0], shift_ref, moved0)
    spread(halo_ref[1], shift_ref, moved1)
    first = part_ref[0] + tap_dot(w_ref, 0, moved0) + tap_dot(w_ref, 1, moved1)
    second = part_ref[1] + tap_dot(w_ref, 0, moved1)
    out_ref[0] = (latent_ref[0].astype(jnp.float32) + first).astype(jnp.bfloat16)
    out_ref[1] = (latent_ref[1].astype(jnp.float32) + second).astype(jnp.bfloat16)


def routes(count):
    own, hop1, swap1, hop2, swap2 = [], [], [], [], []
    for s in range(count):
        r, first, last = s % 4, s < 4, s + 4 >= count
        if r == 0:
            own.append((s, s + 1))
            hop1.append((s, s + 2))
            if not last:
                hop2.append((s, s + 4))
            if not first:
                swap2.append((s, s + 1))
        elif r == 1:
            if not last:
                hop1.append((s, s + 4))
            hop2.append((s, s + 2))
            if not first:
                swap1.append((s, s - 1))
                swap2.append((s, s - 1))
        elif r == 2:
            own.append((s, s + 1))
            if not last:
                hop1.append((s, s - 2))
            swap1.append((s, s + 1))
        else:
            if not last:
                hop1.append((s, s + 4))
            if not first:
                swap1.append((s, s - 1))
                hop2.append((s, s - 2))
            swap2.append((s, s - 1))
    return own, hop1, swap1, hop2, swap2


def shards(queries, keys, values, lookback, proj_weight, features, norm_gain, conv_weight):
    count = lax.axis_size("span")
    me = lax.axis_index("span")
    place = lax.rem(me, 4)
    own, hop1, swap1, hop2, swap2 = routes(count)
    move = functools.partial(lax.ppermute, axis_name="span")

    rows, width = queries.shape
    heads = width // HEAD_DIM
    frames, channels, pixels = features.shape
    spans = LOOKBACK + 1

    k_r1 = move(keys, perm=hop1)
    v_r1 = move(values, perm=hop1)
    k_s0 = move(keys, perm=own)
    v_s0 = move(values, perm=own)
    k_r2 = move(jnp.where(place == 1, keys, k_r1), perm=hop2)
    k_s1 = move(k_r1, perm=swap1)
    v_r2 = move(jnp.where(place == 1, values, v_r1), perm=hop2)
    v_s1 = move(v_r1, perm=swap1)
    k_s2 = move(k_r2, perm=swap2)
    v_s2 = move(v_r2, perm=swap2)

    meta = jnp.stack([place, lookback[0]]).astype(jnp.int32)
    place_matrix = jnp.asarray(unpatch_matrix(frames), jnp.bfloat16)
    shift_matrix = jnp.asarray(shift_matrices(), jnp.bfloat16)
    lagged = conv_weight.reshape(3, TAPS, channels, channels).transpose(0, 2, 1, 3)
    lagged = lagged.reshape(3, channels, TAPS * channels)
    gain = norm_gain.reshape(channels, 1)
    queries, place_matrix, shift_matrix, lagged, gain = lax.optimization_barrier(
        (queries, place_matrix, shift_matrix, lagged, gain)
    )

    held = [pltpu.VMEM((spans * rows, width), jnp.bfloat16), pltpu.SemaphoreType.DMA((spans,))]
    weights, total = pl.pallas_call(
        scores_kernel,
        out_shape=(
            jax.ShapeDtypeStruct((heads, rows, spans * rows), jnp.bfloat16),
            jax.ShapeDtypeStruct((rows, heads), jnp.float32),
        ),
        in_specs=[SMEM, VMEM] + [HBM] * 6,
        out_specs=(VMEM, VMEM),
        scratch_shapes=held,
        compiler_params=params(),
        name="scores",
        cost_estimate=pl.CostEstimate(
            flops=2 * rows * rows * spans * width,
            bytes_accessed=10 * rows * width * 2,
            transcendentals=heads * rows * rows * spans,
        ),
    )(meta, queries, keys, k_s0, k_r1, k_s1, k_r2, k_s2)

    attended, latent, activated = pl.pallas_call(
        latent_kernel,
        out_shape=(
            jax.ShapeDtypeStruct((rows, width), jnp.bfloat16),
            jax.ShapeDtypeStruct(features.shape, jnp.bfloat16),
            jax.ShapeDtypeStruct(features.shape, jnp.bfloat16),
        ),
        in_specs=[SMEM, VMEM, VMEM] + [HBM] * 6 + [VMEM] * 4,
        out_specs=(VMEM, VMEM, VMEM),
        scratch_shapes=[
            held[0],
            pltpu.VMEM((proj_weight.shape[1], rows), jnp.float32),
            held[1],
        ],
        compiler_params=params(),
        name="latent",
        cost_estimate=pl.CostEstimate(
            flops=2 * rows * width * (spans * rows + proj_weight.shape[1]),
            bytes_accessed=10 * rows * width * 2 + proj_weight.size * 2,
            transcendentals=features.size,
        ),
    )(
        meta, weights, total, values, v_s0, v_r1, v_s1, v_r2, v_s2,
        proj_weight, place_matrix, features, gain,
    )

    halo = move(activated, perm=[(s, s + 1) for s in range(count - 1)])

    moved = [pltpu.VMEM((TAPS * channels, pixels), jnp.bfloat16)] * 2
    conv_cost = pl.CostEstimate(
        flops=2 * channels * TAPS * channels * pixels * 3,
        bytes_accessed=conv_weight.size * 2 + shift_matrix.size * 2,
        transcendentals=0,
    )
    part = pl.pallas_call(
        conv_own_kernel,
        out_shape=jax.ShapeDtypeStruct(features.shape, jnp.float32),
        in_specs=[VMEM] * 3,
        out_specs=VMEM,
        scratch_shapes=moved,
        compiler_params=params(),
        name="conv_own",
        cost_estimate=conv_cost,
    )(activated, shift_matrix, lagged)
    decoded = pl.pallas_call(
        conv_halo_kernel,
        out_shape=jax.ShapeDtypeStruct(features.shape, jnp.bfloat16),
        in_specs=[VMEM] * 5,
        out_specs=VMEM,
        scratch_shapes=moved,
        compiler_params=params(),
        name="conv_halo",
        cost_estimate=conv_cost,
    )(halo, shift_matrix, lagged, part, latent)
    return (attended, decoded)


def solution(mesh):
    placed = (
        P(("groups", "span"), None),
        P(("groups", "span"), None),
        P(("groups", "span"), None),
        P(("groups", "span")),
        P(),
        P(("groups", "span"), None, None),
        P(),
        P(),
    )
    return jax.shard_map(
        shards,
        mesh=mesh,
        in_specs=placed,
        out_specs=(P(("groups", "span"), None), P(("groups", "span"), None, None)),
        check_vma=False,
    )
```

```python
import functools

import jax
import jax.numpy as jnp
import numpy as np
from jax import lax
from jax.experimental import pallas as pl
from jax.experimental.pallas import tpu as pltpu
from jax.sharding import PartitionSpec as P

HEAD_DIM = 128
LOOKBACK = 3
SIDE = 16
PATCH = 2
TAPS = 9
EPS = 1e-06

VMEM = pl.BlockSpec(memory_space=pltpu.VMEM)
SMEM = pl.BlockSpec(memory_space=pltpu.SMEM)


def params():
    return pltpu.CompilerParams(vmem_limit_bytes=40 * 1024 * 1024)


def one_hot_kernel(place_ref, shift_ref):
    half = SIDE // PATCH
    patches = half * half
    pixels = SIDE * SIDE
    tokens = place_ref.shape[0] // (PATCH * PATCH)
    column = lax.broadcasted_iota(jnp.int32, (tokens, place_ref.shape[1]), 1)
    pixel = column % pixels
    row, col = pixel // SIDE, pixel % SIDE
    token = column // pixels * patches + row // PATCH * half + col // PATCH
    corner = row % PATCH * PATCH + col % PATCH
    hit = lax.broadcasted_iota(jnp.int32, token.shape, 0) == token
    for k in range(PATCH * PATCH):
        place_ref[pl.ds(k * tokens, tokens), :] = jnp.where(
            hit & (corner == k), 1.0, 0.0
        ).astype(jnp.bfloat16)
    source = lax.broadcasted_iota(jnp.int32, (pixels, pixels), 0)
    target = lax.broadcasted_iota(jnp.int32, (pixels, pixels), 1)
    for b in range(3):
        for e in range(3):
            r, c = target // SIDE + b - 1, target % SIDE + e - 1
            inside = (r >= 0) & (r < SIDE) & (c >= 0) & (c < SIDE)
            tap = 3 * b + e
            shift_ref[:, tap * pixels : (tap + 1) * pixels] = jnp.where(
                inside & (source == r * SIDE + c), 1.0, 0.0
            ).astype(jnp.bfloat16)


UNSEEN = LOOKBACK + 1
DISTANCES = ((0, UNSEEN, 3, 2, 1), (0, 1, UNSEEN, 2, 3), (0, 2, 3, UNSEEN, 1), (0, 1, 3, 2, UNSEEN))
RATE = float(np.log2(np.e) * HEAD_DIM**-0.5)


def scores_of(q_ref, k_ref, cols, bias):
    return lax.dot_general(
        q_ref[:, cols], k_ref[:, cols], (((1,), (1,)), ((), ())),
        preferred_element_type=jnp.float32,
    ) * RATE + bias


def early_kernel(bias, q_ref, k0, k1, k2, v0, v1, v2, mixed_ref, top_ref, total_ref):
    for h in range(q_ref.shape[1] // HEAD_DIM):
        cols = slice(h * HEAD_DIM, (h + 1) * HEAD_DIM)
        scores = [scores_of(q_ref, k, cols, bias[i]) for i, k in enumerate((k0, k1, k2))]
        top = jnp.max(functools.reduce(jnp.maximum, scores), axis=1, keepdims=True)
        probs = [jnp.exp2(s - top) for s in scores]
        top_ref[:, h : h + 1] = top
        total_ref[:, h : h + 1] = jnp.sum(sum(probs), axis=1, keepdims=True)
        mixed_ref[:, cols] = sum(
            jnp.dot(p.astype(jnp.bfloat16), v[:, cols], preferred_element_type=jnp.float32)
            for p, v in zip(probs, (v0, v1, v2))
        )


def late_kernel(
    bias, q_ref, k1, k2, mixed_ref, top_ref, total_ref, p_ref, base_ref, inverse_ref
):
    for h in range(q_ref.shape[1] // HEAD_DIM):
        cols = slice(h * HEAD_DIM, (h + 1) * HEAD_DIM)
        scores = [scores_of(q_ref, k, cols, bias[3 + i]) for i, k in enumerate((k1, k2))]
        before = top_ref[:, h : h + 1]
        top = jnp.maximum(before, jnp.max(jnp.maximum(*scores), axis=1, keepdims=True))
        probs = [jnp.exp2(s - top) for s in scores]
        shrink = jnp.exp2(before - top)
        total = total_ref[:, h : h + 1] * shrink + jnp.sum(sum(probs), axis=1, keepdims=True)
        inverse = 1.0 / total
        inverse_ref[:, h : h + 1] = inverse
        base_ref[:, cols] = mixed_ref[:, cols] * (shrink * inverse)
        for i, p in enumerate(probs):
            p_ref[h, :, i * HEAD_DIM : (i + 1) * HEAD_DIM] = p.astype(jnp.bfloat16)


def latent_kernel(
    p_ref, base_ref, inverse_ref, v1, v2, w_ref, place_ref, features_ref, gain_ref,
    out_ref, latent_ref, act_ref, turned,
):
    rows, width = out_ref.shape
    frames, channels, pixels = features_ref.shape
    for h in range(width // HEAD_DIM):
        cols = slice(h * HEAD_DIM, (h + 1) * HEAD_DIM)
        late = jnp.dot(p_ref[h, :, :rows], v1[:, cols], preferred_element_type=jnp.float32)
        late += jnp.dot(p_ref[h, :, rows:], v2[:, cols], preferred_element_type=jnp.float32)
        late = base_ref[:, cols] + late * inverse_ref[:, h : h + 1]
        out_ref[:, cols] = late.astype(jnp.bfloat16)
    projected = jnp.dot(out_ref[...], w_ref[...], preferred_element_type=jnp.float32)
    turned[...] = projected.T
    parts = [turned[pl.ds(k, channels, stride=4), :] for k in range(4)]
    mixed = jnp.concatenate(parts, axis=1)
    high = mixed.astype(jnp.bfloat16)
    low = (mixed - high.astype(jnp.float32)).astype(jnp.bfloat16)
    placed = jnp.dot(high, place_ref[...], preferred_element_type=jnp.float32)
    placed += jnp.dot(low, place_ref[...], preferred_element_type=jnp.float32)
    for f in range(frames):
        latent = features_ref[f].astype(jnp.float32) + placed[:, f * pixels : (f + 1) * pixels]
        latent = latent.astype(jnp.bfloat16)
        latent_ref[f] = latent
        data = latent.astype(jnp.float32)
        mean_square = jnp.mean(data * data, axis=0, keepdims=True)
        normed = data * lax.rsqrt(mean_square + EPS) * gain_ref[...]
        act_ref[f] = (normed / (1.0 + jnp.exp(-normed))).astype(jnp.bfloat16)


def spread(act, shift_ref, moved):
    channels, pixels = act.shape
    for tap in range(TAPS):
        moved[pl.ds(tap * channels, channels), :] = jnp.dot(
            act, shift_ref[:, tap * pixels : (tap + 1) * pixels],
            preferred_element_type=jnp.float32,
        ).astype(jnp.bfloat16)


def tap_dot(w_ref, lag, moved):
    channels = w_ref.shape[2]
    return sum(
        jnp.dot(
            w_ref[lag * TAPS + tap], moved[pl.ds(tap * channels, channels), :],
            preferred_element_type=jnp.float32,
        )
        for tap in range(TAPS)
    )


def conv_own_kernel(act_ref, shift_ref, w_ref, part_ref, moved0, moved1):
    spread(act_ref[0], shift_ref, moved0)
    spread(act_ref[1], shift_ref, moved1)
    part_ref[0] = tap_dot(w_ref, 2, moved0)
    part_ref[1] = tap_dot(w_ref, 1, moved0) + tap_dot(w_ref, 2, moved1)


def conv_halo_kernel(halo_ref, shift_ref, w_ref, part_ref, latent_ref, out_ref, moved0, moved1):
    spread(halo_ref[0], shift_ref, moved0)
    spread(halo_ref[1], shift_ref, moved1)
    first = part_ref[0] + tap_dot(w_ref, 0, moved0) + tap_dot(w_ref, 1, moved1)
    second = part_ref[1] + tap_dot(w_ref, 0, moved1)
    out_ref[0] = (latent_ref[0].astype(jnp.float32) + first).astype(jnp.bfloat16)
    out_ref[1] = (latent_ref[1].astype(jnp.float32) + second).astype(jnp.bfloat16)


def routes(count):
    own, hop1, swap1, hop2, swap2 = [], [], [], [], []
    for s in range(count):
        r, first, last = s % 4, s < 4, s + 4 >= count
        if r == 0:
            own.append((s, s + 1))
            hop1.append((s, s + 2))
            if not last:
                hop2.append((s, s + 4))
            if not first:
                swap2.append((s, s + 1))
        elif r == 1:
            if not last:
                hop1.append((s, s + 4))
            hop2.append((s, s + 2))
            if not first:
                swap1.append((s, s - 1))
                swap2.append((s, s - 1))
        elif r == 2:
            own.append((s, s + 1))
            if not last:
                hop1.append((s, s - 2))
            swap1.append((s, s + 1))
        else:
            if not last:
                hop1.append((s, s + 4))
            if not first:
                swap1.append((s, s - 1))
                hop2.append((s, s - 2))
            swap2.append((s, s - 1))
    return own, hop1, swap1, hop2, swap2


def shards(queries, keys, values, lookback, proj_weight, features, norm_gain, conv_weight):
    count = lax.axis_size("span")
    me = lax.axis_index("span")
    place = lax.rem(me, 4)
    own, hop1, swap1, hop2, swap2 = routes(count)
    move = functools.partial(lax.ppermute, axis_name="span")

    rows, width = queries.shape
    heads = width // HEAD_DIM
    frames, channels, pixels = features.shape

    block = jax.ShapeDtypeStruct((rows, width), jnp.float32)
    column = jax.ShapeDtypeStruct((rows, heads), jnp.float32)
    picture = jax.ShapeDtypeStruct(features.shape, jnp.bfloat16)

    distances = jnp.asarray(DISTANCES, jnp.int32)[place]
    bias = jnp.where(distances <= lookback[0], 0.0, -jnp.inf).astype(jnp.float32)

    k_r1 = move(keys, perm=hop1)
    k_s0 = move(keys, perm=own)
    v_r1 = move(values, perm=hop1)
    v_s0 = move(values, perm=own)

    tokens = frames * pixels // (PATCH * PATCH)
    place_matrix, shift_matrix = pl.pallas_call(
        one_hot_kernel,
        out_shape=(
            jax.ShapeDtypeStruct((PATCH * PATCH * tokens, frames * pixels), jnp.bfloat16),
            jax.ShapeDtypeStruct((pixels, TAPS * pixels), jnp.bfloat16),
        ),
        out_specs=(VMEM, VMEM),
        compiler_params=params(),
        name="one_hot",
    )()
    gain = norm_gain.reshape(channels, 1)
    k_r1, place_matrix, shift_matrix, gain, bias = lax.optimization_barrier(
        (k_r1, place_matrix, shift_matrix, gain, bias)
    )

    k_r2 = move(jnp.where(place == 1, keys, k_r1), perm=hop2)
    k_s1 = move(k_r1, perm=swap1)
    v_r2 = move(jnp.where(place == 1, values, v_r1), perm=hop2)
    v_s1 = move(v_r1, perm=swap1)

    first_core = lax.rem(place, 2) == 0
    mixed, top, total = pl.pallas_call(
        early_kernel,
        out_shape=(block, column, column),
        in_specs=[SMEM] + [VMEM] * 7,
        out_specs=(VMEM,) * 3,
        compiler_params=params(),
        name="early",
        cost_estimate=pl.CostEstimate(
            flops=12 * rows * rows * width,
            bytes_accessed=9 * rows * width * 2,
            transcendentals=3 * heads * rows * rows,
        ),
    )(
        bias, queries,
        keys, jnp.where(first_core, k_r1, k_s0), k_s1,
        values, jnp.where(first_core, v_r1, v_s0), v_s1,
    )

    k_r2, mixed, top, total = lax.optimization_barrier((k_r2, mixed, top, total))
    k_s2 = move(k_r2, perm=swap2)
    weights, base, inverse = pl.pallas_call(
        late_kernel,
        out_shape=(
            jax.ShapeDtypeStruct((heads, rows, 2 * rows), jnp.bfloat16), block, column,
        ),
        in_specs=[SMEM] + [VMEM] * 6,
        out_specs=(VMEM,) * 3,
        compiler_params=params(),
        name="late",
        cost_estimate=pl.CostEstimate(
            flops=4 * rows * rows * width,
            bytes_accessed=9 * rows * width * 2,
            transcendentals=2 * heads * rows * rows,
        ),
    )(bias, queries, k_r2, k_s2, mixed, top, total)

    v_r2, weights, base, inverse = lax.optimization_barrier((v_r2, weights, base, inverse))
    v_s2 = move(v_r2, perm=swap2)
    attended, latent, activated = pl.pallas_call(
        latent_kernel,
        out_shape=(jax.ShapeDtypeStruct((rows, width), jnp.bfloat16), picture, picture),
        in_specs=[VMEM] * 9,
        out_specs=(VMEM,) * 3,
        scratch_shapes=[pltpu.VMEM((proj_weight.shape[1], rows), jnp.float32)],
        compiler_params=params(),
        name="latent",
        cost_estimate=pl.CostEstimate(
            flops=2 * rows * width * (2 * rows + proj_weight.shape[1]),
            bytes_accessed=10 * rows * width * 2 + proj_weight.size * 2,
            transcendentals=features.size,
        ),
    )(
        weights, base, inverse, v_r2, v_s2, proj_weight, place_matrix, features, gain,
    )

    halo = move(activated, perm=[(s, s + 1) for s in range(count - 1)])

    moved = [pltpu.VMEM((TAPS * channels, pixels), jnp.bfloat16)] * 2
    conv_cost = pl.CostEstimate(
        flops=2 * channels * TAPS * channels * pixels * 3,
        bytes_accessed=conv_weight.size * 2 + shift_matrix.size * 2,
        transcendentals=0,
    )
    part = pl.pallas_call(
        conv_own_kernel,
        out_shape=jax.ShapeDtypeStruct(features.shape, jnp.float32),
        in_specs=[VMEM] * 3,
        out_specs=VMEM,
        scratch_shapes=moved,
        compiler_params=params(),
        name="conv_own",
        cost_estimate=conv_cost,
    )(activated, shift_matrix, conv_weight)
    decoded = pl.pallas_call(
        conv_halo_kernel,
        out_shape=jax.ShapeDtypeStruct(features.shape, jnp.bfloat16),
        in_specs=[VMEM] * 5,
        out_specs=VMEM,
        scratch_shapes=moved,
        compiler_params=params(),
        name="conv_halo",
        cost_estimate=conv_cost,
    )(halo, shift_matrix, conv_weight, part, latent)
    return (attended, decoded)


def solution(mesh):
    placed = (
        P(("groups", "span"), None),
        P(("groups", "span"), None),
        P(("groups", "span"), None),
        P(("groups", "span")),
        P(),
        P(("groups", "span"), None, None),
        P(),
        P(),
    )
    return jax.shard_map(
        shards,
        mesh=mesh,
        in_specs=placed,
        out_specs=(P(("groups", "span"), None), P(("groups", "span"), None, None)),
        check_vma=False,
    )
```

```python
import functools

import jax
import jax.numpy as jnp
import numpy as np
from jax import lax
from jax.experimental import pallas as pl
from jax.experimental.pallas import tpu as pltpu
from jax.sharding import PartitionSpec as P

HEAD_DIM = 128
LOOKBACK = 3
SIDE = 16
PATCH = 2
TAPS = 9
EPS = 1e-06

VMEM = pl.BlockSpec(memory_space=pltpu.VMEM)
SMEM = pl.BlockSpec(memory_space=pltpu.SMEM)


def params():
    return pltpu.CompilerParams(vmem_limit_bytes=16 * 1024 * 1024)


def one_hot_kernel(place_ref, shift_ref):
    half = SIDE // PATCH
    patches = half * half
    pixels = SIDE * SIDE
    tokens = place_ref.shape[0] // (PATCH * PATCH)
    column = lax.broadcasted_iota(jnp.int32, (tokens, place_ref.shape[1]), 1)
    pixel = column % pixels
    row, col = pixel // SIDE, pixel % SIDE
    token = column // pixels * patches + row // PATCH * half + col // PATCH
    corner = row % PATCH * PATCH + col % PATCH
    hit = lax.broadcasted_iota(jnp.int32, token.shape, 0) == token
    for k in range(PATCH * PATCH):
        place_ref[pl.ds(k * tokens, tokens), :] = jnp.where(
            hit & (corner == k), 1.0, 0.0
        ).astype(jnp.bfloat16)
    source = lax.broadcasted_iota(jnp.int32, (pixels, pixels), 0)
    target = lax.broadcasted_iota(jnp.int32, (pixels, pixels), 1)
    for b in range(3):
        for e in range(3):
            r, c = target // SIDE + b - 1, target % SIDE + e - 1
            inside = (r >= 0) & (r < SIDE) & (c >= 0) & (c < SIDE)
            tap = 3 * b + e
            shift_ref[:, tap * pixels : (tap + 1) * pixels] = jnp.where(
                inside & (source == r * SIDE + c), 1.0, 0.0
            ).astype(jnp.bfloat16)


UNSEEN = LOOKBACK + 1
DISTANCES = ((0, UNSEEN, 3, 2, 1), (0, 1, UNSEEN, 2, 3), (0, 2, 3, UNSEEN, 1), (0, 1, 3, 2, UNSEEN))
RATE = float(np.log2(np.e) * HEAD_DIM**-0.5)


def head(h):
    return slice(h * HEAD_DIM, (h + 1) * HEAD_DIM)


def staged(heads, *stages):
    held = {}
    for step in range(heads + len(stages) - 1):
        for i, stage in enumerate(stages):
            h = step - i
            if 0 <= h < heads:
                held[h] = stage(h, held.get(h))


def scores_of(q_ref, blocks, biases, h):
    keys = jnp.concatenate([k[:, head(h)] for k in blocks], axis=0)
    s = lax.dot_general(
        q_ref[:, head(h)], keys, (((1,), (1,)), ((), ())), preferred_element_type=jnp.float32
    )
    rows = blocks[0].shape[0]
    parts = [s[:, i * rows : (i + 1) * rows] for i in range(len(blocks))]
    return [part if bias is None else part + bias for part, bias in zip(parts, biases)]


def top_of(parts):
    return jnp.max(functools.reduce(jnp.maximum, parts), axis=1, keepdims=True)


def early_kernel(bias, q_ref, k0, k1, k2, v0, v1, v2, mixed_ref, top_ref, total_ref):
    rows = q_ref.shape[0]
    ones = jnp.ones((3 * rows, HEAD_DIM), jnp.bfloat16)

    def score(h, _):
        return scores_of(q_ref, (k0, k1, k2), (None, bias[1], bias[2]), h)

    def soften(h, parts):
        top = top_of(parts)
        top_ref[:, head(h)] = jnp.broadcast_to(top, (rows, HEAD_DIM))
        probs = [jnp.exp2((part - top) * RATE).astype(jnp.bfloat16) for part in parts]
        return jnp.concatenate(probs, axis=1)

    def blend(h, probs):
        values = jnp.concatenate([v[:, head(h)] for v in (v0, v1, v2)], axis=0)
        both = jnp.dot(
            probs, jnp.concatenate([values, ones], axis=1), preferred_element_type=jnp.float32
        )
        mixed_ref[:, head(h)] = both[:, :HEAD_DIM]
        total_ref[:, head(h)] = both[:, HEAD_DIM:]

    staged(q_ref.shape[1] // HEAD_DIM, score, soften, blend)


def late_kernel(
    bias, q_ref, k1, k2, mixed_ref, top_ref, total_ref, p_ref, base_ref, inverse_ref
):
    rows = q_ref.shape[0]
    ones = jnp.ones((2 * rows, HEAD_DIM), jnp.bfloat16)

    def score(h, _):
        return scores_of(q_ref, (k1, k2), (bias[3], bias[4]), h)

    def soften(h, parts):
        before = top_ref[:, head(h)]
        top = jnp.maximum(before, top_of(parts))
        probs = [jnp.exp2((part - top) * RATE).astype(jnp.bfloat16) for part in parts]
        probs = jnp.concatenate(probs, axis=1)
        p_ref[h] = probs
        return probs, jnp.exp2((before - top) * RATE)

    def settle(h, held):
        probs, shrink = held
        total = jnp.dot(probs, ones, preferred_element_type=jnp.float32)
        inverse = 1.0 / (total + total_ref[:, head(h)] * shrink)
        inverse_ref[:, head(h)] = inverse
        base_ref[:, head(h)] = mixed_ref[:, head(h)] * (shrink * inverse)

    staged(q_ref.shape[1] // HEAD_DIM, score, soften, settle)


def latent_kernel(
    p_ref, base_ref, inverse_ref, v1, v2, w_ref, place_ref, features_ref, gain_ref,
    out_ref, latent_ref, act_ref, turned,
):
    frames, channels, pixels = features_ref.shape

    def blend(h, _):
        values = jnp.concatenate([v1[:, head(h)], v2[:, head(h)]], axis=0)
        return jnp.dot(p_ref[h], values, preferred_element_type=jnp.float32)

    def settle(h, late):
        late = base_ref[:, head(h)] + late * inverse_ref[:, head(h)]
        out_ref[:, head(h)] = late.astype(jnp.bfloat16)

    staged(out_ref.shape[1] // HEAD_DIM, blend, settle)
    projected = jnp.dot(out_ref[...], w_ref[...], preferred_element_type=jnp.float32)
    turned[...] = projected.T
    parts = [turned[pl.ds(k, channels, stride=4), :] for k in range(4)]
    mixed = jnp.concatenate(parts, axis=1)
    high = mixed.astype(jnp.bfloat16)
    low = (mixed - high.astype(jnp.float32)).astype(jnp.bfloat16)
    placed = jnp.dot(high, place_ref[...], preferred_element_type=jnp.float32)
    placed += jnp.dot(low, place_ref[...], preferred_element_type=jnp.float32)
    for f in range(frames):
        latent = features_ref[f].astype(jnp.float32) + placed[:, f * pixels : (f + 1) * pixels]
        latent = latent.astype(jnp.bfloat16)
        latent_ref[f] = latent
        data = latent.astype(jnp.float32)
        mean_square = jnp.mean(data * data, axis=0, keepdims=True)
        normed = data * lax.rsqrt(mean_square + EPS) * gain_ref[...]
        act_ref[f] = (normed / (1.0 + jnp.exp(-normed))).astype(jnp.bfloat16)


def spread(act, shift_ref, moved):
    channels, pixels = act.shape
    for tap in range(TAPS):
        moved[pl.ds(tap * channels, channels), :] = jnp.dot(
            act, shift_ref[:, tap * pixels : (tap + 1) * pixels],
            preferred_element_type=jnp.float32,
        ).astype(jnp.bfloat16)


def tap_dot(w_ref, lag, moved):
    channels = w_ref.shape[2]
    return sum(
        jnp.dot(
            w_ref[lag * TAPS + tap], moved[pl.ds(tap * channels, channels), :],
            preferred_element_type=jnp.float32,
        )
        for tap in range(TAPS)
    )


def conv_own_kernel(act_ref, shift_ref, w_ref, part_ref, moved0, moved1):
    spread(act_ref[0], shift_ref, moved0)
    spread(act_ref[1], shift_ref, moved1)
    part_ref[0] = tap_dot(w_ref, 2, moved0)
    part_ref[1] = tap_dot(w_ref, 1, moved0) + tap_dot(w_ref, 2, moved1)


def conv_halo_kernel(halo_ref, shift_ref, w_ref, part_ref, latent_ref, out_ref, moved0, moved1):
    spread(halo_ref[0], shift_ref, moved0)
    spread(halo_ref[1], shift_ref, moved1)
    first = part_ref[0] + tap_dot(w_ref, 0, moved0) + tap_dot(w_ref, 1, moved1)
    second = part_ref[1] + tap_dot(w_ref, 0, moved1)
    out_ref[0] = (latent_ref[0].astype(jnp.float32) + first).astype(jnp.bfloat16)
    out_ref[1] = (latent_ref[1].astype(jnp.float32) + second).astype(jnp.bfloat16)


def routes(count):
    own, hop1, swap1, hop2, swap2 = [], [], [], [], []
    for s in range(count):
        r, first, last = s % 4, s < 4, s + 4 >= count
        if r == 0:
            own.append((s, s + 1))
            hop1.append((s, s + 2))
            if not last:
                hop2.append((s, s + 4))
            if not first:
                swap2.append((s, s + 1))
        elif r == 1:
            if not last:
                hop1.append((s, s + 4))
            hop2.append((s, s + 2))
            if not first:
                swap1.append((s, s - 1))
                swap2.append((s, s - 1))
        elif r == 2:
            own.append((s, s + 1))
            if not last:
                hop1.append((s, s - 2))
            swap1.append((s, s + 1))
        else:
            if not last:
                hop1.append((s, s + 4))
            if not first:
                swap1.append((s, s - 1))
                hop2.append((s, s - 2))
            swap2.append((s, s - 1))
    return own, hop1, swap1, hop2, swap2


def shards(queries, keys, values, lookback, proj_weight, features, norm_gain, conv_weight):
    count = lax.axis_size("span")
    me = lax.axis_index("span")
    place = lax.rem(me, 4)
    own, hop1, swap1, hop2, swap2 = routes(count)
    move = functools.partial(lax.ppermute, axis_name="span")

    rows, width = queries.shape
    heads = width // HEAD_DIM
    frames, channels, pixels = features.shape

    block = jax.ShapeDtypeStruct((rows, width), jnp.float32)
    picture = jax.ShapeDtypeStruct(features.shape, jnp.bfloat16)

    distances = jnp.asarray(DISTANCES, jnp.int32)[place]
    bias = jnp.where(distances <= lookback[0], 0.0, -jnp.inf).astype(jnp.float32)

    k_r1 = move(keys, perm=hop1)
    k_s0 = move(keys, perm=own)
    v_r1 = move(values, perm=hop1)
    v_s0 = move(values, perm=own)

    tokens = frames * pixels // (PATCH * PATCH)
    place_matrix, shift_matrix = pl.pallas_call(
        one_hot_kernel,
        out_shape=(
            jax.ShapeDtypeStruct((PATCH * PATCH * tokens, frames * pixels), jnp.bfloat16),
            jax.ShapeDtypeStruct((pixels, TAPS * pixels), jnp.bfloat16),
        ),
        out_specs=(VMEM, VMEM),
        compiler_params=params(),
        name="one_hot",
    )()
    gain = norm_gain.reshape(channels, 1)
    k_r1, place_matrix, shift_matrix, gain, bias = lax.optimization_barrier(
        (k_r1, place_matrix, shift_matrix, gain, bias)
    )

    k_r2 = move(jnp.where(place == 1, keys, k_r1), perm=hop2)
    v_hop = jnp.where(place == 1, values, v_r1)
    v_r2 = move(v_hop, perm=hop2)
    k_r1, v_r1, _ = lax.optimization_barrier((k_r1, v_r1, v_hop))
    k_s1 = move(k_r1, perm=swap1)
    v_s1 = move(v_r1, perm=swap1)

    k_s1, v_s1, k_r1, v_r1 = lax.optimization_barrier((k_s1, v_s1, k_r1, v_r1))
    first_core = lax.rem(place, 2) == 0
    mixed, top, total = pl.pallas_call(
        early_kernel,
        out_shape=(block,) * 3,
        in_specs=[SMEM] + [VMEM] * 7,
        out_specs=(VMEM,) * 3,
        compiler_params=params(),
        name="early",
        cost_estimate=pl.CostEstimate(
            flops=12 * rows * rows * width,
            bytes_accessed=9 * rows * width * 2,
            transcendentals=3 * heads * rows * rows,
        ),
    )(
        bias, queries,
        keys, jnp.where(first_core, k_r1, k_s0), k_s1,
        values, jnp.where(first_core, v_r1, v_s0), v_s1,
    )

    k_s2 = move(k_r2, perm=swap2)
    weights, base, inverse = pl.pallas_call(
        late_kernel,
        out_shape=(
            jax.ShapeDtypeStruct((heads, rows, 2 * rows), jnp.bfloat16), block, block,
        ),
        in_specs=[SMEM] + [VMEM] * 6,
        out_specs=(VMEM,) * 3,
        compiler_params=params(),
        name="late",
        cost_estimate=pl.CostEstimate(
            flops=4 * rows * rows * width,
            bytes_accessed=9 * rows * width * 2,
            transcendentals=2 * heads * rows * rows,
        ),
    )(bias, queries, k_r2, k_s2, mixed, top, total)

    v_r2, weights, base, inverse = lax.optimization_barrier((v_r2, weights, base, inverse))
    v_s2 = move(v_r2, perm=swap2)
    attended, latent, activated = pl.pallas_call(
        latent_kernel,
        out_shape=(jax.ShapeDtypeStruct((rows, width), jnp.bfloat16), picture, picture),
        in_specs=[VMEM] * 9,
        out_specs=(VMEM,) * 3,
        scratch_shapes=[pltpu.VMEM((proj_weight.shape[1], rows), jnp.float32)],
        compiler_params=params(),
        name="latent",
        cost_estimate=pl.CostEstimate(
            flops=2 * rows * width * (2 * rows + proj_weight.shape[1]),
            bytes_accessed=10 * rows * width * 2 + proj_weight.size * 2,
            transcendentals=features.size,
        ),
    )(
        weights, base, inverse, v_r2, v_s2, proj_weight, place_matrix, features, gain,
    )

    halo = move(activated, perm=[(s, s + 1) for s in range(count - 1)])

    moved = [pltpu.VMEM((TAPS * channels, pixels), jnp.bfloat16)] * 2
    conv_cost = pl.CostEstimate(
        flops=2 * channels * TAPS * channels * pixels * 3,
        bytes_accessed=conv_weight.size * 2 + shift_matrix.size * 2,
        transcendentals=0,
    )
    part = pl.pallas_call(
        conv_own_kernel,
        out_shape=jax.ShapeDtypeStruct(features.shape, jnp.float32),
        in_specs=[VMEM] * 3,
        out_specs=VMEM,
        scratch_shapes=moved,
        compiler_params=params(),
        name="conv_own",
        cost_estimate=conv_cost,
    )(activated, shift_matrix, conv_weight)
    decoded = pl.pallas_call(
        conv_halo_kernel,
        out_shape=jax.ShapeDtypeStruct(features.shape, jnp.bfloat16),
        in_specs=[VMEM] * 5,
        out_specs=VMEM,
        scratch_shapes=moved,
        compiler_params=params(),
        name="conv_halo",
        cost_estimate=conv_cost,
    )(halo, shift_matrix, conv_weight, part, latent)
    return (attended, decoded)


def solution(mesh):
    placed = (
        P(("groups", "span"), None),
        P(("groups", "span"), None),
        P(("groups", "span"), None),
        P(("groups", "span")),
        P(),
        P(("groups", "span"), None, None),
        P(),
        P(),
    )
    return jax.shard_map(
        shards,
        mesh=mesh,
        in_specs=placed,
        out_specs=(P(("groups", "span"), None), P(("groups", "span"), None, None)),
        check_vma=False,
    )
```

```python
import functools

import jax
import jax.numpy as jnp
import numpy as np
from jax import lax
from jax.experimental import pallas as pl
from jax.experimental.pallas import tpu as pltpu
from jax.sharding import PartitionSpec as P

HEAD_DIM = 128
LOOKBACK = 3
SIDE = 16
PATCH = 2
TAPS = 9
EPS = 1e-06

VMEM = pl.BlockSpec(memory_space=pltpu.VMEM)
SMEM = pl.BlockSpec(memory_space=pltpu.SMEM)


def params():
    return pltpu.CompilerParams(vmem_limit_bytes=16 * 1024 * 1024)


def one_hot_kernel(place_ref, shift_ref):
    half = SIDE // PATCH
    patches = half * half
    pixels = SIDE * SIDE
    tokens = place_ref.shape[0] // (PATCH * PATCH)
    column = lax.broadcasted_iota(jnp.int32, (tokens, place_ref.shape[1]), 1)
    pixel = column % pixels
    row, col = pixel // SIDE, pixel % SIDE
    token = column // pixels * patches + row // PATCH * half + col // PATCH
    corner = row % PATCH * PATCH + col % PATCH
    hit = lax.broadcasted_iota(jnp.int32, token.shape, 0) == token
    for k in range(PATCH * PATCH):
        place_ref[pl.ds(k * tokens, tokens), :] = jnp.where(
            hit & (corner == k), 1.0, 0.0
        ).astype(jnp.bfloat16)
    source = lax.broadcasted_iota(jnp.int32, (pixels, pixels), 0)
    target = lax.broadcasted_iota(jnp.int32, (pixels, pixels), 1)
    for b in range(3):
        for e in range(3):
            r, c = target // SIDE + b - 1, target % SIDE + e - 1
            inside = (r >= 0) & (r < SIDE) & (c >= 0) & (c < SIDE)
            tap = 3 * b + e
            shift_ref[:, tap * pixels : (tap + 1) * pixels] = jnp.where(
                inside & (source == r * SIDE + c), 1.0, 0.0
            ).astype(jnp.bfloat16)


UNSEEN = LOOKBACK + 1
DISTANCES = ((0, UNSEEN, 3, 2, 1), (0, 1, UNSEEN, 2, 3), (0, 2, 3, UNSEEN, 1), (0, 1, 3, 2, UNSEEN))
RATE = float(np.log2(np.e) * HEAD_DIM**-0.5)


def biases(lookback):
    place = lax.rem(lax.axis_index("span"), 4)
    out = []
    for ways in zip(*DISTANCES):
        distance = ways[0]
        for k, way in enumerate(ways[1:], 1):
            distance = jnp.where(place == k, way, distance)
        out.append(jnp.where(distance <= lookback[0], 0.0, -jnp.inf).astype(jnp.float32))
    return out


def head(h):
    return slice(h * HEAD_DIM, (h + 1) * HEAD_DIM)


def staged(heads, *stages):
    held = {}
    for step in range(heads + len(stages) - 1):
        for i, stage in enumerate(stages):
            h = step - i
            if 0 <= h < heads:
                held[h] = stage(h, held.get(h))


def scores_of(q_ref, blocks, biases, h):
    keys = jnp.concatenate(blocks, axis=0)
    s = lax.dot_general(
        q_ref[:, head(h)], keys, (((1,), (1,)), ((), ())), preferred_element_type=jnp.float32
    )
    rows = blocks[0].shape[0]
    parts = [s[:, i * rows : (i + 1) * rows] for i in range(len(blocks))]
    return [part if bias is None else part + bias for part, bias in zip(parts, biases)]


def top_of(parts):
    return jnp.max(functools.reduce(jnp.maximum, parts), axis=1, keepdims=True)


def early_kernel(
    lookback, q_ref, k0, k_hop, k_own, k2, v0, v_hop, v_own, v2, mixed_ref, top_ref, total_ref
):
    rows = q_ref.shape[0]
    bias = biases(lookback)
    hopped = lax.rem(lax.axis_index("span"), 2) == 0
    ones = jnp.ones((3 * rows, HEAD_DIM), jnp.bfloat16)

    def score(h, _):
        k1 = jnp.where(hopped, k_hop[:, head(h)], k_own[:, head(h)])
        keys = (k0[:, head(h)], k1, k2[:, head(h)])
        return scores_of(q_ref, keys, (None, bias[1], bias[2]), h)

    def soften(h, parts):
        top = top_of(parts)
        top_ref[:, head(h)] = jnp.broadcast_to(top, (rows, HEAD_DIM))
        probs = [jnp.exp2((part - top) * RATE).astype(jnp.bfloat16) for part in parts]
        return jnp.concatenate(probs, axis=1)

    def blend(h, probs):
        v1 = jnp.where(hopped, v_hop[:, head(h)], v_own[:, head(h)])
        values = jnp.concatenate([v0[:, head(h)], v1, v2[:, head(h)]], axis=0)
        both = jnp.dot(
            probs, jnp.concatenate([values, ones], axis=1), preferred_element_type=jnp.float32
        )
        mixed_ref[:, head(h)] = both[:, :HEAD_DIM]
        total_ref[:, head(h)] = both[:, HEAD_DIM:]

    staged(q_ref.shape[1] // HEAD_DIM, score, soften, blend)


def late_kernel(
    lookback, q_ref, k1, k2, mixed_ref, top_ref, total_ref, p_ref, base_ref, inverse_ref
):
    rows = q_ref.shape[0]
    ones = jnp.ones((2 * rows, HEAD_DIM), jnp.bfloat16)
    bias = biases(lookback)

    def score(h, _):
        return scores_of(q_ref, (k1[:, head(h)], k2[:, head(h)]), (bias[3], bias[4]), h)

    def soften(h, parts):
        before = top_ref[:, head(h)]
        top = jnp.maximum(before, top_of(parts))
        probs = [jnp.exp2((part - top) * RATE).astype(jnp.bfloat16) for part in parts]
        probs = jnp.concatenate(probs, axis=1)
        p_ref[h] = probs
        return probs, jnp.exp2((before - top) * RATE)

    def settle(h, held):
        probs, shrink = held
        total = jnp.dot(probs, ones, preferred_element_type=jnp.float32)
        inverse = 1.0 / (total + total_ref[:, head(h)] * shrink)
        inverse_ref[:, head(h)] = inverse
        base_ref[:, head(h)] = mixed_ref[:, head(h)] * (shrink * inverse)

    staged(q_ref.shape[1] // HEAD_DIM, score, soften, settle)


def latent_kernel(
    p_ref, base_ref, inverse_ref, v1, v2, w_ref, place_ref, features_ref, gain_ref,
    out_ref, latent_ref, act_ref, turned,
):
    frames, channels, pixels = features_ref.shape

    def blend(h, _):
        values = jnp.concatenate([v1[:, head(h)], v2[:, head(h)]], axis=0)
        return jnp.dot(p_ref[h], values, preferred_element_type=jnp.float32)

    def settle(h, late):
        late = base_ref[:, head(h)] + late * inverse_ref[:, head(h)]
        out_ref[:, head(h)] = late.astype(jnp.bfloat16)

    staged(out_ref.shape[1] // HEAD_DIM, blend, settle)
    projected = jnp.dot(out_ref[...], w_ref[...], preferred_element_type=jnp.float32)
    turned[...] = projected.T
    parts = [turned[pl.ds(k, channels, stride=4), :] for k in range(4)]
    mixed = jnp.concatenate(parts, axis=1)
    high = mixed.astype(jnp.bfloat16)
    low = (mixed - high.astype(jnp.float32)).astype(jnp.bfloat16)
    placed = jnp.dot(high, place_ref[...], preferred_element_type=jnp.float32)
    placed += jnp.dot(low, place_ref[...], preferred_element_type=jnp.float32)
    gain = jnp.broadcast_to(gain_ref[...], (8, channels)).T[:, :1]
    for f in range(frames):
        latent = features_ref[f].astype(jnp.float32) + placed[:, f * pixels : (f + 1) * pixels]
        latent = latent.astype(jnp.bfloat16)
        latent_ref[f] = latent
        data = latent.astype(jnp.float32)
        mean_square = jnp.mean(data * data, axis=0, keepdims=True)
        normed = data * lax.rsqrt(mean_square + EPS) * gain
        act_ref[f] = (normed / (1.0 + jnp.exp(-normed))).astype(jnp.bfloat16)


def spread(act, shift_ref, moved):
    channels, pixels = act.shape
    for tap in range(TAPS):
        moved[pl.ds(tap * channels, channels), :] = jnp.dot(
            act, shift_ref[:, tap * pixels : (tap + 1) * pixels],
            preferred_element_type=jnp.float32,
        ).astype(jnp.bfloat16)


def tap_dot(w_ref, lag, moved):
    channels = w_ref.shape[2]
    return sum(
        jnp.dot(
            w_ref[lag * TAPS + tap], moved[pl.ds(tap * channels, channels), :],
            preferred_element_type=jnp.float32,
        )
        for tap in range(TAPS)
    )


def conv_own_kernel(act_ref, shift_ref, w_ref, part_ref, moved0, moved1):
    spread(act_ref[0], shift_ref, moved0)
    spread(act_ref[1], shift_ref, moved1)
    part_ref[0] = tap_dot(w_ref, 2, moved0)
    part_ref[1] = tap_dot(w_ref, 1, moved0) + tap_dot(w_ref, 2, moved1)


def conv_halo_kernel(halo_ref, shift_ref, w_ref, part_ref, latent_ref, out_ref, moved0, moved1):
    spread(halo_ref[0], shift_ref, moved0)
    spread(halo_ref[1], shift_ref, moved1)
    first = part_ref[0] + tap_dot(w_ref, 0, moved0) + tap_dot(w_ref, 1, moved1)
    second = part_ref[1] + tap_dot(w_ref, 0, moved1)
    out_ref[0] = (latent_ref[0].astype(jnp.float32) + first).astype(jnp.bfloat16)
    out_ref[1] = (latent_ref[1].astype(jnp.float32) + second).astype(jnp.bfloat16)


def routes(count):
    own, hop1, swap1, hop2, swap2 = [], [], [], [], []
    for s in range(count):
        r, first, last = s % 4, s < 4, s + 4 >= count
        if r == 0:
            own.append((s, s + 1))
            hop1.append((s, s + 2))
            if not last:
                hop2.append((s, s + 4))
            if not first:
                swap2.append((s, s + 1))
        elif r == 1:
            if not last:
                hop1.append((s, s + 4))
            hop2.append((s, s + 2))
            if not first:
                swap1.append((s, s - 1))
                swap2.append((s, s - 1))
        elif r == 2:
            own.append((s, s + 1))
            if not last:
                hop1.append((s, s - 2))
            swap1.append((s, s + 1))
        else:
            if not last:
                hop1.append((s, s + 4))
            if not first:
                swap1.append((s, s - 1))
                hop2.append((s, s - 2))
            swap2.append((s, s - 1))
    return own, hop1, swap1, hop2, swap2


def shards(queries, keys, values, lookback, proj_weight, features, norm_gain, conv_weight):
    count = lax.axis_size("span")
    me = lax.axis_index("span")
    place = lax.rem(me, 4)
    own, hop1, swap1, hop2, swap2 = routes(count)
    move = functools.partial(lax.ppermute, axis_name="span")

    rows, width = queries.shape
    heads = width // HEAD_DIM
    frames, channels, pixels = features.shape

    block = jax.ShapeDtypeStruct((rows, width), jnp.float32)
    picture = jax.ShapeDtypeStruct(features.shape, jnp.bfloat16)

    k_r1 = move(keys, perm=hop1)
    k_s0 = move(keys, perm=own)
    v_r1 = move(values, perm=hop1)
    v_s0 = move(values, perm=own)

    tokens = frames * pixels // (PATCH * PATCH)
    place_matrix, shift_matrix = pl.pallas_call(
        one_hot_kernel,
        out_shape=(
            jax.ShapeDtypeStruct((PATCH * PATCH * tokens, frames * pixels), jnp.bfloat16),
            jax.ShapeDtypeStruct((pixels, TAPS * pixels), jnp.bfloat16),
        ),
        out_specs=(VMEM, VMEM),
        compiler_params=params(),
        name="one_hot",
    )()
    k_r1, place_matrix, shift_matrix = lax.optimization_barrier(
        (k_r1, place_matrix, shift_matrix)
    )

    k_r2 = move(jnp.where(place == 1, keys, k_r1), perm=hop2)
    k_s1 = move(k_r1, perm=swap1)
    v_r2 = move(jnp.where(place == 1, values, v_r1), perm=hop2)
    v_s1 = move(v_r1, perm=swap1)

    mixed, top, total = pl.pallas_call(
        early_kernel,
        out_shape=(block,) * 3,
        in_specs=[SMEM] + [VMEM] * 9,
        out_specs=(VMEM,) * 3,
        compiler_params=params(),
        name="early",
        cost_estimate=pl.CostEstimate(
            flops=12 * rows * rows * width,
            bytes_accessed=9 * rows * width * 2,
            transcendentals=3 * heads * rows * rows,
        ),
    )(
        lookback, queries, keys, k_r1, k_s0, k_s1, values, v_r1, v_s0, v_s1,
    )

    k_s2 = move(k_r2, perm=swap2)
    weights, base, inverse = pl.pallas_call(
        late_kernel,
        out_shape=(
            jax.ShapeDtypeStruct((heads, rows, 2 * rows), jnp.bfloat16), block, block,
        ),
        in_specs=[SMEM] + [VMEM] * 6,
        out_specs=(VMEM,) * 3,
        compiler_params=params(),
        name="late",
        cost_estimate=pl.CostEstimate(
            flops=4 * rows * rows * width,
            bytes_accessed=9 * rows * width * 2,
            transcendentals=2 * heads * rows * rows,
        ),
    )(lookback, queries, k_r2, k_s2, mixed, top, total)

    v_r2, _ = lax.optimization_barrier((v_r2, mixed))
    v_s2 = move(v_r2, perm=swap2)
    attended, latent, activated = pl.pallas_call(
        latent_kernel,
        out_shape=(jax.ShapeDtypeStruct((rows, width), jnp.bfloat16), picture, picture),
        in_specs=[VMEM] * 9,
        out_specs=(VMEM,) * 3,
        scratch_shapes=[pltpu.VMEM((proj_weight.shape[1], rows), jnp.float32)],
        compiler_params=params(),
        name="latent",
        cost_estimate=pl.CostEstimate(
            flops=2 * rows * width * (2 * rows + proj_weight.shape[1]),
            bytes_accessed=10 * rows * width * 2 + proj_weight.size * 2,
            transcendentals=features.size,
        ),
    )(
        weights, base, inverse, v_r2, v_s2, proj_weight, place_matrix, features, norm_gain.reshape(1, channels),
    )

    halo = move(activated, perm=[(s, s + 1) for s in range(count - 1)])

    moved = [pltpu.VMEM((TAPS * channels, pixels), jnp.bfloat16)] * 2
    conv_cost = pl.CostEstimate(
        flops=2 * channels * TAPS * channels * pixels * 3,
        bytes_accessed=conv_weight.size * 2 + shift_matrix.size * 2,
        transcendentals=0,
    )
    part = pl.pallas_call(
        conv_own_kernel,
        out_shape=jax.ShapeDtypeStruct(features.shape, jnp.float32),
        in_specs=[VMEM] * 3,
        out_specs=VMEM,
        scratch_shapes=moved,
        compiler_params=params(),
        name="conv_own",
        cost_estimate=conv_cost,
    )(activated, shift_matrix, conv_weight)
    decoded = pl.pallas_call(
        conv_halo_kernel,
        out_shape=jax.ShapeDtypeStruct(features.shape, jnp.bfloat16),
        in_specs=[VMEM] * 5,
        out_specs=VMEM,
        scratch_shapes=moved,
        compiler_params=params(),
        name="conv_halo",
        cost_estimate=conv_cost,
    )(halo, shift_matrix, conv_weight, part, latent)
    return (attended, decoded)


def solution(mesh):
    placed = (
        P(("groups", "span"), None),
        P(("groups", "span"), None),
        P(("groups", "span"), None),
        P(("groups", "span")),
        P(),
        P(("groups", "span"), None, None),
        P(),
        P(),
    )
    return jax.shard_map(
        shards,
        mesh=mesh,
        in_specs=placed,
        out_specs=(P(("groups", "span"), None), P(("groups", "span"), None, None)),
        check_vma=False,
    )
```

```python
import functools

import jax
import jax.numpy as jnp
import numpy as np
from jax import lax
from jax.experimental import pallas as pl
from jax.experimental.pallas import tpu as pltpu
from jax.sharding import PartitionSpec as P

HEAD_DIM = 128
LOOKBACK = 3
SIDE = 16
PATCH = 2
TAPS = 9
EPS = 1e-06

VMEM = pl.BlockSpec(memory_space=pltpu.VMEM)
SMEM = pl.BlockSpec(memory_space=pltpu.SMEM)


def params():
    return pltpu.CompilerParams(vmem_limit_bytes=16 * 1024 * 1024)


def one_hot_kernel(place_ref, shift_ref):
    half = SIDE // PATCH
    patches = half * half
    pixels = SIDE * SIDE
    tokens = place_ref.shape[0] // (PATCH * PATCH)
    column = lax.broadcasted_iota(jnp.int32, (tokens, place_ref.shape[1]), 1)
    pixel = column % pixels
    row, col = pixel // SIDE, pixel % SIDE
    token = column // pixels * patches + row // PATCH * half + col // PATCH
    corner = row % PATCH * PATCH + col % PATCH
    hit = lax.broadcasted_iota(jnp.int32, token.shape, 0) == token
    for k in range(PATCH * PATCH):
        place_ref[pl.ds(k * tokens, tokens), :] = jnp.where(
            hit & (corner == k), 1.0, 0.0
        ).astype(jnp.bfloat16)
    source = lax.broadcasted_iota(jnp.int32, (pixels, pixels), 0)
    target = lax.broadcasted_iota(jnp.int32, (pixels, pixels), 1)
    for b in range(3):
        for e in range(3):
            r, c = target // SIDE + b - 1, target % SIDE + e - 1
            inside = (r >= 0) & (r < SIDE) & (c >= 0) & (c < SIDE)
            tap = 3 * b + e
            shift_ref[:, tap * pixels : (tap + 1) * pixels] = jnp.where(
                inside & (source == r * SIDE + c), 1.0, 0.0
            ).astype(jnp.bfloat16)


UNSEEN = LOOKBACK + 1
DISTANCES = ((0, UNSEEN, 3, 2, 1), (0, 1, UNSEEN, 2, 3), (0, 2, 3, UNSEEN, 1), (0, 1, 3, 2, UNSEEN))
RATE = float(np.log2(np.e) * HEAD_DIM**-0.5)


def biases(lookback):
    place = lax.rem(lax.axis_index("span"), 4)
    out = []
    for ways in zip(*DISTANCES):
        distance = ways[0]
        for k, way in enumerate(ways[1:], 1):
            distance = jnp.where(place == k, way, distance)
        out.append(jnp.where(distance <= lookback[0], 0.0, -jnp.inf).astype(jnp.float32))
    return out


def head(h):
    return slice(h * HEAD_DIM, (h + 1) * HEAD_DIM)


def staged(heads, *stages):
    held = {}
    for step in range(heads + len(stages) - 1):
        for i, stage in enumerate(stages):
            h = step - i
            if 0 <= h < heads:
                held[h] = stage(h, held.get(h))


def scores_of(q_ref, blocks, biases, h):
    keys = jnp.concatenate(blocks, axis=0)
    s = lax.dot_general(
        q_ref[:, head(h)], keys, (((1,), (1,)), ((), ())), preferred_element_type=jnp.float32
    )
    rows = blocks[0].shape[0]
    parts = [s[:, i * rows : (i + 1) * rows] for i in range(len(blocks))]
    return [part if bias is None else part + bias for part, bias in zip(parts, biases)]


def top_of(parts):
    return jnp.max(functools.reduce(jnp.maximum, parts), axis=1, keepdims=True)


def early_kernel(
    lookback, q_ref, k0, k_hop, k_own, k2, v0, v_hop, v_own, v2, mixed_ref, top_ref, total_ref
):
    rows = q_ref.shape[0]
    bias = biases(lookback)
    hopped = lax.rem(lax.axis_index("span"), 2) == 0
    ones = jnp.ones((3 * rows, HEAD_DIM), jnp.bfloat16)

    def score(h, _):
        k1 = jnp.where(hopped, k_hop[:, head(h)], k_own[:, head(h)])
        keys = (k0[:, head(h)], k1, k2[:, head(h)])
        return scores_of(q_ref, keys, (None, bias[1], bias[2]), h)

    def soften(h, parts):
        top = top_of(parts)
        top_ref[:, head(h)] = jnp.broadcast_to(top, (rows, HEAD_DIM))
        probs = [jnp.exp2((part - top) * RATE).astype(jnp.bfloat16) for part in parts]
        return jnp.concatenate(probs, axis=1)

    def blend(h, probs):
        v1 = jnp.where(hopped, v_hop[:, head(h)], v_own[:, head(h)])
        values = jnp.concatenate([v0[:, head(h)], v1, v2[:, head(h)]], axis=0)
        both = jnp.dot(
            probs, jnp.concatenate([values, ones], axis=1), preferred_element_type=jnp.float32
        )
        mixed_ref[:, head(h)] = both[:, :HEAD_DIM]
        total_ref[:, head(h)] = both[:, HEAD_DIM:]

    staged(q_ref.shape[1] // HEAD_DIM, score, soften, blend)


def late_kernel(
    lookback, q_ref, k1, k2, mixed_ref, top_ref, total_ref, p_ref, base_ref, inverse_ref
):
    rows = q_ref.shape[0]
    ones = jnp.ones((2 * rows, HEAD_DIM), jnp.bfloat16)
    bias = biases(lookback)

    def score(h, _):
        return scores_of(q_ref, (k1[:, head(h)], k2[:, head(h)]), (bias[3], bias[4]), h)

    def soften(h, parts):
        before = top_ref[:, head(h)]
        top = jnp.maximum(before, top_of(parts))
        probs = [jnp.exp2((part - top) * RATE).astype(jnp.bfloat16) for part in parts]
        probs = jnp.concatenate(probs, axis=1)
        p_ref[h] = probs
        return probs, jnp.exp2((before - top) * RATE)

    def settle(h, held):
        probs, shrink = held
        total = jnp.dot(probs, ones, preferred_element_type=jnp.float32)
        inverse = 1.0 / (total + total_ref[:, head(h)] * shrink)
        inverse_ref[:, head(h)] = inverse
        base_ref[:, head(h)] = mixed_ref[:, head(h)] * (shrink * inverse)

    staged(q_ref.shape[1] // HEAD_DIM, score, soften, settle)


def blend_late(heads, shift, p_ref, base_ref, inverse_ref, v1, v2, out_ref):
    def blend(h, _):
        values = jnp.concatenate([v1[:, head(h)], v2[:, head(h)]], axis=0)
        return jnp.dot(p_ref[shift + h], values, preferred_element_type=jnp.float32)

    def settle(h, late):
        late = base_ref[:, head(shift + h)] + late * inverse_ref[:, head(shift + h)]
        out_ref[:, head(h)] = late.astype(jnp.bfloat16)

    staged(heads, blend, settle)


def first_half_kernel(p_ref, base_ref, inverse_ref, v1, v2, w_ref, out_ref, projected_ref):
    width = out_ref.shape[1]
    blend_late(width // HEAD_DIM, 0, p_ref, base_ref, inverse_ref, v1, v2, out_ref)
    projected_ref[...] = jnp.dot(
        out_ref[...], w_ref[:width, :], preferred_element_type=jnp.float32
    )


def latent_kernel(
    p_ref, base_ref, inverse_ref, v1, v2, w_ref, first_ref, begun_ref, place_ref, features_ref,
    gain_ref, out_ref, latent_ref, act_ref, mine, turned, sems,
):
    frames, channels, pixels = features_ref.shape
    before, width = first_ref.shape[1], mine.shape[1]
    copies = [
        pltpu.make_async_copy(first_ref, out_ref.at[:, pl.ds(0, before)], sems.at[0]),
        pltpu.make_async_copy(mine, out_ref.at[:, pl.ds(before, width)], sems.at[1]),
    ]
    copies[0].start()
    blend_late(
        width // HEAD_DIM, before // HEAD_DIM, p_ref, base_ref, inverse_ref, v1, v2, mine
    )
    copies[1].start()
    projected = begun_ref[...] + jnp.dot(
        mine[...], w_ref[before:, :], preferred_element_type=jnp.float32
    )
    turned[...] = projected.T
    parts = [turned[pl.ds(k, channels, stride=4), :] for k in range(4)]
    mixed = jnp.concatenate(parts, axis=1)
    high = mixed.astype(jnp.bfloat16)
    low = (mixed - high.astype(jnp.float32)).astype(jnp.bfloat16)
    placed = jnp.dot(high, place_ref[...], preferred_element_type=jnp.float32)
    placed += jnp.dot(low, place_ref[...], preferred_element_type=jnp.float32)
    gain = jnp.broadcast_to(gain_ref[...], (8, channels)).T[:, :1]
    for f in range(frames):
        latent = features_ref[f].astype(jnp.float32) + placed[:, f * pixels : (f + 1) * pixels]
        latent = latent.astype(jnp.bfloat16)
        latent_ref[f] = latent
        data = latent.astype(jnp.float32)
        mean_square = jnp.mean(data * data, axis=0, keepdims=True)
        normed = data * lax.rsqrt(mean_square + EPS) * gain
        act_ref[f] = (normed / (1.0 + jnp.exp(-normed))).astype(jnp.bfloat16)
    for copy in copies:
        copy.wait()


def spread(act, shift_ref, moved):
    channels, pixels = act.shape
    for tap in range(TAPS):
        moved[pl.ds(tap * channels, channels), :] = jnp.dot(
            act, shift_ref[:, tap * pixels : (tap + 1) * pixels],
            preferred_element_type=jnp.float32,
        ).astype(jnp.bfloat16)


def tap_dot(w_ref, lag, moved):
    channels = w_ref.shape[2]
    return sum(
        jnp.dot(
            w_ref[lag * TAPS + tap], moved[pl.ds(tap * channels, channels), :],
            preferred_element_type=jnp.float32,
        )
        for tap in range(TAPS)
    )


def conv_own_kernel(act_ref, shift_ref, w_ref, part_ref, moved0, moved1):
    spread(act_ref[0], shift_ref, moved0)
    spread(act_ref[1], shift_ref, moved1)
    part_ref[0] = tap_dot(w_ref, 2, moved0)
    part_ref[1] = tap_dot(w_ref, 1, moved0) + tap_dot(w_ref, 2, moved1)


def conv_halo_kernel(halo_ref, shift_ref, w_ref, part_ref, latent_ref, out_ref, moved0, moved1):
    spread(halo_ref[0], shift_ref, moved0)
    spread(halo_ref[1], shift_ref, moved1)
    first = part_ref[0] + tap_dot(w_ref, 0, moved0) + tap_dot(w_ref, 1, moved1)
    second = part_ref[1] + tap_dot(w_ref, 0, moved1)
    out_ref[0] = (latent_ref[0].astype(jnp.float32) + first).astype(jnp.bfloat16)
    out_ref[1] = (latent_ref[1].astype(jnp.float32) + second).astype(jnp.bfloat16)


def routes(count):
    own, hop1, swap1, hop2, swap2 = [], [], [], [], []
    for s in range(count):
        r, first, last = s % 4, s < 4, s + 4 >= count
        if r == 0:
            own.append((s, s + 1))
            hop1.append((s, s + 2))
            if not last:
                hop2.append((s, s + 4))
            if not first:
                swap2.append((s, s + 1))
        elif r == 1:
            if not last:
                hop1.append((s, s + 4))
            hop2.append((s, s + 2))
            if not first:
                swap1.append((s, s - 1))
                swap2.append((s, s - 1))
        elif r == 2:
            own.append((s, s + 1))
            if not last:
                hop1.append((s, s - 2))
            swap1.append((s, s + 1))
        else:
            if not last:
                hop1.append((s, s + 4))
            if not first:
                swap1.append((s, s - 1))
                hop2.append((s, s - 2))
            swap2.append((s, s - 1))
    return own, hop1, swap1, hop2, swap2


def shards(queries, keys, values, lookback, proj_weight, features, norm_gain, conv_weight):
    count = lax.axis_size("span")
    me = lax.axis_index("span")
    place = lax.rem(me, 4)
    own, hop1, swap1, hop2, swap2 = routes(count)
    move = functools.partial(lax.ppermute, axis_name="span")

    rows, width = queries.shape
    heads = width // HEAD_DIM
    frames, channels, pixels = features.shape

    block = jax.ShapeDtypeStruct((rows, width), jnp.float32)
    picture = jax.ShapeDtypeStruct(features.shape, jnp.bfloat16)

    k_r1 = move(keys, perm=hop1)
    k_s0 = move(keys, perm=own)
    v_r1 = move(values, perm=hop1)
    v_s0 = move(values, perm=own)

    tokens = frames * pixels // (PATCH * PATCH)
    place_matrix, shift_matrix = pl.pallas_call(
        one_hot_kernel,
        out_shape=(
            jax.ShapeDtypeStruct((PATCH * PATCH * tokens, frames * pixels), jnp.bfloat16),
            jax.ShapeDtypeStruct((pixels, TAPS * pixels), jnp.bfloat16),
        ),
        out_specs=(VMEM, VMEM),
        compiler_params=params(),
        name="one_hot",
    )()
    k_r1, place_matrix, shift_matrix = lax.optimization_barrier(
        (k_r1, place_matrix, shift_matrix)
    )

    k_r2 = move(jnp.where(place == 1, keys, k_r1), perm=hop2)
    k_s1 = move(k_r1, perm=swap1)
    half = heads // 2 * HEAD_DIM
    halves = slice(0, half), slice(half, width)
    v_hop = jnp.where(place == 1, values[:, halves[0]], v_r1[:, halves[0]])
    v_rest, _ = lax.optimization_barrier((v_r1, v_hop))
    v_rest = jnp.where(place == 1, values[:, halves[1]], v_rest[:, halves[1]])
    v_r2 = [move(part, perm=hop2) for part in (v_hop, v_rest)]
    v_s1 = move(v_r1, perm=swap1)

    mixed, top, total = pl.pallas_call(
        early_kernel,
        out_shape=(block,) * 3,
        in_specs=[SMEM] + [VMEM] * 9,
        out_specs=(VMEM,) * 3,
        compiler_params=params(),
        name="early",
        cost_estimate=pl.CostEstimate(
            flops=12 * rows * rows * width,
            bytes_accessed=9 * rows * width * 2,
            transcendentals=3 * heads * rows * rows,
        ),
    )(
        lookback, queries, keys, k_r1, k_s0, k_s1, values, v_r1, v_s0, v_s1,
    )

    k_s2 = move(k_r2, perm=swap2)
    weights, base, inverse = pl.pallas_call(
        late_kernel,
        out_shape=(
            jax.ShapeDtypeStruct((heads, rows, 2 * rows), jnp.bfloat16), block, block,
        ),
        in_specs=[SMEM] + [VMEM] * 6,
        out_specs=(VMEM,) * 3,
        compiler_params=params(),
        name="late",
        cost_estimate=pl.CostEstimate(
            flops=4 * rows * rows * width,
            bytes_accessed=9 * rows * width * 2,
            transcendentals=2 * heads * rows * rows,
        ),
    )(lookback, queries, k_r2, k_s2, mixed, top, total)

    v_r2[0], _ = lax.optimization_barrier((v_r2[0], mixed))
    v_r2[1], _ = lax.optimization_barrier((v_r2[1], weights))
    v_s2 = [move(part, perm=swap2) for part in v_r2]

    patch_width = proj_weight.shape[1]
    first, begun = pl.pallas_call(
        first_half_kernel,
        out_shape=(
            jax.ShapeDtypeStruct((rows, half), jnp.bfloat16),
            jax.ShapeDtypeStruct((rows, patch_width), jnp.float32),
        ),
        in_specs=[VMEM] * 6,
        out_specs=(VMEM,) * 2,
        compiler_params=params(),
        name="first_half",
        cost_estimate=pl.CostEstimate(
            flops=2 * rows * half * (2 * rows + patch_width),
            bytes_accessed=6 * rows * width + half * patch_width * 2,
            transcendentals=0,
        ),
    )(weights, base, inverse, v_r2[0], v_s2[0], proj_weight)

    attended, latent, activated = pl.pallas_call(
        latent_kernel,
        out_shape=(jax.ShapeDtypeStruct((rows, width), jnp.bfloat16), picture, picture),
        in_specs=[VMEM] * 11,
        out_specs=(pl.BlockSpec(memory_space=pl.ANY), VMEM, VMEM),
        scratch_shapes=[
            pltpu.VMEM((rows, width - half), jnp.bfloat16),
            pltpu.VMEM((patch_width, rows), jnp.float32),
            pltpu.SemaphoreType.DMA((2,)),
        ],
        compiler_params=params(),
        name="latent",
        cost_estimate=pl.CostEstimate(
            flops=2 * rows * (width - half) * (2 * rows + patch_width),
            bytes_accessed=10 * rows * width + (width - half) * patch_width * 2,
            transcendentals=features.size,
        ),
    )(
        weights, base, inverse, v_r2[1], v_s2[1], proj_weight, first, begun,
        place_matrix, features, norm_gain.reshape(1, channels),
    )

    halo = move(activated, perm=[(s, s + 1) for s in range(count - 1)])

    moved = [pltpu.VMEM((TAPS * channels, pixels), jnp.bfloat16)] * 2
    conv_cost = pl.CostEstimate(
        flops=2 * channels * TAPS * channels * pixels * 3,
        bytes_accessed=conv_weight.size * 2 + shift_matrix.size * 2,
        transcendentals=0,
    )
    part = pl.pallas_call(
        conv_own_kernel,
        out_shape=jax.ShapeDtypeStruct(features.shape, jnp.float32),
        in_specs=[VMEM] * 3,
        out_specs=VMEM,
        scratch_shapes=moved,
        compiler_params=params(),
        name="conv_own",
        cost_estimate=conv_cost,
    )(activated, shift_matrix, conv_weight)
    decoded = pl.pallas_call(
        conv_halo_kernel,
        out_shape=jax.ShapeDtypeStruct(features.shape, jnp.bfloat16),
        in_specs=[VMEM] * 5,
        out_specs=VMEM,
        scratch_shapes=moved,
        compiler_params=params(),
        name="conv_halo",
        cost_estimate=conv_cost,
    )(halo, shift_matrix, conv_weight, part, latent)
    return (attended, decoded)


def solution(mesh):
    placed = (
        P(("groups", "span"), None),
        P(("groups", "span"), None),
        P(("groups", "span"), None),
        P(("groups", "span")),
        P(),
        P(("groups", "span"), None, None),
        P(),
        P(),
    )
    return jax.shard_map(
        shards,
        mesh=mesh,
        in_specs=placed,
        out_specs=(P(("groups", "span"), None), P(("groups", "span"), None, None)),
        check_vma=False,
    )
```

```python
import functools

import jax
import jax.numpy as jnp
import numpy as np
from jax import lax
from jax.experimental import pallas as pl
from jax.experimental.pallas import tpu as pltpu
from jax.sharding import PartitionSpec as P

HEAD_DIM = 128
LOOKBACK = 3
SIDE = 16
PATCH = 2
TAPS = 9
EPS = 1e-06

VMEM = pl.BlockSpec(memory_space=pltpu.VMEM)
SMEM = pl.BlockSpec(memory_space=pltpu.SMEM)


def params():
    return pltpu.CompilerParams(vmem_limit_bytes=16 * 1024 * 1024)


def one_hot_kernel(place_ref, shift_ref):
    half = SIDE // PATCH
    patches = half * half
    pixels = SIDE * SIDE
    tokens = place_ref.shape[0] // (PATCH * PATCH)
    column = lax.broadcasted_iota(jnp.int32, (tokens, place_ref.shape[1]), 1)
    pixel = column % pixels
    row, col = pixel // SIDE, pixel % SIDE
    token = column // pixels * patches + row // PATCH * half + col // PATCH
    corner = row % PATCH * PATCH + col % PATCH
    hit = lax.broadcasted_iota(jnp.int32, token.shape, 0) == token
    for k in range(PATCH * PATCH):
        place_ref[pl.ds(k * tokens, tokens), :] = jnp.where(
            hit & (corner == k), 1.0, 0.0
        ).astype(jnp.bfloat16)
    source = lax.broadcasted_iota(jnp.int32, (pixels, pixels), 0)
    target = lax.broadcasted_iota(jnp.int32, (pixels, pixels), 1)
    for b in range(3):
        for e in range(3):
            r, c = target // SIDE + b - 1, target % SIDE + e - 1
            inside = (r >= 0) & (r < SIDE) & (c >= 0) & (c < SIDE)
            tap = 3 * b + e
            shift_ref[:, tap * pixels : (tap + 1) * pixels] = jnp.where(
                inside & (source == r * SIDE + c), 1.0, 0.0
            ).astype(jnp.bfloat16)


UNSEEN = LOOKBACK + 1
DISTANCES = ((0, UNSEEN, 3, 2, 1), (0, 1, UNSEEN, 2, 3), (0, 2, 3, UNSEEN, 1), (0, 1, 3, 2, UNSEEN))
RATE = float(np.log2(np.e) * HEAD_DIM**-0.5)


def biases(lookback):
    place = lax.rem(lax.axis_index("span"), 4)
    out = []
    for ways in zip(*DISTANCES):
        distance = ways[0]
        for k, way in enumerate(ways[1:], 1):
            distance = jnp.where(place == k, way, distance)
        out.append(jnp.where(distance <= lookback[0], 0.0, -jnp.inf).astype(jnp.float32))
    return out


def head(h):
    return slice(h * HEAD_DIM, (h + 1) * HEAD_DIM)


def staged(heads, *stages):
    held = {}
    for step in range(heads + len(stages) - 1):
        for i, stage in enumerate(stages):
            h = step - i
            if 0 <= h < heads:
                held[h] = stage(h, held.get(h))


def scores_of(q_ref, blocks, biases, h):
    keys = jnp.concatenate(blocks, axis=0)
    s = lax.dot_general(
        q_ref[:, head(h)], keys, (((1,), (1,)), ((), ())), preferred_element_type=jnp.float32
    )
    rows = blocks[0].shape[0]
    parts = [s[:, i * rows : (i + 1) * rows] for i in range(len(blocks))]
    return [part if bias is None else part + bias for part, bias in zip(parts, biases)]


def top_of(parts):
    return jnp.max(functools.reduce(jnp.maximum, parts), axis=1, keepdims=True)


def early_kernel(
    lookback, q_ref, k0, k_hop, k_pair, k_hops, v0, v_hop, v_pair, v_hops,
    mixed_ref, top_ref, total_ref
):
    other = 1 - lax.rem(lax.axis_index("span"), 2)
    k_own, v_own = k_pair.at[0], v_pair.at[0]
    k2, v2 = k_hops.at[other], v_hops.at[other]
    rows = q_ref.shape[0]
    bias = biases(lookback)
    hopped = lax.rem(lax.axis_index("span"), 2) == 0
    ones = jnp.ones((3 * rows, HEAD_DIM), jnp.bfloat16)

    def score(h, _):
        k1 = jnp.where(hopped, k_hop[:, head(h)], k_own[:, head(h)])
        keys = (k0[:, head(h)], k1, k2[:, head(h)])
        return scores_of(q_ref, keys, (None, bias[1], bias[2]), h)

    def soften(h, parts):
        top = top_of(parts)
        top_ref[:, head(h)] = jnp.broadcast_to(top, (rows, HEAD_DIM))
        probs = [jnp.exp2((part - top) * RATE).astype(jnp.bfloat16) for part in parts]
        return jnp.concatenate(probs, axis=1)

    def blend(h, probs):
        v1 = jnp.where(hopped, v_hop[:, head(h)], v_own[:, head(h)])
        values = jnp.concatenate([v0[:, head(h)], v1, v2[:, head(h)]], axis=0)
        both = jnp.dot(
            probs, jnp.concatenate([values, ones], axis=1), preferred_element_type=jnp.float32
        )
        mixed_ref[:, head(h)] = both[:, :HEAD_DIM]
        total_ref[:, head(h)] = both[:, HEAD_DIM:]

    staged(q_ref.shape[1] // HEAD_DIM, score, soften, blend)


def late_kernel(
    lookback, q_ref, k1, k2, mixed_ref, top_ref, total_ref, p_ref, base_ref, inverse_ref
):
    rows = q_ref.shape[0]
    ones = jnp.ones((2 * rows, HEAD_DIM), jnp.bfloat16)
    bias = biases(lookback)

    def score(h, _):
        return scores_of(q_ref, (k1[:, head(h)], k2[:, head(h)]), (bias[3], bias[4]), h)

    def soften(h, parts):
        before = top_ref[:, head(h)]
        top = jnp.maximum(before, top_of(parts))
        probs = [jnp.exp2((part - top) * RATE).astype(jnp.bfloat16) for part in parts]
        probs = jnp.concatenate(probs, axis=1)
        p_ref[h] = probs
        return probs, jnp.exp2((before - top) * RATE)

    def settle(h, held):
        probs, shrink = held
        total = jnp.dot(probs, ones, preferred_element_type=jnp.float32)
        inverse = 1.0 / (total + total_ref[:, head(h)] * shrink)
        inverse_ref[:, head(h)] = inverse
        base_ref[:, head(h)] = mixed_ref[:, head(h)] * (shrink * inverse)

    staged(q_ref.shape[1] // HEAD_DIM, score, soften, settle)


def latent_kernel(
    p_ref, base_ref, inverse_ref, v1, v2, w_ref, place_ref, features_ref, gain_ref,
    out_ref, latent_ref, act_ref, mine, turned, sem,
):
    frames, channels, pixels = features_ref.shape

    def blend(h, _):
        values = jnp.concatenate([v1[:, head(h)], v2[:, head(h)]], axis=0)
        return jnp.dot(p_ref[h], values, preferred_element_type=jnp.float32)

    def settle(h, late):
        late = base_ref[:, head(h)] + late * inverse_ref[:, head(h)]
        mine[:, head(h)] = late.astype(jnp.bfloat16)

    staged(mine.shape[1] // HEAD_DIM, blend, settle)
    copy = pltpu.make_async_copy(mine, out_ref, sem)
    copy.start()
    projected = jnp.dot(mine[...], w_ref[...], preferred_element_type=jnp.float32)
    turned[...] = projected.T
    parts = [turned[pl.ds(k, channels, stride=4), :] for k in range(4)]
    mixed = jnp.concatenate(parts, axis=1)
    high = mixed.astype(jnp.bfloat16)
    low = (mixed - high.astype(jnp.float32)).astype(jnp.bfloat16)
    placed = jnp.dot(high, place_ref[...], preferred_element_type=jnp.float32)
    placed += jnp.dot(low, place_ref[...], preferred_element_type=jnp.float32)
    gain = jnp.broadcast_to(gain_ref[...], (8, channels)).T[:, :1]
    for f in range(frames):
        latent = features_ref[f].astype(jnp.float32) + placed[:, f * pixels : (f + 1) * pixels]
        latent = latent.astype(jnp.bfloat16)
        latent_ref[f] = latent
        data = latent.astype(jnp.float32)
        mean_square = jnp.mean(data * data, axis=0, keepdims=True)
        normed = data * lax.rsqrt(mean_square + EPS) * gain
        act_ref[f] = (normed / (1.0 + jnp.exp(-normed))).astype(jnp.bfloat16)
    copy.wait()


def spread(act, shift_ref, moved):
    channels, pixels = act.shape
    for tap in range(TAPS):
        moved[pl.ds(tap * channels, channels), :] = jnp.dot(
            act, shift_ref[:, tap * pixels : (tap + 1) * pixels],
            preferred_element_type=jnp.float32,
        ).astype(jnp.bfloat16)


def tap_dot(w_ref, lag, moved):
    channels = w_ref.shape[2]
    return sum(
        jnp.dot(
            w_ref[lag * TAPS + tap], moved[pl.ds(tap * channels, channels), :],
            preferred_element_type=jnp.float32,
        )
        for tap in range(TAPS)
    )


def conv_own_kernel(act_ref, shift_ref, w_ref, part_ref, moved0, moved1):
    spread(act_ref[0], shift_ref, moved0)
    spread(act_ref[1], shift_ref, moved1)
    part_ref[0] = tap_dot(w_ref, 2, moved0)
    part_ref[1] = tap_dot(w_ref, 1, moved0) + tap_dot(w_ref, 2, moved1)


def conv_halo_kernel(halo_ref, shift_ref, w_ref, part_ref, latent_ref, out_ref, moved0, moved1):
    spread(halo_ref[0], shift_ref, moved0)
    spread(halo_ref[1], shift_ref, moved1)
    first = part_ref[0] + tap_dot(w_ref, 0, moved0) + tap_dot(w_ref, 1, moved1)
    second = part_ref[1] + tap_dot(w_ref, 0, moved1)
    out_ref[0] = (latent_ref[0].astype(jnp.float32) + first).astype(jnp.bfloat16)
    out_ref[1] = (latent_ref[1].astype(jnp.float32) + second).astype(jnp.bfloat16)


def routes(count):
    hop1, hop2, swap2 = [], [], []
    for s in range(count):
        r, first, last = s % 4, s < 4, s + 4 >= count
        if r == 0:
            hop1.append((s, s + 2))
            if not last:
                hop2.append((s, s + 4))
            if not first:
                swap2.append((s, s + 1))
        elif r == 1:
            if not last:
                hop1.append((s, s + 4))
            hop2.append((s, s + 2))
            if not first:
                swap2.append((s, s - 1))
        elif r == 2:
            if not last:
                hop1.append((s, s - 2))
        else:
            if not last:
                hop1.append((s, s + 4))
            if not first:
                hop2.append((s, s - 2))
            swap2.append((s, s - 1))
    return hop1, hop2, swap2


def shards(queries, keys, values, lookback, proj_weight, features, norm_gain, conv_weight):
    count = lax.axis_size("span")
    me = lax.axis_index("span")
    place = lax.rem(me, 4)
    hop1, hop2, swap2 = routes(count)
    move = functools.partial(lax.ppermute, axis_name="span")

    rows, width = queries.shape
    heads = width // HEAD_DIM
    frames, channels, pixels = features.shape

    block = jax.ShapeDtypeStruct((rows, width), jnp.float32)
    picture = jax.ShapeDtypeStruct(features.shape, jnp.bfloat16)

    k_r1 = move(keys, perm=hop1)
    pairs = [[s, s + 1] for s in range(0, count, 2)]

    def shared(value):
        return lax.all_gather(value, "span", axis_index_groups=pairs)

    k_s0 = shared(keys)
    v_r1 = move(values, perm=hop1)
    v_s0 = shared(values)

    tokens = frames * pixels // (PATCH * PATCH)
    place_matrix, shift_matrix = pl.pallas_call(
        one_hot_kernel,
        out_shape=(
            jax.ShapeDtypeStruct((PATCH * PATCH * tokens, frames * pixels), jnp.bfloat16),
            jax.ShapeDtypeStruct((pixels, TAPS * pixels), jnp.bfloat16),
        ),
        out_specs=(VMEM, VMEM),
        compiler_params=params(),
        name="one_hot",
    )()
    k_r1, place_matrix, shift_matrix = lax.optimization_barrier(
        (k_r1, place_matrix, shift_matrix)
    )

    k_hop = jnp.where(place == 1, keys, k_r1)
    k_r2 = move(k_hop, perm=hop2)
    k_s1 = shared(k_r1)
    v_hop = jnp.where(place == 1, values, v_r1)
    v_r2 = move(v_hop, perm=hop2)
    v_in, _ = lax.optimization_barrier((v_r1, (k_hop, v_hop)))
    v_s1 = shared(v_in)

    mixed, top, total = pl.pallas_call(
        early_kernel,
        out_shape=(block,) * 3,
        in_specs=[SMEM] + [VMEM] * 9,
        out_specs=(VMEM,) * 3,
        compiler_params=params(),
        name="early",
        cost_estimate=pl.CostEstimate(
            flops=12 * rows * rows * width,
            bytes_accessed=9 * rows * width * 2,
            transcendentals=3 * heads * rows * rows,
        ),
    )(
        lookback, queries, keys, k_r1, k_s0, k_s1, values, v_r1, v_s0, v_s1,
    )

    k_s2 = move(k_r2, perm=swap2)
    weights, base, inverse = pl.pallas_call(
        late_kernel,
        out_shape=(
            jax.ShapeDtypeStruct((heads, rows, 2 * rows), jnp.bfloat16), block, block,
        ),
        in_specs=[SMEM] + [VMEM] * 6,
        out_specs=(VMEM,) * 3,
        compiler_params=params(),
        name="late",
        cost_estimate=pl.CostEstimate(
            flops=4 * rows * rows * width,
            bytes_accessed=9 * rows * width * 2,
            transcendentals=2 * heads * rows * rows,
        ),
    )(lookback, queries, k_r2, k_s2, mixed, top, total)

    v_r2, _ = lax.optimization_barrier((v_r2, mixed))
    v_s2 = move(v_r2, perm=swap2)
    patch_width = proj_weight.shape[1]
    attended, latent, activated = pl.pallas_call(
        latent_kernel,
        out_shape=(jax.ShapeDtypeStruct((rows, width), jnp.bfloat16), picture, picture),
        in_specs=[VMEM] * 9,
        out_specs=(pl.BlockSpec(memory_space=pl.ANY), VMEM, VMEM),
        scratch_shapes=[
            pltpu.VMEM((rows, width), jnp.bfloat16),
            pltpu.VMEM((patch_width, rows), jnp.float32),
            pltpu.SemaphoreType.DMA,
        ],
        compiler_params=params(),
        name="latent",
        cost_estimate=pl.CostEstimate(
            flops=2 * rows * width * (2 * rows + patch_width),
            bytes_accessed=10 * rows * width * 2 + width * patch_width * 2,
            transcendentals=features.size,
        ),
    )(
        weights, base, inverse, v_r2, v_s2, proj_weight, place_matrix, features,
        norm_gain.reshape(1, channels),
    )

    halo = move(activated, perm=[(s, s + 1) for s in range(count - 1)])

    moved = [pltpu.VMEM((TAPS * channels, pixels), jnp.bfloat16)] * 2
    conv_cost = pl.CostEstimate(
        flops=2 * channels * TAPS * channels * pixels * 3,
        bytes_accessed=conv_weight.size * 2 + shift_matrix.size * 2,
        transcendentals=0,
    )
    part = pl.pallas_call(
        conv_own_kernel,
        out_shape=jax.ShapeDtypeStruct(features.shape, jnp.float32),
        in_specs=[VMEM] * 3,
        out_specs=VMEM,
        scratch_shapes=moved,
        compiler_params=params(),
        name="conv_own",
        cost_estimate=conv_cost,
    )(activated, shift_matrix, conv_weight)
    decoded = pl.pallas_call(
        conv_halo_kernel,
        out_shape=jax.ShapeDtypeStruct(features.shape, jnp.bfloat16),
        in_specs=[VMEM] * 5,
        out_specs=VMEM,
        scratch_shapes=moved,
        compiler_params=params(),
        name="conv_halo",
        cost_estimate=conv_cost,
    )(halo, shift_matrix, conv_weight, part, latent)
    return (attended, decoded)


def solution(mesh):
    placed = (
        P(("groups", "span"), None),
        P(("groups", "span"), None),
        P(("groups", "span"), None),
        P(("groups", "span")),
        P(),
        P(("groups", "span"), None, None),
        P(),
        P(),
    )
    return jax.shard_map(
        shards,
        mesh=mesh,
        in_specs=placed,
        out_specs=(P(("groups", "span"), None), P(("groups", "span"), None, None)),
        check_vma=False,
    )
```

```python
import functools

import jax
import jax.numpy as jnp
import numpy as np
from jax import lax
from jax.experimental import pallas as pl
from jax.experimental.pallas import tpu as pltpu
from jax.sharding import PartitionSpec as P

HEAD_DIM = 128
LOOKBACK = 3
SIDE = 16
PATCH = 2
TAPS = 9
EPS = 1e-06

VMEM = pl.BlockSpec(memory_space=pltpu.VMEM)
SMEM = pl.BlockSpec(memory_space=pltpu.SMEM)


def params():
    return pltpu.CompilerParams(vmem_limit_bytes=16 * 1024 * 1024)


def one_hot_kernel(place_ref, shift_ref):
    half = SIDE // PATCH
    patches = half * half
    pixels = SIDE * SIDE
    tokens = place_ref.shape[0] // (PATCH * PATCH)
    column = lax.broadcasted_iota(jnp.int32, (tokens, place_ref.shape[1]), 1)
    pixel = column % pixels
    row, col = pixel // SIDE, pixel % SIDE
    token = column // pixels * patches + row // PATCH * half + col // PATCH
    corner = row % PATCH * PATCH + col % PATCH
    hit = lax.broadcasted_iota(jnp.int32, token.shape, 0) == token
    for k in range(PATCH * PATCH):
        place_ref[pl.ds(k * tokens, tokens), :] = jnp.where(
            hit & (corner == k), 1.0, 0.0
        ).astype(jnp.bfloat16)
    source = lax.broadcasted_iota(jnp.int32, (pixels, pixels), 0)
    target = lax.broadcasted_iota(jnp.int32, (pixels, pixels), 1)
    for b in range(3):
        for e in range(3):
            r, c = target // SIDE + b - 1, target % SIDE + e - 1
            inside = (r >= 0) & (r < SIDE) & (c >= 0) & (c < SIDE)
            tap = 3 * b + e
            shift_ref[:, tap * pixels : (tap + 1) * pixels] = jnp.where(
                inside & (source == r * SIDE + c), 1.0, 0.0
            ).astype(jnp.bfloat16)


UNSEEN = LOOKBACK + 1
DISTANCES = ((0, UNSEEN, 3, 2, 1), (0, 1, UNSEEN, 2, 3), (0, 2, 3, UNSEEN, 1), (0, 1, 3, 2, UNSEEN))
RATE = float(np.log2(np.e) * HEAD_DIM**-0.5)


def biases(lookback):
    place = lax.rem(lax.axis_index("span"), 4)
    out = []
    for ways in zip(*DISTANCES):
        distance = ways[0]
        for k, way in enumerate(ways[1:], 1):
            distance = jnp.where(place == k, way, distance)
        out.append(jnp.where(distance <= lookback[0], 0.0, -jnp.inf).astype(jnp.float32))
    return out


def head(h):
    return slice(h * HEAD_DIM, (h + 1) * HEAD_DIM)


def staged(heads, *stages):
    held = {}
    for step in range(heads + len(stages) - 1):
        for i, stage in enumerate(stages):
            h = step - i
            if 0 <= h < heads:
                held[h] = stage(h, held.get(h))


def scores_of(q_ref, blocks, biases, h):
    keys = jnp.concatenate(blocks, axis=0)
    s = lax.dot_general(
        q_ref[:, head(h)], keys, (((1,), (1,)), ((), ())), preferred_element_type=jnp.float32
    )
    rows = blocks[0].shape[0]
    parts = [s[:, i * rows : (i + 1) * rows] for i in range(len(blocks))]
    return [part if bias is None else part + bias for part, bias in zip(parts, biases)]


def top_of(parts):
    return jnp.max(functools.reduce(jnp.maximum, parts), axis=1, keepdims=True)


def early_kernel(
    lookback, q_ref, k0, k_hop, k_own, k2, v0, v_hop, v_own, v2, mixed_ref, top_ref, total_ref
):
    rows = q_ref.shape[0]
    bias = biases(lookback)
    hopped = lax.rem(lax.axis_index("span"), 2) == 0
    ones = jnp.ones((3 * rows, HEAD_DIM), jnp.bfloat16)

    def score(h, _):
        k1 = jnp.where(hopped, k_hop[:, head(h)], k_own[:, head(h)])
        keys = (k0[:, head(h)], k1, k2[:, head(h)])
        return scores_of(q_ref, keys, (None, bias[1], bias[2]), h)

    def soften(h, parts):
        top = top_of(parts)
        top_ref[:, head(h)] = jnp.broadcast_to(top, (rows, HEAD_DIM))
        probs = [jnp.exp2((part - top) * RATE).astype(jnp.bfloat16) for part in parts]
        return jnp.concatenate(probs, axis=1)

    def blend(h, probs):
        v1 = jnp.where(hopped, v_hop[:, head(h)], v_own[:, head(h)])
        values = jnp.concatenate([v0[:, head(h)], v1, v2[:, head(h)]], axis=0)
        both = jnp.dot(
            probs, jnp.concatenate([values, ones], axis=1), preferred_element_type=jnp.float32
        )
        mixed_ref[:, head(h)] = both[:, :HEAD_DIM]
        total_ref[:, head(h)] = both[:, HEAD_DIM:]

    staged(q_ref.shape[1] // HEAD_DIM, score, soften, blend)


def late_kernel(
    lookback, q_ref, k1, k2, mixed_ref, top_ref, total_ref, p_ref, base_ref, inverse_ref
):
    rows = q_ref.shape[0]
    ones = jnp.ones((2 * rows, HEAD_DIM), jnp.bfloat16)
    bias = biases(lookback)

    def score(h, _):
        return scores_of(q_ref, (k1[:, head(h)], k2[:, head(h)]), (bias[3], bias[4]), h)

    def soften(h, parts):
        before = top_ref[:, head(h)]
        top = jnp.maximum(before, top_of(parts))
        probs = [jnp.exp2((part - top) * RATE).astype(jnp.bfloat16) for part in parts]
        probs = jnp.concatenate(probs, axis=1)
        p_ref[h] = probs
        return probs, jnp.exp2((before - top) * RATE)

    def settle(h, held):
        probs, shrink = held
        total = jnp.dot(probs, ones, preferred_element_type=jnp.float32)
        inverse = 1.0 / (total + total_ref[:, head(h)] * shrink)
        inverse_ref[:, head(h)] = inverse
        base_ref[:, head(h)] = mixed_ref[:, head(h)] * (shrink * inverse)

    staged(q_ref.shape[1] // HEAD_DIM, score, soften, settle)


def latent_kernel(
    p_ref, base_ref, inverse_ref, v1, v2, w_ref, place_ref, features_ref, gain_ref,
    out_ref, latent_ref, act_ref, mine, turned, sem,
):
    frames, channels, pixels = features_ref.shape

    def blend(h, _):
        values = jnp.concatenate([v1[:, head(h)], v2[:, head(h)]], axis=0)
        return jnp.dot(p_ref[h], values, preferred_element_type=jnp.float32)

    def settle(h, late):
        late = base_ref[:, head(h)] + late * inverse_ref[:, head(h)]
        mine[:, head(h)] = late.astype(jnp.bfloat16)

    staged(mine.shape[1] // HEAD_DIM, blend, settle)
    copy = pltpu.make_async_copy(mine, out_ref, sem)
    copy.start()
    projected = jnp.dot(mine[...], w_ref[...], preferred_element_type=jnp.float32)
    turned[...] = projected.T
    parts = [turned[pl.ds(k, channels, stride=4), :] for k in range(4)]
    mixed = jnp.concatenate(parts, axis=1)
    high = mixed.astype(jnp.bfloat16)
    low = (mixed - high.astype(jnp.float32)).astype(jnp.bfloat16)
    placed = jnp.dot(high, place_ref[...], preferred_element_type=jnp.float32)
    placed += jnp.dot(low, place_ref[...], preferred_element_type=jnp.float32)
    gain = jnp.broadcast_to(gain_ref[...], (8, channels)).T[:, :1]
    for f in range(frames):
        latent = features_ref[f].astype(jnp.float32) + placed[:, f * pixels : (f + 1) * pixels]
        latent = latent.astype(jnp.bfloat16)
        latent_ref[f] = latent
        data = latent.astype(jnp.float32)
        mean_square = jnp.mean(data * data, axis=0, keepdims=True)
        normed = data * lax.rsqrt(mean_square + EPS) * gain
        act_ref[f] = (normed / (1.0 + jnp.exp(-normed))).astype(jnp.bfloat16)
    copy.wait()


def spread(act, shift_ref, moved):
    channels, pixels = act.shape
    for tap in range(TAPS):
        moved[pl.ds(tap * channels, channels), :] = jnp.dot(
            act, shift_ref[:, tap * pixels : (tap + 1) * pixels],
            preferred_element_type=jnp.float32,
        ).astype(jnp.bfloat16)


def tap_dot(w_ref, lag, moved):
    channels = w_ref.shape[2]
    return sum(
        jnp.dot(
            w_ref[lag * TAPS + tap], moved[pl.ds(tap * channels, channels), :],
            preferred_element_type=jnp.float32,
        )
        for tap in range(TAPS)
    )


def conv_own_kernel(act_ref, shift_ref, w_ref, part_ref, moved0, moved1):
    spread(act_ref[0], shift_ref, moved0)
    spread(act_ref[1], shift_ref, moved1)
    part_ref[0] = tap_dot(w_ref, 2, moved0)
    part_ref[1] = tap_dot(w_ref, 1, moved0) + tap_dot(w_ref, 2, moved1)


def conv_halo_kernel(halo_ref, shift_ref, w_ref, part_ref, latent_ref, out_ref, moved0, moved1):
    spread(halo_ref[0], shift_ref, moved0)
    spread(halo_ref[1], shift_ref, moved1)
    first = part_ref[0] + tap_dot(w_ref, 0, moved0) + tap_dot(w_ref, 1, moved1)
    second = part_ref[1] + tap_dot(w_ref, 0, moved1)
    out_ref[0] = (latent_ref[0].astype(jnp.float32) + first).astype(jnp.bfloat16)
    out_ref[1] = (latent_ref[1].astype(jnp.float32) + second).astype(jnp.bfloat16)


def routes(count):
    own, hop1, swap1, hop2, swap2 = [], [], [], [], []
    for s in range(count):
        r, first, last = s % 4, s < 4, s + 4 >= count
        if r == 0:
            own.append((s, s + 1))
            hop1.append((s, s + 2))
            if not last:
                hop2.append((s, s + 4))
            if not first:
                swap2.append((s, s + 1))
        elif r == 1:
            if not last:
                hop1.append((s, s + 4))
            hop2.append((s, s + 2))
            if not first:
                swap1.append((s, s - 1))
                swap2.append((s, s - 1))
        elif r == 2:
            own.append((s, s + 1))
            if not last:
                hop1.append((s, s - 2))
            swap1.append((s, s + 1))
        else:
            if not last:
                hop1.append((s, s + 4))
            if not first:
                swap1.append((s, s - 1))
                hop2.append((s, s - 2))
            swap2.append((s, s - 1))
    return own, hop1, swap1, hop2, swap2


def shards(queries, keys, values, lookback, proj_weight, features, norm_gain, conv_weight):
    count = lax.axis_size("span")
    me = lax.axis_index("span")
    second = lax.rem(me, 4) == 1
    second, keys, values = lax.optimization_barrier((second, keys, values))
    own, hop1, swap1, hop2, swap2 = routes(count)
    move = functools.partial(lax.ppermute, axis_name="span")

    rows, width = queries.shape
    heads = width // HEAD_DIM
    frames, channels, pixels = features.shape

    block = jax.ShapeDtypeStruct((rows, width), jnp.float32)
    picture = jax.ShapeDtypeStruct(features.shape, jnp.bfloat16)

    k_r1 = move(keys, perm=hop1)
    k_s0 = move(keys, perm=own)
    v_r1 = move(values, perm=hop1)
    v_s0 = move(values, perm=own)

    tokens = frames * pixels // (PATCH * PATCH)
    place_matrix, shift_matrix = pl.pallas_call(
        one_hot_kernel,
        out_shape=(
            jax.ShapeDtypeStruct((PATCH * PATCH * tokens, frames * pixels), jnp.bfloat16),
            jax.ShapeDtypeStruct((pixels, TAPS * pixels), jnp.bfloat16),
        ),
        out_specs=(VMEM, VMEM),
        compiler_params=params(),
        name="one_hot",
    )()
    k_r1, place_matrix, shift_matrix = lax.optimization_barrier(
        (k_r1, place_matrix, shift_matrix)
    )

    k_r2 = move(jnp.where(second, keys, k_r1), perm=hop2)
    k_s1 = move(k_r1, perm=swap1)
    v_hop = jnp.where(second, values, v_r1)
    v_r2 = move(v_hop, perm=hop2)
    v_s1 = move(v_r1, perm=swap1)

    mixed, top, total = pl.pallas_call(
        early_kernel,
        out_shape=(block,) * 3,
        in_specs=[SMEM] + [VMEM] * 9,
        out_specs=(VMEM,) * 3,
        compiler_params=params(),
        name="early",
        cost_estimate=pl.CostEstimate(
            flops=12 * rows * rows * width,
            bytes_accessed=9 * rows * width * 2,
            transcendentals=3 * heads * rows * rows,
        ),
    )(
        lookback, queries, keys, k_r1, k_s0, k_s1, values, v_r1, v_s0, v_s1,
    )

    k_s2 = move(k_r2, perm=swap2)
    weights, base, inverse = pl.pallas_call(
        late_kernel,
        out_shape=(
            jax.ShapeDtypeStruct((heads, rows, 2 * rows), jnp.bfloat16), block, block,
        ),
        in_specs=[SMEM] + [VMEM] * 6,
        out_specs=(VMEM,) * 3,
        compiler_params=params(),
        name="late",
        cost_estimate=pl.CostEstimate(
            flops=4 * rows * rows * width,
            bytes_accessed=9 * rows * width * 2,
            transcendentals=2 * heads * rows * rows,
        ),
    )(lookback, queries, k_r2, k_s2, mixed, top, total)

    v_r2, _ = lax.optimization_barrier((v_r2, mixed))
    v_s2 = move(v_r2, perm=swap2)
    patch_width = proj_weight.shape[1]
    attended, latent, activated = pl.pallas_call(
        latent_kernel,
        out_shape=(jax.ShapeDtypeStruct((rows, width), jnp.bfloat16), picture, picture),
        in_specs=[VMEM] * 9,
        out_specs=(pl.BlockSpec(memory_space=pl.ANY), VMEM, VMEM),
        scratch_shapes=[
            pltpu.VMEM((rows, width), jnp.bfloat16),
            pltpu.VMEM((patch_width, rows), jnp.float32),
            pltpu.SemaphoreType.DMA,
        ],
        compiler_params=params(),
        name="latent",
        cost_estimate=pl.CostEstimate(
            flops=2 * rows * width * (2 * rows + patch_width),
            bytes_accessed=10 * rows * width * 2 + width * patch_width * 2,
            transcendentals=features.size,
        ),
    )(
        weights, base, inverse, v_r2, v_s2, proj_weight, place_matrix, features,
        norm_gain.reshape(1, channels),
    )

    halo = move(activated, perm=[(s, s + 1) for s in range(count - 1)])

    moved = [pltpu.VMEM((TAPS * channels, pixels), jnp.bfloat16)] * 2
    conv_cost = pl.CostEstimate(
        flops=2 * channels * TAPS * channels * pixels * 3,
        bytes_accessed=conv_weight.size * 2 + shift_matrix.size * 2,
        transcendentals=0,
    )
    part = pl.pallas_call(
        conv_own_kernel,
        out_shape=jax.ShapeDtypeStruct(features.shape, jnp.float32),
        in_specs=[VMEM] * 3,
        out_specs=VMEM,
        scratch_shapes=moved,
        compiler_params=params(),
        name="conv_own",
        cost_estimate=conv_cost,
    )(activated, shift_matrix, conv_weight)
    decoded = pl.pallas_call(
        conv_halo_kernel,
        out_shape=jax.ShapeDtypeStruct(features.shape, jnp.bfloat16),
        in_specs=[VMEM] * 5,
        out_specs=VMEM,
        scratch_shapes=moved,
        compiler_params=params(),
        name="conv_halo",
        cost_estimate=conv_cost,
    )(halo, shift_matrix, conv_weight, part, latent)
    return (attended, decoded)


def solution(mesh):
    placed = (
        P(("groups", "span"), None),
        P(("groups", "span"), None),
        P(("groups", "span"), None),
        P(("groups", "span")),
        P(),
        P(("groups", "span"), None, None),
        P(),
        P(),
    )
    return jax.shard_map(
        shards,
        mesh=mesh,
        in_specs=placed,
        out_specs=(P(("groups", "span"), None), P(("groups", "span"), None, None)),
        check_vma=False,
    )
```

```python
import functools

import jax
import jax.numpy as jnp
import numpy as np
from jax import lax
from jax.experimental import pallas as pl
from jax.experimental.pallas import tpu as pltpu
from jax.sharding import PartitionSpec as P

HEAD_DIM = 128
LOOKBACK = 3
SIDE = 16
PATCH = 2
TAPS = 9
EPS = 1e-06

VMEM = pl.BlockSpec(memory_space=pltpu.VMEM)
SMEM = pl.BlockSpec(memory_space=pltpu.SMEM)


def params():
    return pltpu.CompilerParams(vmem_limit_bytes=16 * 1024 * 1024)


def one_hot_kernel(place_ref, shift_ref):
    half = SIDE // PATCH
    patches = half * half
    pixels = SIDE * SIDE
    tokens = place_ref.shape[0] // (PATCH * PATCH)
    column = lax.broadcasted_iota(jnp.int32, (tokens, place_ref.shape[1]), 1)
    pixel = column % pixels
    row, col = pixel // SIDE, pixel % SIDE
    token = column // pixels * patches + row // PATCH * half + col // PATCH
    corner = row % PATCH * PATCH + col % PATCH
    hit = lax.broadcasted_iota(jnp.int32, token.shape, 0) == token
    for k in range(PATCH * PATCH):
        place_ref[pl.ds(k * tokens, tokens), :] = jnp.where(
            hit & (corner == k), 1.0, 0.0
        ).astype(jnp.bfloat16)
    source = lax.broadcasted_iota(jnp.int32, (pixels, pixels), 0)
    target = lax.broadcasted_iota(jnp.int32, (pixels, pixels), 1)
    for b in range(3):
        for e in range(3):
            r, c = target // SIDE + b - 1, target % SIDE + e - 1
            inside = (r >= 0) & (r < SIDE) & (c >= 0) & (c < SIDE)
            tap = 3 * b + e
            shift_ref[:, tap * pixels : (tap + 1) * pixels] = jnp.where(
                inside & (source == r * SIDE + c), 1.0, 0.0
            ).astype(jnp.bfloat16)


UNSEEN = LOOKBACK + 1
DISTANCES = ((0, UNSEEN, 3, 2, 1), (0, 1, UNSEEN, 2, 3), (0, 2, 3, UNSEEN, 1), (0, 1, 3, 2, UNSEEN))
RATE = float(np.log2(np.e) * HEAD_DIM**-0.5)


def biases(lookback):
    place = lax.rem(lax.axis_index("span"), 4)
    out = []
    for ways in zip(*DISTANCES):
        distance = ways[0]
        for k, way in enumerate(ways[1:], 1):
            distance = jnp.where(place == k, way, distance)
        out.append(jnp.where(distance <= lookback[0], 0.0, -jnp.inf).astype(jnp.float32))
    return out


def head(h):
    return slice(h * HEAD_DIM, (h + 1) * HEAD_DIM)


def staged(heads, *stages):
    held = {}
    for step in range(heads + len(stages) - 1):
        for i, stage in enumerate(stages):
            h = step - i
            if 0 <= h < heads:
                held[h] = stage(h, held.get(h))


def scores_of(q_ref, blocks, biases, h):
    keys = jnp.concatenate(blocks, axis=0)
    s = lax.dot_general(
        q_ref[:, head(h)], keys, (((1,), (1,)), ((), ())), preferred_element_type=jnp.float32
    )
    rows = blocks[0].shape[0]
    parts = [s[:, i * rows : (i + 1) * rows] for i in range(len(blocks))]
    return [part if bias is None else part + bias for part, bias in zip(parts, biases)]


def top_of(parts):
    return jnp.max(functools.reduce(jnp.maximum, parts), axis=1, keepdims=True)


def early_kernel(
    lookback, q_ref, k0, k_hop, k_own, k2, v0, v_hop, v_own, v2, mixed_ref, top_ref, total_ref
):
    rows = q_ref.shape[0]
    bias = biases(lookback)
    hopped = lax.rem(lax.axis_index("span"), 2) == 0
    ones = jnp.ones((3 * rows, HEAD_DIM), jnp.bfloat16)

    def score(h, _):
        k1 = jnp.where(hopped, k_hop[:, head(h)], k_own[:, head(h)])
        keys = (k0[:, head(h)], k1, k2[:, head(h)])
        return scores_of(q_ref, keys, (None, bias[1], bias[2]), h)

    def soften(h, parts):
        top = top_of(parts)
        top_ref[:, head(h)] = jnp.broadcast_to(top, (rows, HEAD_DIM))
        probs = [jnp.exp2((part - top) * RATE).astype(jnp.bfloat16) for part in parts]
        return jnp.concatenate(probs, axis=1)

    def blend(h, probs):
        v1 = jnp.where(hopped, v_hop[:, head(h)], v_own[:, head(h)])
        values = jnp.concatenate([v0[:, head(h)], v1, v2[:, head(h)]], axis=0)
        both = jnp.dot(
            probs, jnp.concatenate([values, ones], axis=1), preferred_element_type=jnp.float32
        )
        mixed_ref[:, head(h)] = both[:, :HEAD_DIM]
        total_ref[:, head(h)] = both[:, HEAD_DIM:]

    staged(q_ref.shape[1] // HEAD_DIM, score, soften, blend)


def late_kernel(
    lookback, q_ref, k1, k2, mixed_ref, top_ref, total_ref, p_ref, base_ref, inverse_ref
):
    rows = q_ref.shape[0]
    ones = jnp.ones((2 * rows, HEAD_DIM), jnp.bfloat16)
    bias = biases(lookback)

    def score(h, _):
        return scores_of(q_ref, (k1[:, head(h)], k2[:, head(h)]), (bias[3], bias[4]), h)

    def soften(h, parts):
        before = top_ref[:, head(h)]
        top = jnp.maximum(before, top_of(parts))
        probs = [jnp.exp2((part - top) * RATE).astype(jnp.bfloat16) for part in parts]
        probs = jnp.concatenate(probs, axis=1)
        p_ref[h] = probs
        return probs, jnp.exp2((before - top) * RATE)

    def settle(h, held):
        probs, shrink = held
        total = jnp.dot(probs, ones, preferred_element_type=jnp.float32)
        inverse = 1.0 / (total + total_ref[:, head(h)] * shrink)
        inverse_ref[:, head(h)] = inverse
        base_ref[:, head(h)] = mixed_ref[:, head(h)] * (shrink * inverse)

    staged(q_ref.shape[1] // HEAD_DIM, score, soften, settle)


def latent_kernel(
    p_ref, base_ref, inverse_ref, v1, v2, w_ref, place_ref, features_ref, gain_ref,
    out_ref, latent_ref, act_ref, mine, turned, sem,
):
    frames, channels, pixels = features_ref.shape

    def blend(h, _):
        values = jnp.concatenate([v1[:, head(h)], v2[:, head(h)]], axis=0)
        return jnp.dot(p_ref[h], values, preferred_element_type=jnp.float32)

    def settle(h, late):
        late = base_ref[:, head(h)] + late * inverse_ref[:, head(h)]
        mine[:, head(h)] = late.astype(jnp.bfloat16)

    staged(mine.shape[1] // HEAD_DIM, blend, settle)
    copy = pltpu.make_async_copy(mine, out_ref, sem)
    copy.start()
    projected = jnp.dot(mine[...], w_ref[...], preferred_element_type=jnp.float32)
    turned[...] = projected.T
    parts = [turned[pl.ds(k, channels, stride=4), :] for k in range(4)]
    mixed = jnp.concatenate(parts, axis=1)
    high = mixed.astype(jnp.bfloat16)
    low = (mixed - high.astype(jnp.float32)).astype(jnp.bfloat16)
    placed = jnp.dot(high, place_ref[...], preferred_element_type=jnp.float32)
    placed += jnp.dot(low, place_ref[...], preferred_element_type=jnp.float32)
    gain = jnp.broadcast_to(gain_ref[...], (8, channels)).T[:, :1]
    for f in range(frames):
        latent = features_ref[f].astype(jnp.float32) + placed[:, f * pixels : (f + 1) * pixels]
        latent = latent.astype(jnp.bfloat16)
        latent_ref[f] = latent
        data = latent.astype(jnp.float32)
        mean_square = jnp.mean(data * data, axis=0, keepdims=True)
        normed = data * lax.rsqrt(mean_square + EPS) * gain
        act_ref[f] = (normed / (1.0 + jnp.exp(-normed))).astype(jnp.bfloat16)
    copy.wait()


def spread(act, shift_ref, moved):
    channels, pixels = act.shape
    for tap in range(TAPS):
        moved[pl.ds(tap * channels, channels), :] = jnp.dot(
            act, shift_ref[:, tap * pixels : (tap + 1) * pixels],
            preferred_element_type=jnp.float32,
        ).astype(jnp.bfloat16)


def tap_dot(w_ref, lag, moved):
    channels = w_ref.shape[2]
    return sum(
        jnp.dot(
            w_ref[lag * TAPS + tap], moved[pl.ds(tap * channels, channels), :],
            preferred_element_type=jnp.float32,
        )
        for tap in range(TAPS)
    )


def conv_own_kernel(act_ref, shift_ref, w_ref, part_ref, moved0, moved1):
    spread(act_ref[0], shift_ref, moved0)
    spread(act_ref[1], shift_ref, moved1)
    part_ref[0] = tap_dot(w_ref, 2, moved0)
    part_ref[1] = tap_dot(w_ref, 1, moved0) + tap_dot(w_ref, 2, moved1)


def conv_halo_kernel(halo_ref, shift_ref, w_ref, part_ref, latent_ref, out_ref, moved0, moved1):
    spread(halo_ref[0], shift_ref, moved0)
    spread(halo_ref[1], shift_ref, moved1)
    first = part_ref[0] + tap_dot(w_ref, 0, moved0) + tap_dot(w_ref, 1, moved1)
    second = part_ref[1] + tap_dot(w_ref, 0, moved1)
    out_ref[0] = (latent_ref[0].astype(jnp.float32) + first).astype(jnp.bfloat16)
    out_ref[1] = (latent_ref[1].astype(jnp.float32) + second).astype(jnp.bfloat16)


def routes(count):
    own, hop1, swap1, hop2, swap2 = [], [], [], [], []
    for s in range(count):
        r, first, last = s % 4, s < 4, s + 4 >= count
        if r == 0:
            own.append((s, s + 1))
            hop1.append((s, s + 2))
            if not last:
                hop2.append((s, s + 4))
            if not first:
                swap2.append((s, s + 1))
        elif r == 1:
            if not last:
                hop1.append((s, s + 4))
            hop2.append((s, s + 2))
            if not first:
                swap1.append((s, s - 1))
                swap2.append((s, s - 1))
        elif r == 2:
            own.append((s, s + 1))
            if not last:
                hop1.append((s, s - 2))
            swap1.append((s, s + 1))
        else:
            if not last:
                hop1.append((s, s + 4))
            if not first:
                swap1.append((s, s - 1))
                hop2.append((s, s - 2))
            swap2.append((s, s - 1))
    return own, hop1, swap1, hop2, swap2


def shards(queries, keys, values, lookback, proj_weight, features, norm_gain, conv_weight):
    count = lax.axis_size("span")
    me = lax.axis_index("span")
    second = lax.rem(me, 4) == 1
    second, keys, values = lax.optimization_barrier((second, keys, values))
    own, hop1, swap1, hop2, swap2 = routes(count)
    move = functools.partial(lax.ppermute, axis_name="span")

    rows, width = queries.shape
    heads = width // HEAD_DIM
    frames, channels, pixels = features.shape

    block = jax.ShapeDtypeStruct((rows, width), jnp.float32)
    picture = jax.ShapeDtypeStruct(features.shape, jnp.bfloat16)

    k_r1 = move(keys, perm=hop1)
    k_s0 = move(keys, perm=own)
    v_r1 = move(values, perm=hop1)
    v_s0 = move(values, perm=own)

    tokens = frames * pixels // (PATCH * PATCH)
    place_matrix, shift_matrix = pl.pallas_call(
        one_hot_kernel,
        out_shape=(
            jax.ShapeDtypeStruct((PATCH * PATCH * tokens, frames * pixels), jnp.bfloat16),
            jax.ShapeDtypeStruct((pixels, TAPS * pixels), jnp.bfloat16),
        ),
        out_specs=(VMEM, VMEM),
        compiler_params=params(),
        name="one_hot",
    )()
    k_r1, place_matrix, shift_matrix = lax.optimization_barrier(
        (k_r1, place_matrix, shift_matrix)
    )

    k_r2 = move(jnp.where(second, keys, k_r1), perm=hop2)
    k_s1 = move(k_r1, perm=swap1)
    v_hop = jnp.where(second, values, v_r1)
    v_r2 = move(v_hop, perm=hop2)
    v_s1 = move(v_r1, perm=swap1)

    mixed, top, total = pl.pallas_call(
        early_kernel,
        out_shape=(block,) * 3,
        in_specs=[SMEM] + [VMEM] * 9,
        out_specs=(VMEM,) * 3,
        compiler_params=params(),
        name="early",
        cost_estimate=pl.CostEstimate(
            flops=12 * rows * rows * width,
            bytes_accessed=9 * rows * width * 2,
            transcendentals=3 * heads * rows * rows,
        ),
    )(
        lookback, queries, keys, k_r1, k_s0, k_s1, values, v_r1, v_s0, v_s1,
    )

    k_s2 = move(k_r2, perm=swap2)
    weights, base, inverse = pl.pallas_call(
        late_kernel,
        out_shape=(
            jax.ShapeDtypeStruct((heads, rows, 2 * rows), jnp.bfloat16), block, block,
        ),
        in_specs=[SMEM] + [VMEM] * 6,
        out_specs=(VMEM,) * 3,
        compiler_params=params(),
        name="late",
        cost_estimate=pl.CostEstimate(
            flops=4 * rows * rows * width,
            bytes_accessed=9 * rows * width * 2,
            transcendentals=2 * heads * rows * rows,
        ),
    )(lookback, queries, k_r2, k_s2, mixed, top, total)

    v_s2 = move(v_r2, perm=swap2)
    patch_width = proj_weight.shape[1]
    attended, latent, activated = pl.pallas_call(
        latent_kernel,
        out_shape=(jax.ShapeDtypeStruct((rows, width), jnp.bfloat16), picture, picture),
        in_specs=[VMEM] * 9,
        out_specs=(pl.BlockSpec(memory_space=pl.ANY), VMEM, VMEM),
        scratch_shapes=[
            pltpu.VMEM((rows, width), jnp.bfloat16),
            pltpu.VMEM((patch_width, rows), jnp.float32),
            pltpu.SemaphoreType.DMA,
        ],
        compiler_params=params(),
        name="latent",
        cost_estimate=pl.CostEstimate(
            flops=2 * rows * width * (2 * rows + patch_width),
            bytes_accessed=10 * rows * width * 2 + width * patch_width * 2,
            transcendentals=features.size,
        ),
    )(
        weights, base, inverse, v_r2, v_s2, proj_weight, place_matrix, features,
        norm_gain.reshape(1, channels),
    )

    halo = move(activated, perm=[(s, s + 1) for s in range(count - 1)])

    moved = [pltpu.VMEM((TAPS * channels, pixels), jnp.bfloat16)] * 2
    conv_cost = pl.CostEstimate(
        flops=2 * channels * TAPS * channels * pixels * 3,
        bytes_accessed=conv_weight.size * 2 + shift_matrix.size * 2,
        transcendentals=0,
    )
    part = pl.pallas_call(
        conv_own_kernel,
        out_shape=jax.ShapeDtypeStruct(features.shape, jnp.float32),
        in_specs=[VMEM] * 3,
        out_specs=VMEM,
        scratch_shapes=moved,
        compiler_params=params(),
        name="conv_own",
        cost_estimate=conv_cost,
    )(activated, shift_matrix, conv_weight)
    decoded = pl.pallas_call(
        conv_halo_kernel,
        out_shape=jax.ShapeDtypeStruct(features.shape, jnp.bfloat16),
        in_specs=[VMEM] * 5,
        out_specs=VMEM,
        scratch_shapes=moved,
        compiler_params=params(),
        name="conv_halo",
        cost_estimate=conv_cost,
    )(halo, shift_matrix, conv_weight, part, latent)
    return (attended, decoded)


def solution(mesh):
    placed = (
        P(("groups", "span"), None),
        P(("groups", "span"), None),
        P(("groups", "span"), None),
        P(("groups", "span")),
        P(),
        P(("groups", "span"), None, None),
        P(),
        P(),
    )
    return jax.shard_map(
        shards,
        mesh=mesh,
        in_specs=placed,
        out_specs=(P(("groups", "span"), None), P(("groups", "span"), None, None)),
        check_vma=False,
    )
```

```python
import functools

import jax
import jax.numpy as jnp
import numpy as np
from jax import lax
from jax.experimental import pallas as pl
from jax.experimental.pallas import tpu as pltpu
from jax.sharding import PartitionSpec as P

HEAD_DIM = 128
LOOKBACK = 3
SIDE = 16
PATCH = 2
TAPS = 9
EPS = 1e-06

VMEM = pl.BlockSpec(memory_space=pltpu.VMEM)
SMEM = pl.BlockSpec(memory_space=pltpu.SMEM)


def params():
    return pltpu.CompilerParams(vmem_limit_bytes=16 * 1024 * 1024)


def one_hot_kernel(place_ref, shift_ref):
    half = SIDE // PATCH
    patches = half * half
    pixels = SIDE * SIDE
    tokens = place_ref.shape[0] // (PATCH * PATCH)
    column = lax.broadcasted_iota(jnp.int32, (tokens, place_ref.shape[1]), 1)
    pixel = column % pixels
    row, col = pixel // SIDE, pixel % SIDE
    token = column // pixels * patches + row // PATCH * half + col // PATCH
    corner = row % PATCH * PATCH + col % PATCH
    hit = lax.broadcasted_iota(jnp.int32, token.shape, 0) == token
    for k in range(PATCH * PATCH):
        place_ref[pl.ds(k * tokens, tokens), :] = jnp.where(
            hit & (corner == k), 1.0, 0.0
        ).astype(jnp.bfloat16)
    source = lax.broadcasted_iota(jnp.int32, (pixels, pixels), 0)
    target = lax.broadcasted_iota(jnp.int32, (pixels, pixels), 1)
    for b in range(3):
        for e in range(3):
            r, c = target // SIDE + b - 1, target % SIDE + e - 1
            inside = (r >= 0) & (r < SIDE) & (c >= 0) & (c < SIDE)
            tap = 3 * b + e
            shift_ref[:, tap * pixels : (tap + 1) * pixels] = jnp.where(
                inside & (source == r * SIDE + c), 1.0, 0.0
            ).astype(jnp.bfloat16)


UNSEEN = LOOKBACK + 1
DISTANCES = ((0, UNSEEN, 3, 2, 1), (0, 1, UNSEEN, 2, 3), (0, 2, 3, UNSEEN, 1), (0, 1, 3, 2, UNSEEN))
RATE = float(np.log2(np.e) * HEAD_DIM**-0.5)


def biases(lookback):
    place = lax.rem(lax.axis_index("span"), 4)
    out = []
    for ways in zip(*DISTANCES):
        distance = ways[0]
        for k, way in enumerate(ways[1:], 1):
            distance = jnp.where(place == k, way, distance)
        out.append(jnp.where(distance <= lookback[0], 0.0, -jnp.inf).astype(jnp.float32))
    return out


def head(h):
    return slice(h * HEAD_DIM, (h + 1) * HEAD_DIM)


def staged(heads, *stages):
    held = {}
    for step in range(heads + len(stages) - 1):
        for i, stage in enumerate(stages):
            h = step - i
            if 0 <= h < heads:
                held[h] = stage(h, held.get(h))


def scores_of(q_ref, blocks, biases, h):
    keys = jnp.concatenate(blocks, axis=0)
    s = lax.dot_general(
        q_ref[:, head(h)], keys, (((1,), (1,)), ((), ())), preferred_element_type=jnp.float32
    )
    rows = blocks[0].shape[0]
    parts = [s[:, i * rows : (i + 1) * rows] for i in range(len(blocks))]
    return [part if bias is None else part + bias for part, bias in zip(parts, biases)]


def top_of(parts):
    return jnp.max(functools.reduce(jnp.maximum, parts), axis=1, keepdims=True)


def early_kernel(
    lookback, q_ref, k0, k_hop, k_own, k2, v0, v_hop, v_own, v2, mixed_ref, top_ref, total_ref
):
    rows = q_ref.shape[0]
    bias = biases(lookback)
    hopped = lax.rem(lax.axis_index("span"), 2) == 0
    ones = jnp.ones((3 * rows, HEAD_DIM), jnp.bfloat16)

    def score(h, _):
        k1 = jnp.where(hopped, k_hop[:, head(h)], k_own[:, head(h)])
        keys = (k0[:, head(h)], k1, k2[:, head(h)])
        return scores_of(q_ref, keys, (None, bias[1], bias[2]), h)

    def soften(h, parts):
        top = top_of(parts)
        top_ref[:, head(h)] = jnp.broadcast_to(top, (rows, HEAD_DIM))
        probs = [jnp.exp2((part - top) * RATE).astype(jnp.bfloat16) for part in parts]
        return jnp.concatenate(probs, axis=1)

    def blend(h, probs):
        v1 = jnp.where(hopped, v_hop[:, head(h)], v_own[:, head(h)])
        values = jnp.concatenate([v0[:, head(h)], v1, v2[:, head(h)]], axis=0)
        both = jnp.dot(
            probs, jnp.concatenate([values, ones], axis=1), preferred_element_type=jnp.float32
        )
        mixed_ref[:, head(h)] = both[:, :HEAD_DIM]
        total_ref[:, head(h)] = both[:, HEAD_DIM:]

    staged(q_ref.shape[1] // HEAD_DIM, score, soften, blend)


def late_kernel(
    lookback, q_ref, k1, k2, mixed_ref, top_ref, total_ref, p_ref, base_ref, inverse_ref
):
    rows = q_ref.shape[0]
    ones = jnp.ones((2 * rows, HEAD_DIM), jnp.bfloat16)
    bias = biases(lookback)

    def score(h, _):
        return scores_of(q_ref, (k1[:, head(h)], k2[:, head(h)]), (bias[3], bias[4]), h)

    def soften(h, parts):
        before = top_ref[:, head(h)]
        top = jnp.maximum(before, top_of(parts))
        probs = [jnp.exp2((part - top) * RATE).astype(jnp.bfloat16) for part in parts]
        probs = jnp.concatenate(probs, axis=1)
        p_ref[h] = probs
        return probs, jnp.exp2((before - top) * RATE)

    def settle(h, held):
        probs, shrink = held
        total = jnp.dot(probs, ones, preferred_element_type=jnp.float32)
        inverse = 1.0 / (total + total_ref[:, head(h)] * shrink)
        inverse_ref[:, head(h)] = inverse
        base_ref[:, head(h)] = mixed_ref[:, head(h)] * (shrink * inverse)

    staged(q_ref.shape[1] // HEAD_DIM, score, soften, settle)


def latent_kernel(
    p_ref, base_ref, inverse_ref, v1, v2, w_ref, place_ref, features_ref, gain_ref,
    out_ref, latent_ref, act_ref, mine, turned, sem,
):
    frames, channels, pixels = features_ref.shape

    def blend(h, _):
        values = jnp.concatenate([v1[:, head(h)], v2[:, head(h)]], axis=0)
        return jnp.dot(p_ref[h], values, preferred_element_type=jnp.float32)

    def settle(h, late):
        late = base_ref[:, head(h)] + late * inverse_ref[:, head(h)]
        mine[:, head(h)] = late.astype(jnp.bfloat16)

    staged(mine.shape[1] // HEAD_DIM, blend, settle)
    copy = pltpu.make_async_copy(mine, out_ref, sem)
    copy.start()
    projected = jnp.dot(mine[...], w_ref[...], preferred_element_type=jnp.float32)
    turned[...] = projected.T
    parts = [turned[pl.ds(k, channels, stride=4), :] for k in range(4)]
    mixed = jnp.concatenate(parts, axis=1)
    high = mixed.astype(jnp.bfloat16)
    low = (mixed - high.astype(jnp.float32)).astype(jnp.bfloat16)
    placed = jnp.dot(
        jnp.concatenate([high, low], axis=0), place_ref[...], preferred_element_type=jnp.float32
    )
    placed = placed[:channels] + placed[channels:]
    gain = jnp.broadcast_to(gain_ref[...], (8, channels)).T[:, :1]
    for f in range(frames):
        latent = features_ref[f].astype(jnp.float32) + placed[:, f * pixels : (f + 1) * pixels]
        latent = latent.astype(jnp.bfloat16)
        latent_ref[f] = latent
        data = latent.astype(jnp.float32)
        mean_square = jnp.mean(data * data, axis=0, keepdims=True)
        normed = data * lax.rsqrt(mean_square + EPS) * gain
        act_ref[f] = (normed / (1.0 + jnp.exp(-normed))).astype(jnp.bfloat16)
    copy.wait()


def spread(frames_ref, shift_ref, moved):
    frames, channels, pixels = frames_ref.shape
    stacked = frames_ref[...].reshape(frames * channels, pixels)
    for tap in range(TAPS):
        shifted = jnp.dot(
            stacked, shift_ref[:, tap * pixels : (tap + 1) * pixels],
            preferred_element_type=jnp.float32,
        ).astype(jnp.bfloat16)
        for f in range(frames):
            moved[f, pl.ds(tap * channels, channels), :] = shifted[
                f * channels : (f + 1) * channels
            ]


def tap_dots(w_ref, lags, moved):
    channels = w_ref.shape[2]
    total = 0.0
    for tap in range(TAPS):
        weights = jnp.concatenate([w_ref[lag * TAPS + tap] for lag in lags], axis=0)
        total += jnp.dot(
            weights, moved[pl.ds(tap * channels, channels), :],
            preferred_element_type=jnp.float32,
        )
    return [total[i * channels : (i + 1) * channels] for i in range(len(lags))]


def conv_own_kernel(act_ref, shift_ref, w_ref, part_ref, moved):
    spread(act_ref, shift_ref, moved)
    part_ref[0], second = tap_dots(w_ref, (2, 1), moved.at[0])
    part_ref[1] = second + tap_dots(w_ref, (2,), moved.at[1])[0]


def conv_halo_kernel(halo_ref, shift_ref, w_ref, part_ref, latent_ref, out_ref, moved):
    spread(halo_ref, shift_ref, moved)
    first, second = tap_dots(w_ref, (1, 0), moved.at[1])
    second += part_ref[1] + latent_ref[1].astype(jnp.float32)
    out_ref[1] = second.astype(jnp.bfloat16)
    first += part_ref[0] + tap_dots(w_ref, (0,), moved.at[0])[0]
    out_ref[0] = (latent_ref[0].astype(jnp.float32) + first).astype(jnp.bfloat16)


def routes(count):
    own, hop1, swap1, hop2, swap2 = [], [], [], [], []
    for s in range(count):
        r, first, last = s % 4, s < 4, s + 4 >= count
        if r == 0:
            own.append((s, s + 1))
            hop1.append((s, s + 2))
            if not last:
                hop2.append((s, s + 4))
            if not first:
                swap2.append((s, s + 1))
        elif r == 1:
            if not last:
                hop1.append((s, s + 4))
            hop2.append((s, s + 2))
            if not first:
                swap1.append((s, s - 1))
                swap2.append((s, s - 1))
        elif r == 2:
            own.append((s, s + 1))
            if not last:
                hop1.append((s, s - 2))
            swap1.append((s, s + 1))
        else:
            if not last:
                hop1.append((s, s + 4))
            if not first:
                swap1.append((s, s - 1))
                hop2.append((s, s - 2))
            swap2.append((s, s - 1))
    return own, hop1, swap1, hop2, swap2


def shards(queries, keys, values, lookback, proj_weight, features, norm_gain, conv_weight):
    count = lax.axis_size("span")
    me = lax.axis_index("span")
    second = lax.rem(me, 4) == 1
    second, keys, values = lax.optimization_barrier((second, keys, values))
    own, hop1, swap1, hop2, swap2 = routes(count)
    move = functools.partial(lax.ppermute, axis_name="span")

    rows, width = queries.shape
    heads = width // HEAD_DIM
    frames, channels, pixels = features.shape

    block = jax.ShapeDtypeStruct((rows, width), jnp.float32)
    picture = jax.ShapeDtypeStruct(features.shape, jnp.bfloat16)

    k_r1 = move(keys, perm=hop1)
    k_s0 = move(keys, perm=own)
    v_r1 = move(values, perm=hop1)
    v_s0 = move(values, perm=own)

    tokens = frames * pixels // (PATCH * PATCH)
    place_matrix, shift_matrix = pl.pallas_call(
        one_hot_kernel,
        out_shape=(
            jax.ShapeDtypeStruct((PATCH * PATCH * tokens, frames * pixels), jnp.bfloat16),
            jax.ShapeDtypeStruct((pixels, TAPS * pixels), jnp.bfloat16),
        ),
        out_specs=(VMEM, VMEM),
        compiler_params=params(),
        name="one_hot",
    )()
    k_r1, place_matrix, shift_matrix = lax.optimization_barrier(
        (k_r1, place_matrix, shift_matrix)
    )

    k_r2 = move(jnp.where(second, keys, k_r1), perm=hop2)
    k_s1 = move(k_r1, perm=swap1)
    v_hop = jnp.where(second, values, v_r1)
    v_r2 = move(v_hop, perm=hop2)
    v_s1 = move(v_r1, perm=swap1)

    mixed, top, total = pl.pallas_call(
        early_kernel,
        out_shape=(block,) * 3,
        in_specs=[SMEM] + [VMEM] * 9,
        out_specs=(VMEM,) * 3,
        compiler_params=params(),
        name="early",
        cost_estimate=pl.CostEstimate(
            flops=12 * rows * rows * width,
            bytes_accessed=9 * rows * width * 2,
            transcendentals=3 * heads * rows * rows,
        ),
    )(
        lookback, queries, keys, k_r1, k_s0, k_s1, values, v_r1, v_s0, v_s1,
    )

    k_s2 = move(k_r2, perm=swap2)
    weights, base, inverse = pl.pallas_call(
        late_kernel,
        out_shape=(
            jax.ShapeDtypeStruct((heads, rows, 2 * rows), jnp.bfloat16), block, block,
        ),
        in_specs=[SMEM] + [VMEM] * 6,
        out_specs=(VMEM,) * 3,
        compiler_params=params(),
        name="late",
        cost_estimate=pl.CostEstimate(
            flops=4 * rows * rows * width,
            bytes_accessed=9 * rows * width * 2,
            transcendentals=2 * heads * rows * rows,
        ),
    )(lookback, queries, k_r2, k_s2, mixed, top, total)

    v_r2, _ = lax.optimization_barrier((v_r2, mixed))
    v_s2 = move(v_r2, perm=swap2)
    patch_width = proj_weight.shape[1]
    attended, latent, activated = pl.pallas_call(
        latent_kernel,
        out_shape=(jax.ShapeDtypeStruct((rows, width), jnp.bfloat16), picture, picture),
        in_specs=[VMEM] * 9,
        out_specs=(pl.BlockSpec(memory_space=pl.ANY), VMEM, VMEM),
        scratch_shapes=[
            pltpu.VMEM((rows, width), jnp.bfloat16),
            pltpu.VMEM((patch_width, rows), jnp.float32),
            pltpu.SemaphoreType.DMA,
        ],
        compiler_params=params(),
        name="latent",
        cost_estimate=pl.CostEstimate(
            flops=2 * rows * width * (2 * rows + patch_width),
            bytes_accessed=10 * rows * width * 2 + width * patch_width * 2,
            transcendentals=features.size,
        ),
    )(
        weights, base, inverse, v_r2, v_s2, proj_weight, place_matrix, features,
        norm_gain.reshape(1, channels),
    )

    halo = move(activated, perm=[(s, s + 1) for s in range(count - 1)])

    moved = [pltpu.VMEM((frames, TAPS * channels, pixels), jnp.bfloat16)]
    conv_cost = pl.CostEstimate(
        flops=2 * channels * TAPS * channels * pixels * 3,
        bytes_accessed=conv_weight.size * 2 + shift_matrix.size * 2,
        transcendentals=0,
    )
    part = pl.pallas_call(
        conv_own_kernel,
        out_shape=jax.ShapeDtypeStruct(features.shape, jnp.float32),
        in_specs=[VMEM] * 3,
        out_specs=VMEM,
        scratch_shapes=moved,
        compiler_params=params(),
        name="conv_own",
        cost_estimate=conv_cost,
    )(activated, shift_matrix, conv_weight)
    decoded = pl.pallas_call(
        conv_halo_kernel,
        out_shape=jax.ShapeDtypeStruct(features.shape, jnp.bfloat16),
        in_specs=[VMEM] * 5,
        out_specs=VMEM,
        scratch_shapes=moved,
        compiler_params=params(),
        name="conv_halo",
        cost_estimate=conv_cost,
    )(halo, shift_matrix, conv_weight, part, latent)
    return (attended, decoded)


def solution(mesh):
    placed = (
        P(("groups", "span"), None),
        P(("groups", "span"), None),
        P(("groups", "span"), None),
        P(("groups", "span")),
        P(),
        P(("groups", "span"), None, None),
        P(),
        P(),
    )
    return jax.shard_map(
        shards,
        mesh=mesh,
        in_specs=placed,
        out_specs=(P(("groups", "span"), None), P(("groups", "span"), None, None)),
        check_vma=False,
    )
```

```python
import functools

import jax
import jax.numpy as jnp
import numpy as np
from jax import lax
from jax.experimental import pallas as pl
from jax.experimental.pallas import tpu as pltpu
from jax.sharding import PartitionSpec as P

HEAD_DIM = 128
LOOKBACK = 3
SIDE = 16
PATCH = 2
TAPS = 9
EPS = 1e-06

VMEM = pl.BlockSpec(memory_space=pltpu.VMEM)
SMEM = pl.BlockSpec(memory_space=pltpu.SMEM)


def params():
    return pltpu.CompilerParams(vmem_limit_bytes=16 * 1024 * 1024)


def one_hot_kernel(place_ref, shift_ref):
    half = SIDE // PATCH
    patches = half * half
    pixels = SIDE * SIDE
    tokens = place_ref.shape[0] // (PATCH * PATCH)
    column = lax.broadcasted_iota(jnp.int32, (tokens, place_ref.shape[1]), 1)
    pixel = column % pixels
    row, col = pixel // SIDE, pixel % SIDE
    token = column // pixels * patches + row // PATCH * half + col // PATCH
    corner = row % PATCH * PATCH + col % PATCH
    hit = lax.broadcasted_iota(jnp.int32, token.shape, 0) == token
    for k in range(PATCH * PATCH):
        place_ref[pl.ds(k * tokens, tokens), :] = jnp.where(
            hit & (corner == k), 1.0, 0.0
        ).astype(jnp.bfloat16)
    source = lax.broadcasted_iota(jnp.int32, (pixels, pixels), 0)
    target = lax.broadcasted_iota(jnp.int32, (pixels, pixels), 1)
    for b in range(3):
        for e in range(3):
            r, c = target // SIDE + b - 1, target % SIDE + e - 1
            inside = (r >= 0) & (r < SIDE) & (c >= 0) & (c < SIDE)
            tap = 3 * b + e
            shift_ref[:, tap * pixels : (tap + 1) * pixels] = jnp.where(
                inside & (source == r * SIDE + c), 1.0, 0.0
            ).astype(jnp.bfloat16)


UNSEEN = LOOKBACK + 1
DISTANCES = ((0, UNSEEN, 3, 2, 1), (0, 1, UNSEEN, 2, 3), (0, 2, 3, UNSEEN, 1), (0, 1, 3, 2, UNSEEN))
RATE = float(np.log2(np.e) * HEAD_DIM**-0.5)


def biases(lookback):
    place = lax.rem(lax.axis_index("span"), 4)
    out = []
    for ways in zip(*DISTANCES):
        distance = ways[0]
        for k, way in enumerate(ways[1:], 1):
            distance = jnp.where(place == k, way, distance)
        out.append(jnp.where(distance <= lookback[0], 0.0, -jnp.inf).astype(jnp.float32))
    return out


def head(h):
    return slice(h * HEAD_DIM, (h + 1) * HEAD_DIM)


def staged(heads, *stages):
    held = {}
    for step in range(heads + len(stages) - 1):
        for i, stage in enumerate(stages):
            h = step - i
            if 0 <= h < heads:
                held[h] = stage(h, held.get(h))


def scores_of(q_ref, blocks, biases, h):
    keys = jnp.concatenate(blocks, axis=0)
    s = lax.dot_general(
        q_ref[:, head(h)], keys, (((1,), (1,)), ((), ())), preferred_element_type=jnp.float32
    )
    rows = blocks[0].shape[0]
    parts = [s[:, i * rows : (i + 1) * rows] for i in range(len(blocks))]
    return [part if bias is None else part + bias for part, bias in zip(parts, biases)]


def top_of(parts):
    return jnp.max(functools.reduce(jnp.maximum, parts), axis=1, keepdims=True)


def early_kernel(
    lookback, q_ref, k0, k_hop, k_own, k2, v0, v_hop, v_own, v2, _, mixed_ref, top_ref, total_ref
):
    rows = q_ref.shape[0]
    bias = biases(lookback)
    hopped = lax.rem(lax.axis_index("span"), 2) == 0
    ones = jnp.ones((3 * rows, HEAD_DIM), jnp.bfloat16)

    def score(h, _):
        k1 = jnp.where(hopped, k_hop[:, head(h)], k_own[:, head(h)])
        keys = (k0[:, head(h)], k1, k2[:, head(h)])
        return scores_of(q_ref, keys, (None, bias[1], bias[2]), h)

    def soften(h, parts):
        top = top_of(parts)
        top_ref[:, head(h)] = jnp.broadcast_to(top, (rows, HEAD_DIM))
        probs = [jnp.exp2((part - top) * RATE).astype(jnp.bfloat16) for part in parts]
        return jnp.concatenate(probs, axis=1)

    def blend(h, probs):
        v1 = jnp.where(hopped, v_hop[:, head(h)], v_own[:, head(h)])
        values = jnp.concatenate([v0[:, head(h)], v1, v2[:, head(h)]], axis=0)
        both = jnp.dot(
            probs, jnp.concatenate([values, ones], axis=1), preferred_element_type=jnp.float32
        )
        mixed_ref[:, head(h)] = both[:, :HEAD_DIM]
        total_ref[:, head(h)] = both[:, HEAD_DIM:]

    staged(q_ref.shape[1] // HEAD_DIM, score, soften, blend)


def late_kernel(
    lookback, q_ref, k1, k2, mixed_ref, top_ref, total_ref, p_ref, base_ref, inverse_ref
):
    rows = q_ref.shape[0]
    ones = jnp.ones((2 * rows, HEAD_DIM), jnp.bfloat16)
    bias = biases(lookback)

    def score(h, _):
        return scores_of(q_ref, (k1[:, head(h)], k2[:, head(h)]), (bias[3], bias[4]), h)

    def soften(h, parts):
        before = top_ref[:, head(h)]
        top = jnp.maximum(before, top_of(parts))
        probs = [jnp.exp2((part - top) * RATE).astype(jnp.bfloat16) for part in parts]
        probs = jnp.concatenate(probs, axis=1)
        p_ref[h] = probs
        return probs, jnp.exp2((before - top) * RATE)

    def settle(h, held):
        probs, shrink = held
        total = jnp.dot(probs, ones, preferred_element_type=jnp.float32)
        inverse = 1.0 / (total + total_ref[:, head(h)] * shrink)
        inverse_ref[:, head(h)] = inverse
        base_ref[:, head(h)] = mixed_ref[:, head(h)] * (shrink * inverse)

    staged(q_ref.shape[1] // HEAD_DIM, score, soften, settle)


def latent_kernel(
    p_ref, base_ref, inverse_ref, v1, v2, w_ref, place_ref, features_ref, gain_ref,
    out_ref, latent_ref, act_ref, mine, turned, sem,
):
    frames, channels, pixels = features_ref.shape

    heads = mine.shape[1] // HEAD_DIM
    group = 4

    def blend(g, _):
        late = []
        for h in range(g * group, (g + 1) * group):
            values = jnp.concatenate([v1[:, head(h)], v2[:, head(h)]], axis=0)
            late.append(jnp.dot(p_ref[h], values, preferred_element_type=jnp.float32))
        return late

    def settle(g, late):
        for h, part in zip(range(g * group, (g + 1) * group), late):
            part = base_ref[:, head(h)] + part * inverse_ref[:, head(h)]
            mine[:, head(h)] = part.astype(jnp.bfloat16)

    def project(g, _):
        cols = slice(g * group * HEAD_DIM, (g + 1) * group * HEAD_DIM)
        part = jnp.dot(mine[:, cols], w_ref[cols, :], preferred_element_type=jnp.float32)
        products.append(part if not products else products.pop() + part)

    products = []
    staged(heads // group, blend, settle, project)
    copy = pltpu.make_async_copy(mine, out_ref, sem)
    copy.start()
    projected = products[0]
    turned[...] = projected.T
    parts = [turned[pl.ds(k, channels, stride=4), :] for k in range(4)]
    mixed = jnp.concatenate(parts, axis=1)
    high = mixed.astype(jnp.bfloat16)
    low = (mixed - high.astype(jnp.float32)).astype(jnp.bfloat16)
    placed = jnp.dot(high, place_ref[...], preferred_element_type=jnp.float32)
    placed += jnp.dot(low, place_ref[...], preferred_element_type=jnp.float32)
    gain = jnp.broadcast_to(gain_ref[...], (8, channels)).T[:, :1]
    for f in range(frames):
        latent = features_ref[f].astype(jnp.float32) + placed[:, f * pixels : (f + 1) * pixels]
        latent = latent.astype(jnp.bfloat16)
        latent_ref[f] = latent
        data = latent.astype(jnp.float32)
        mean_square = jnp.mean(data * data, axis=0, keepdims=True)
        normed = data * lax.rsqrt(mean_square + EPS) * gain
        act_ref[f] = (normed / (1.0 + jnp.exp(-normed))).astype(jnp.bfloat16)
    copy.wait()


def spread(act, shift_ref, moved):
    channels, pixels = act.shape
    for tap in range(TAPS):
        moved[pl.ds(tap * channels, channels), :] = jnp.dot(
            act, shift_ref[:, tap * pixels : (tap + 1) * pixels],
            preferred_element_type=jnp.float32,
        ).astype(jnp.bfloat16)


def tap_dot(w_ref, lag, moved):
    channels = w_ref.shape[2]
    return sum(
        jnp.dot(
            w_ref[lag * TAPS + tap], moved[pl.ds(tap * channels, channels), :],
            preferred_element_type=jnp.float32,
        )
        for tap in range(TAPS)
    )


def conv_own_kernel(act_ref, shift_ref, w_ref, part_ref, moved0, moved1):
    spread(act_ref[0], shift_ref, moved0)
    spread(act_ref[1], shift_ref, moved1)
    part_ref[0] = tap_dot(w_ref, 2, moved0)
    part_ref[1] = tap_dot(w_ref, 1, moved0) + tap_dot(w_ref, 2, moved1)


def conv_halo_kernel(
    halo_ref, shift_ref, w_ref, part_ref, latent_ref, out_ref, moved0, moved1, done, sems
):
    copies = [pltpu.make_async_copy(done.at[f], out_ref.at[f], sems.at[f]) for f in range(2)]
    spread(halo_ref[1], shift_ref, moved1)
    second = part_ref[1] + tap_dot(w_ref, 0, moved1)
    done[1] = (latent_ref[1].astype(jnp.float32) + second).astype(jnp.bfloat16)
    copies[1].start()
    spread(halo_ref[0], shift_ref, moved0)
    first = part_ref[0] + tap_dot(w_ref, 0, moved0) + tap_dot(w_ref, 1, moved1)
    done[0] = (latent_ref[0].astype(jnp.float32) + first).astype(jnp.bfloat16)
    copies[0].start()
    for copy in copies:
        copy.wait()


def routes(count):
    own, hop1, swap1, hop2, swap2 = [], [], [], [], []
    for s in range(count):
        r, first, last = s % 4, s < 4, s + 4 >= count
        if r == 0:
            own.append((s, s + 1))
            hop1.append((s, s + 2))
            if not last:
                hop2.append((s, s + 4))
            if not first:
                swap2.append((s, s + 1))
        elif r == 1:
            if not last:
                hop1.append((s, s + 4))
            hop2.append((s, s + 2))
            if not first:
                swap1.append((s, s - 1))
                swap2.append((s, s - 1))
        elif r == 2:
            own.append((s, s + 1))
            if not last:
                hop1.append((s, s - 2))
            swap1.append((s, s + 1))
        else:
            if not last:
                hop1.append((s, s + 4))
            if not first:
                swap1.append((s, s - 1))
                hop2.append((s, s - 2))
            swap2.append((s, s - 1))
    return own, hop1, swap1, hop2, swap2


def shards(queries, keys, values, lookback, proj_weight, features, norm_gain, conv_weight):
    count = lax.axis_size("span")
    me = lax.axis_index("span")
    second = lax.rem(me, 4) == 1
    second, keys, values = lax.optimization_barrier((second, keys, values))
    own, hop1, swap1, hop2, swap2 = routes(count)
    move = functools.partial(lax.ppermute, axis_name="span")

    rows, width = queries.shape
    heads = width // HEAD_DIM
    frames, channels, pixels = features.shape

    block = jax.ShapeDtypeStruct((rows, width), jnp.float32)
    picture = jax.ShapeDtypeStruct(features.shape, jnp.bfloat16)

    k_r1 = move(keys, perm=hop1)
    k_s0 = move(keys, perm=own)
    v_r1 = move(values, perm=hop1)
    v_s0 = move(values, perm=own)

    tokens = frames * pixels // (PATCH * PATCH)
    place_matrix, shift_matrix = pl.pallas_call(
        one_hot_kernel,
        out_shape=(
            jax.ShapeDtypeStruct((PATCH * PATCH * tokens, frames * pixels), jnp.bfloat16),
            jax.ShapeDtypeStruct((pixels, TAPS * pixels), jnp.bfloat16),
        ),
        out_specs=(VMEM, VMEM),
        compiler_params=params(),
        name="one_hot",
    )()
    k_r1, place_matrix, shift_matrix = lax.optimization_barrier(
        (k_r1, place_matrix, shift_matrix)
    )

    k_r2 = move(jnp.where(second, keys, k_r1), perm=hop2)
    k_s1 = move(k_r1, perm=swap1)
    v_hop = jnp.where(second, values, v_r1)
    v_r2 = move(v_hop, perm=hop2)
    v_s1 = move(v_r1, perm=swap1)

    mixed, top, total = pl.pallas_call(
        early_kernel,
        out_shape=(block,) * 3,
        in_specs=[SMEM] + [VMEM] * 10,
        out_specs=(VMEM,) * 3,
        compiler_params=params(),
        name="early",
        cost_estimate=pl.CostEstimate(
            flops=12 * rows * rows * width,
            bytes_accessed=9 * rows * width * 2,
            transcendentals=3 * heads * rows * rows,
        ),
    )(
        lookback, queries, keys, k_r1, k_s0, k_s1, values, v_r1, v_s0, v_s1, proj_weight,
    )

    k_s2 = move(k_r2, perm=swap2)
    weights, base, inverse = pl.pallas_call(
        late_kernel,
        out_shape=(
            jax.ShapeDtypeStruct((heads, rows, 2 * rows), jnp.bfloat16), block, block,
        ),
        in_specs=[SMEM] + [VMEM] * 6,
        out_specs=(VMEM,) * 3,
        compiler_params=params(),
        name="late",
        cost_estimate=pl.CostEstimate(
            flops=4 * rows * rows * width,
            bytes_accessed=9 * rows * width * 2,
            transcendentals=2 * heads * rows * rows,
        ),
    )(lookback, queries, k_r2, k_s2, mixed, top, total)

    v_r2, _ = lax.optimization_barrier((v_r2, mixed))
    v_s2 = move(v_r2, perm=swap2)
    patch_width = proj_weight.shape[1]
    attended, latent, activated = pl.pallas_call(
        latent_kernel,
        out_shape=(jax.ShapeDtypeStruct((rows, width), jnp.bfloat16), picture, picture),
        in_specs=[VMEM] * 9,
        out_specs=(pl.BlockSpec(memory_space=pl.ANY), VMEM, VMEM),
        scratch_shapes=[
            pltpu.VMEM((rows, width), jnp.bfloat16),
            pltpu.VMEM((patch_width, rows), jnp.float32),
            pltpu.SemaphoreType.DMA,
        ],
        compiler_params=params(),
        name="latent",
        cost_estimate=pl.CostEstimate(
            flops=2 * rows * width * (2 * rows + patch_width),
            bytes_accessed=10 * rows * width * 2 + width * patch_width * 2,
            transcendentals=features.size,
        ),
    )(
        weights, base, inverse, v_r2, v_s2, proj_weight, place_matrix, features,
        norm_gain.reshape(1, channels),
    )

    halo = move(activated, perm=[(s, s + 1) for s in range(count - 1)])

    moved = [pltpu.VMEM((TAPS * channels, pixels), jnp.bfloat16)] * 2
    conv_cost = pl.CostEstimate(
        flops=2 * channels * TAPS * channels * pixels * 3,
        bytes_accessed=conv_weight.size * 2 + shift_matrix.size * 2,
        transcendentals=0,
    )
    part = pl.pallas_call(
        conv_own_kernel,
        out_shape=jax.ShapeDtypeStruct(features.shape, jnp.float32),
        in_specs=[VMEM] * 3,
        out_specs=VMEM,
        scratch_shapes=moved,
        compiler_params=params(),
        name="conv_own",
        cost_estimate=conv_cost,
    )(activated, shift_matrix, conv_weight)
    decoded = pl.pallas_call(
        conv_halo_kernel,
        out_shape=jax.ShapeDtypeStruct(features.shape, jnp.bfloat16),
        in_specs=[VMEM] * 5,
        out_specs=pl.BlockSpec(memory_space=pl.ANY),
        scratch_shapes=moved
        + [pltpu.VMEM(features.shape, jnp.bfloat16), pltpu.SemaphoreType.DMA((frames,))],
        compiler_params=params(),
        name="conv_halo",
        cost_estimate=conv_cost,
    )(halo, shift_matrix, conv_weight, part, latent)
    return (attended, decoded)


def solution(mesh):
    placed = (
        P(("groups", "span"), None),
        P(("groups", "span"), None),
        P(("groups", "span"), None),
        P(("groups", "span")),
        P(),
        P(("groups", "span"), None, None),
        P(),
        P(),
    )
    return jax.shard_map(
        shards,
        mesh=mesh,
        in_specs=placed,
        out_specs=(P(("groups", "span"), None), P(("groups", "span"), None, None)),
        check_vma=False,
    )
```

```python
import functools

import jax
import jax.numpy as jnp
import numpy as np
from jax import lax
from jax.experimental import pallas as pl
from jax.experimental.pallas import tpu as pltpu
from jax.sharding import PartitionSpec as P

HEAD_DIM = 128
LOOKBACK = 3
SIDE = 16
PATCH = 2
TAPS = 9
EPS = 1e-06

VMEM = pl.BlockSpec(memory_space=pltpu.VMEM)
SMEM = pl.BlockSpec(memory_space=pltpu.SMEM)


def params():
    return pltpu.CompilerParams(vmem_limit_bytes=16 * 1024 * 1024)


def one_hot_kernel(w_far, place_ref, shift_ref, w_near, sem):
    copy = pltpu.make_async_copy(w_far, w_near, sem)
    copy.start()
    half = SIDE // PATCH
    patches = half * half
    pixels = SIDE * SIDE
    tokens = place_ref.shape[0] // (PATCH * PATCH)
    column = lax.broadcasted_iota(jnp.int32, (tokens, place_ref.shape[1]), 1)
    pixel = column % pixels
    row, col = pixel // SIDE, pixel % SIDE
    token = column // pixels * patches + row // PATCH * half + col // PATCH
    corner = row % PATCH * PATCH + col % PATCH
    hit = lax.broadcasted_iota(jnp.int32, token.shape, 0) == token
    for k in range(PATCH * PATCH):
        place_ref[pl.ds(k * tokens, tokens), :] = jnp.where(
            hit & (corner == k), 1.0, 0.0
        ).astype(jnp.bfloat16)
    source = lax.broadcasted_iota(jnp.int32, (pixels, pixels), 0)
    target = lax.broadcasted_iota(jnp.int32, (pixels, pixels), 1)
    for b in range(3):
        for e in range(3):
            r, c = target // SIDE + b - 1, target % SIDE + e - 1
            inside = (r >= 0) & (r < SIDE) & (c >= 0) & (c < SIDE)
            tap = 3 * b + e
            shift_ref[:, tap * pixels : (tap + 1) * pixels] = jnp.where(
                inside & (source == r * SIDE + c), 1.0, 0.0
            ).astype(jnp.bfloat16)
    copy.wait()


UNSEEN = LOOKBACK + 1
DISTANCES = ((0, UNSEEN, 3, 2, 1), (0, 1, UNSEEN, 2, 3), (0, 2, 3, UNSEEN, 1), (0, 1, 3, 2, UNSEEN))
RATE = float(np.log2(np.e) * HEAD_DIM**-0.5)


def biases(lookback):
    place = lax.rem(lax.axis_index("span"), 4)
    out = []
    for ways in zip(*DISTANCES):
        distance = ways[0]
        for k, way in enumerate(ways[1:], 1):
            distance = jnp.where(place == k, way, distance)
        out.append(jnp.where(distance <= lookback[0], 0.0, -jnp.inf).astype(jnp.float32))
    return out


def head(h):
    return slice(h * HEAD_DIM, (h + 1) * HEAD_DIM)


def staged(heads, *stages):
    held = {}
    for step in range(heads + len(stages) - 1):
        for i, stage in enumerate(stages):
            h = step - i
            if 0 <= h < heads:
                held[h] = stage(h, held.get(h))


def scores_of(q_ref, blocks, biases, h):
    keys = jnp.concatenate(blocks, axis=0)
    s = lax.dot_general(
        q_ref[:, head(h)], keys, (((1,), (1,)), ((), ())), preferred_element_type=jnp.float32
    )
    rows = blocks[0].shape[0]
    parts = [s[:, i * rows : (i + 1) * rows] for i in range(len(blocks))]
    return [part if bias is None else part + bias for part, bias in zip(parts, biases)]


def top_of(parts):
    return jnp.max(functools.reduce(jnp.maximum, parts), axis=1, keepdims=True)


def early_kernel(
    lookback, q_ref, k0, k_hop, k_own, k2, v0, v_hop, v_own, v2, mixed_ref, top_ref, total_ref
):
    rows = q_ref.shape[0]
    bias = biases(lookback)
    hopped = lax.rem(lax.axis_index("span"), 2) == 0
    ones = jnp.ones((3 * rows, HEAD_DIM), jnp.bfloat16)

    def score(h, _):
        k1 = jnp.where(hopped, k_hop[:, head(h)], k_own[:, head(h)])
        keys = (k0[:, head(h)], k1, k2[:, head(h)])
        return scores_of(q_ref, keys, (None, bias[1], bias[2]), h)

    def soften(h, parts):
        top = top_of(parts)
        top_ref[:, head(h)] = jnp.broadcast_to(top, (rows, HEAD_DIM))
        probs = [jnp.exp2((part - top) * RATE).astype(jnp.bfloat16) for part in parts]
        return jnp.concatenate(probs, axis=1)

    def blend(h, probs):
        v1 = jnp.where(hopped, v_hop[:, head(h)], v_own[:, head(h)])
        values = jnp.concatenate([v0[:, head(h)], v1, v2[:, head(h)]], axis=0)
        both = jnp.dot(
            probs, jnp.concatenate([values, ones], axis=1), preferred_element_type=jnp.float32
        )
        mixed_ref[:, head(h)] = both[:, :HEAD_DIM]
        total_ref[:, head(h)] = both[:, HEAD_DIM:]

    staged(q_ref.shape[1] // HEAD_DIM, score, soften, blend)


def late_kernel(
    lookback, q_ref, k1, k2, mixed_ref, top_ref, total_ref, p_ref, base_ref, inverse_ref
):
    rows = q_ref.shape[0]
    ones = jnp.ones((2 * rows, HEAD_DIM), jnp.bfloat16)
    bias = biases(lookback)

    def score(h, _):
        return scores_of(q_ref, (k1[:, head(h)], k2[:, head(h)]), (bias[3], bias[4]), h)

    def soften(h, parts):
        before = top_ref[:, head(h)]
        top = jnp.maximum(before, top_of(parts))
        probs = [jnp.exp2((part - top) * RATE).astype(jnp.bfloat16) for part in parts]
        probs = jnp.concatenate(probs, axis=1)
        p_ref[h] = probs
        return probs, jnp.exp2((before - top) * RATE)

    def settle(h, held):
        probs, shrink = held
        total = jnp.dot(probs, ones, preferred_element_type=jnp.float32)
        inverse = 1.0 / (total + total_ref[:, head(h)] * shrink)
        inverse_ref[:, head(h)] = inverse
        base_ref[:, head(h)] = mixed_ref[:, head(h)] * (shrink * inverse)

    staged(q_ref.shape[1] // HEAD_DIM, score, soften, settle)


def latent_kernel(
    p_ref, base_ref, inverse_ref, v1, v2, w_ref, place_ref, features_ref, gain_ref,
    out_ref, latent_ref, act_ref, mine, turned, sem,
):
    frames, channels, pixels = features_ref.shape

    heads = mine.shape[1] // HEAD_DIM
    group = 4

    def blend(g, _):
        late = []
        for h in range(g * group, (g + 1) * group):
            values = jnp.concatenate([v1[:, head(h)], v2[:, head(h)]], axis=0)
            late.append(jnp.dot(p_ref[h], values, preferred_element_type=jnp.float32))
        return late

    def settle(g, late):
        for h, part in zip(range(g * group, (g + 1) * group), late):
            part = base_ref[:, head(h)] + part * inverse_ref[:, head(h)]
            mine[:, head(h)] = part.astype(jnp.bfloat16)

    def project(g, _):
        cols = slice(g * group * HEAD_DIM, (g + 1) * group * HEAD_DIM)
        part = jnp.dot(mine[:, cols], w_ref[cols, :], preferred_element_type=jnp.float32)
        products.append(part if not products else products.pop() + part)

    products = []
    staged(heads // group, blend, settle, project)
    copy = pltpu.make_async_copy(mine, out_ref, sem)
    copy.start()
    projected = products[0]
    turned[...] = projected.T
    parts = [turned[pl.ds(k, channels, stride=4), :] for k in range(4)]
    mixed = jnp.concatenate(parts, axis=1)
    high = mixed.astype(jnp.bfloat16)
    low = (mixed - high.astype(jnp.float32)).astype(jnp.bfloat16)
    placed = jnp.dot(high, place_ref[...], preferred_element_type=jnp.float32)
    placed += jnp.dot(low, place_ref[...], preferred_element_type=jnp.float32)
    gain = jnp.broadcast_to(gain_ref[...], (8, channels)).T[:, :1]
    for f in range(frames):
        latent = features_ref[f].astype(jnp.float32) + placed[:, f * pixels : (f + 1) * pixels]
        latent = latent.astype(jnp.bfloat16)
        latent_ref[f] = latent
        data = latent.astype(jnp.float32)
        mean_square = jnp.mean(data * data, axis=0, keepdims=True)
        normed = data * lax.rsqrt(mean_square + EPS) * gain
        act_ref[f] = (normed / (1.0 + jnp.exp(-normed))).astype(jnp.bfloat16)
    copy.wait()


def shifted_taps(frames_ref, shift_ref, use):
    pixels = frames_ref.shape[2]

    def shift(tap, _):
        return [
            jnp.dot(
                frames_ref[f], shift_ref[:, tap * pixels : (tap + 1) * pixels],
                preferred_element_type=jnp.float32,
            ).astype(jnp.bfloat16)
            for f in range(2)
        ]

    staged(TAPS, shift, use)


def conv_own_kernel(act_ref, shift_ref, w_ref, part_ref):
    def use(tap, frames):
        first = tap_dot(w_ref, 2, tap, frames[0])
        second = tap_dot(w_ref, 1, tap, frames[0]) + tap_dot(w_ref, 2, tap, frames[1])
        part_ref[0] = first if tap == 0 else part_ref[0] + first
        part_ref[1] = second if tap == 0 else part_ref[1] + second

    shifted_taps(act_ref, shift_ref, use)


def conv_halo_kernel(halo_ref, shift_ref, w_ref, part_ref, latent_ref, out_ref, sums):
    def use(tap, frames):
        first = tap_dot(w_ref, 0, tap, frames[0]) + tap_dot(w_ref, 1, tap, frames[1])
        second = tap_dot(w_ref, 0, tap, frames[1])
        before = part_ref if tap == 0 else sums
        first, second = before[0] + first, before[1] + second
        if tap < TAPS - 1:
            sums[0], sums[1] = first, second
        else:
            out_ref[0] = (latent_ref[0].astype(jnp.float32) + first).astype(jnp.bfloat16)
            out_ref[1] = (latent_ref[1].astype(jnp.float32) + second).astype(jnp.bfloat16)

    shifted_taps(halo_ref, shift_ref, use)


def tap_dot(w_ref, lag, tap, frame):
    return jnp.dot(w_ref[lag * TAPS + tap], frame, preferred_element_type=jnp.float32)


def routes(count):
    own, hop1, swap1, hop2, swap2 = [], [], [], [], []
    for s in range(count):
        r, first, last = s % 4, s < 4, s + 4 >= count
        if r == 0:
            own.append((s, s + 1))
            hop1.append((s, s + 2))
            if not last:
                hop2.append((s, s + 4))
            if not first:
                swap2.append((s, s + 1))
        elif r == 1:
            if not last:
                hop1.append((s, s + 4))
            hop2.append((s, s + 2))
            if not first:
                swap1.append((s, s - 1))
                swap2.append((s, s - 1))
        elif r == 2:
            own.append((s, s + 1))
            if not last:
                hop1.append((s, s - 2))
            swap1.append((s, s + 1))
        else:
            if not last:
                hop1.append((s, s + 4))
            if not first:
                swap1.append((s, s - 1))
                hop2.append((s, s - 2))
            swap2.append((s, s - 1))
    return own, hop1, swap1, hop2, swap2


def shards(queries, keys, values, lookback, proj_weight, features, norm_gain, conv_weight):
    count = lax.axis_size("span")
    me = lax.axis_index("span")
    second = lax.rem(me, 4) == 1
    second, keys, values = lax.optimization_barrier((second, keys, values))
    own, hop1, swap1, hop2, swap2 = routes(count)
    move = functools.partial(lax.ppermute, axis_name="span")

    rows, width = queries.shape
    heads = width // HEAD_DIM
    frames, channels, pixels = features.shape

    block = jax.ShapeDtypeStruct((rows, width), jnp.float32)
    picture = jax.ShapeDtypeStruct(features.shape, jnp.bfloat16)

    k_r1 = move(keys, perm=hop1)
    k_s0 = move(keys, perm=own)
    v_r1 = move(values, perm=hop1)
    v_s0 = move(values, perm=own)

    tokens = frames * pixels // (PATCH * PATCH)
    place_matrix, shift_matrix, w_near = pl.pallas_call(
        one_hot_kernel,
        out_shape=(
            jax.ShapeDtypeStruct((PATCH * PATCH * tokens, frames * pixels), jnp.bfloat16),
            jax.ShapeDtypeStruct((pixels, TAPS * pixels), jnp.bfloat16),
            jax.ShapeDtypeStruct(proj_weight.shape, jnp.bfloat16),
        ),
        in_specs=[pl.BlockSpec(memory_space=pl.ANY)],
        out_specs=(VMEM,) * 3,
        scratch_shapes=[pltpu.SemaphoreType.DMA],
        compiler_params=params(),
        name="one_hot",
    )(proj_weight)
    k_r1, place_matrix, shift_matrix, w_near = lax.optimization_barrier(
        (k_r1, place_matrix, shift_matrix, w_near)
    )

    k_r2 = move(jnp.where(second, keys, k_r1), perm=hop2)
    k_s1 = move(k_r1, perm=swap1)
    v_hop = jnp.where(second, values, v_r1)
    v_r2 = move(v_hop, perm=hop2)
    v_s1 = move(v_r1, perm=swap1)

    mixed, top, total = pl.pallas_call(
        early_kernel,
        out_shape=(block,) * 3,
        in_specs=[SMEM] + [VMEM] * 9,
        out_specs=(VMEM,) * 3,
        compiler_params=params(),
        name="early",
        cost_estimate=pl.CostEstimate(
            flops=12 * rows * rows * width,
            bytes_accessed=9 * rows * width * 2,
            transcendentals=3 * heads * rows * rows,
        ),
    )(
        lookback, queries, keys, k_r1, k_s0, k_s1, values, v_r1, v_s0, v_s1,
    )

    k_s2 = move(k_r2, perm=swap2)
    weights, base, inverse = pl.pallas_call(
        late_kernel,
        out_shape=(
            jax.ShapeDtypeStruct((heads, rows, 2 * rows), jnp.bfloat16), block, block,
        ),
        in_specs=[SMEM] + [VMEM] * 6,
        out_specs=(VMEM,) * 3,
        compiler_params=params(),
        name="late",
        cost_estimate=pl.CostEstimate(
            flops=4 * rows * rows * width,
            bytes_accessed=9 * rows * width * 2,
            transcendentals=2 * heads * rows * rows,
        ),
    )(lookback, queries, k_r2, k_s2, mixed, top, total)

    v_r2, _ = lax.optimization_barrier((v_r2, mixed))
    v_s2 = move(v_r2, perm=swap2)
    patch_width = proj_weight.shape[1]
    attended, latent, activated = pl.pallas_call(
        latent_kernel,
        out_shape=(jax.ShapeDtypeStruct((rows, width), jnp.bfloat16), picture, picture),
        in_specs=[VMEM] * 9,
        out_specs=(pl.BlockSpec(memory_space=pl.ANY), VMEM, VMEM),
        scratch_shapes=[
            pltpu.VMEM((rows, width), jnp.bfloat16),
            pltpu.VMEM((patch_width, rows), jnp.float32),
            pltpu.SemaphoreType.DMA,
        ],
        compiler_params=params(),
        name="latent",
        cost_estimate=pl.CostEstimate(
            flops=2 * rows * width * (2 * rows + patch_width),
            bytes_accessed=10 * rows * width * 2 + width * patch_width * 2,
            transcendentals=features.size,
        ),
    )(
        weights, base, inverse, v_r2, v_s2, w_near, place_matrix, features,
        norm_gain.reshape(1, channels),
    )

    halo = move(activated, perm=[(s, s + 1) for s in range(count - 1)])

    conv_cost = pl.CostEstimate(
        flops=2 * channels * TAPS * channels * pixels * 3,
        bytes_accessed=conv_weight.size * 2 + shift_matrix.size * 2,
        transcendentals=0,
    )
    part = pl.pallas_call(
        conv_own_kernel,
        out_shape=jax.ShapeDtypeStruct(features.shape, jnp.float32),
        in_specs=[VMEM] * 3,
        out_specs=VMEM,
        compiler_params=params(),
        name="conv_own",
        cost_estimate=conv_cost,
    )(activated, shift_matrix, conv_weight)
    decoded = pl.pallas_call(
        conv_halo_kernel,
        out_shape=jax.ShapeDtypeStruct(features.shape, jnp.bfloat16),
        in_specs=[VMEM] * 5,
        out_specs=VMEM,
        scratch_shapes=[pltpu.VMEM(features.shape, jnp.float32)],
        compiler_params=params(),
        name="conv_halo",
        cost_estimate=conv_cost,
    )(halo, shift_matrix, conv_weight, part, latent)
    return (attended, decoded)


def solution(mesh):
    placed = (
        P(("groups", "span"), None),
        P(("groups", "span"), None),
        P(("groups", "span"), None),
        P(("groups", "span")),
        P(),
        P(("groups", "span"), None, None),
        P(),
        P(),
    )
    return jax.shard_map(
        shards,
        mesh=mesh,
        in_specs=placed,
        out_specs=(P(("groups", "span"), None), P(("groups", "span"), None, None)),
        check_vma=False,
    )
```

```python
import functools

import jax
import jax.numpy as jnp
import numpy as np
from jax import lax
from jax.experimental import pallas as pl
from jax.experimental.pallas import tpu as pltpu
from jax.sharding import PartitionSpec as P

HEAD_DIM = 128
LOOKBACK = 3
SIDE = 16
PATCH = 2
TAPS = 9
EPS = 1e-06

VMEM = pl.BlockSpec(memory_space=pltpu.VMEM)
SMEM = pl.BlockSpec(memory_space=pltpu.SMEM)


def params():
    return pltpu.CompilerParams(vmem_limit_bytes=16 * 1024 * 1024)


def one_hot_kernel(w_far, place_ref, shift_ref, w_near, sem):
    copy = pltpu.make_async_copy(w_far, w_near, sem)
    copy.start()
    half = SIDE // PATCH
    patches = half * half
    pixels = SIDE * SIDE
    tokens = place_ref.shape[0] // (PATCH * PATCH)
    column = lax.broadcasted_iota(jnp.int32, (tokens, place_ref.shape[1]), 1)
    pixel = column % pixels
    row, col = pixel // SIDE, pixel % SIDE
    token = column // pixels * patches + row // PATCH * half + col // PATCH
    corner = row % PATCH * PATCH + col % PATCH
    hit = lax.broadcasted_iota(jnp.int32, token.shape, 0) == token
    for k in range(PATCH * PATCH):
        place_ref[pl.ds(k * tokens, tokens), :] = jnp.where(
            hit & (corner == k), 1.0, 0.0
        ).astype(jnp.bfloat16)
    source = lax.broadcasted_iota(jnp.int32, (pixels, pixels), 0)
    target = lax.broadcasted_iota(jnp.int32, (pixels, pixels), 1)
    for b in range(3):
        for e in range(3):
            r, c = target // SIDE + b - 1, target % SIDE + e - 1
            inside = (r >= 0) & (r < SIDE) & (c >= 0) & (c < SIDE)
            tap = 3 * b + e
            shift_ref[:, tap * pixels : (tap + 1) * pixels] = jnp.where(
                inside & (source == r * SIDE + c), 1.0, 0.0
            ).astype(jnp.bfloat16)
    copy.wait()


UNSEEN = LOOKBACK + 1
DISTANCES = ((0, UNSEEN, 3, 2, 1), (0, 1, UNSEEN, 2, 3), (0, 2, 3, UNSEEN, 1), (0, 1, 3, 2, UNSEEN))
RATE = float(np.log2(np.e) * HEAD_DIM**-0.5)


def biases(lookback):
    place = lax.rem(lax.axis_index("span"), 4)
    out = []
    for ways in zip(*DISTANCES):
        distance = ways[0]
        for k, way in enumerate(ways[1:], 1):
            distance = jnp.where(place == k, way, distance)
        out.append(jnp.where(distance <= lookback[0], 0.0, -jnp.inf).astype(jnp.float32))
    return out


def head(h):
    return slice(h * HEAD_DIM, (h + 1) * HEAD_DIM)


def staged(heads, *stages):
    held = {}
    for step in range(heads + len(stages) - 1):
        for i, stage in enumerate(stages):
            h = step - i
            if 0 <= h < heads:
                held[h] = stage(h, held.get(h))


def scores_of(q_ref, blocks, biases, h):
    keys = jnp.concatenate(blocks, axis=0)
    s = lax.dot_general(
        q_ref[:, head(h)], keys, (((1,), (1,)), ((), ())), preferred_element_type=jnp.float32
    )
    rows = blocks[0].shape[0]
    parts = [s[:, i * rows : (i + 1) * rows] for i in range(len(blocks))]
    return [part if bias is None else part + bias for part, bias in zip(parts, biases)]


def top_of(parts):
    return jnp.max(functools.reduce(jnp.maximum, parts), axis=1, keepdims=True)


def early_kernel(
    lookback, q_ref, k0, k_hop, k_own, v0, v_hop, v_own, mixed_ref, top_ref, total_ref
):
    rows = q_ref.shape[0]
    bias = biases(lookback)
    hopped = lax.rem(lax.axis_index("span"), 2) == 0
    ones = jnp.ones((2 * rows, HEAD_DIM), jnp.bfloat16)

    def score(h, _):
        k1 = jnp.where(hopped, k_hop[:, head(h)], k_own[:, head(h)])
        return scores_of(q_ref, (k0[:, head(h)], k1), (None, bias[1]), h)

    def soften(h, parts):
        top = top_of(parts)
        top_ref[:, head(h)] = jnp.broadcast_to(top, (rows, HEAD_DIM))
        probs = [jnp.exp2((part - top) * RATE).astype(jnp.bfloat16) for part in parts]
        return jnp.concatenate(probs, axis=1)

    def blend(h, probs):
        v1 = jnp.where(hopped, v_hop[:, head(h)], v_own[:, head(h)])
        values = jnp.concatenate([v0[:, head(h)], v1], axis=0)
        both = jnp.dot(
            probs, jnp.concatenate([values, ones], axis=1), preferred_element_type=jnp.float32
        )
        mixed_ref[:, head(h)] = both[:, :HEAD_DIM]
        total_ref[:, head(h)] = both[:, HEAD_DIM:]

    staged(q_ref.shape[1] // HEAD_DIM, score, soften, blend)


def late_kernel(
    lookback, q_ref, k0, k1, k2, mixed_ref, top_ref, total_ref, p_ref, base_ref, inverse_ref
):
    rows = q_ref.shape[0]
    ones = jnp.ones((3 * rows, HEAD_DIM), jnp.bfloat16)
    bias = biases(lookback)

    def score(h, _):
        return scores_of(q_ref, [k[:, head(h)] for k in (k0, k1, k2)], bias[2:], h)

    def soften(h, parts):
        before = top_ref[:, head(h)]
        top = jnp.maximum(before, top_of(parts))
        probs = [jnp.exp2((part - top) * RATE).astype(jnp.bfloat16) for part in parts]
        probs = jnp.concatenate(probs, axis=1)
        p_ref[h] = probs
        return probs, jnp.exp2((before - top) * RATE)

    def settle(h, held):
        probs, shrink = held
        total = jnp.dot(probs, ones, preferred_element_type=jnp.float32)
        inverse = 1.0 / (total + total_ref[:, head(h)] * shrink)
        inverse_ref[:, head(h)] = inverse
        base_ref[:, head(h)] = mixed_ref[:, head(h)] * (shrink * inverse)

    staged(q_ref.shape[1] // HEAD_DIM, score, soften, settle)


def latent_kernel(
    p_ref, base_ref, inverse_ref, v0, v1, v2, w_ref, place_ref, features_ref, gain_ref,
    out_ref, latent_ref, act_ref, mine, turned, sem,
):
    frames, channels, pixels = features_ref.shape

    heads = mine.shape[1] // HEAD_DIM
    group = 4

    def blend(g, _):
        late = []
        for h in range(g * group, (g + 1) * group):
            values = jnp.concatenate([v[:, head(h)] for v in (v0, v1, v2)], axis=0)
            late.append(jnp.dot(p_ref[h], values, preferred_element_type=jnp.float32))
        return late

    def settle(g, late):
        for h, part in zip(range(g * group, (g + 1) * group), late):
            part = base_ref[:, head(h)] + part * inverse_ref[:, head(h)]
            mine[:, head(h)] = part.astype(jnp.bfloat16)

    def project(g, _):
        cols = slice(g * group * HEAD_DIM, (g + 1) * group * HEAD_DIM)
        part = jnp.dot(mine[:, cols], w_ref[cols, :], preferred_element_type=jnp.float32)
        products.append(part if not products else products.pop() + part)

    products = []
    staged(heads // group, blend, settle, project)
    copy = pltpu.make_async_copy(mine, out_ref, sem)
    copy.start()
    projected = products[0]
    turned[...] = projected.T
    parts = [turned[pl.ds(k, channels, stride=4), :] for k in range(4)]
    mixed = jnp.concatenate(parts, axis=1)
    high = mixed.astype(jnp.bfloat16)
    low = (mixed - high.astype(jnp.float32)).astype(jnp.bfloat16)
    placed = jnp.dot(high, place_ref[...], preferred_element_type=jnp.float32)
    placed += jnp.dot(low, place_ref[...], preferred_element_type=jnp.float32)
    gain = jnp.broadcast_to(gain_ref[...], (8, channels)).T[:, :1]
    for f in range(frames):
        latent = features_ref[f].astype(jnp.float32) + placed[:, f * pixels : (f + 1) * pixels]
        latent = latent.astype(jnp.bfloat16)
        latent_ref[f] = latent
        data = latent.astype(jnp.float32)
        mean_square = jnp.mean(data * data, axis=0, keepdims=True)
        normed = data * lax.rsqrt(mean_square + EPS) * gain
        act_ref[f] = (normed / (1.0 + jnp.exp(-normed))).astype(jnp.bfloat16)
    copy.wait()


def spread(act, shift_ref, moved):
    channels, pixels = act.shape
    for tap in range(TAPS):
        moved[pl.ds(tap * channels, channels), :] = jnp.dot(
            act, shift_ref[:, tap * pixels : (tap + 1) * pixels],
            preferred_element_type=jnp.float32,
        ).astype(jnp.bfloat16)


def tap_dot(w_ref, lag, moved):
    channels = w_ref.shape[2]
    return sum(
        jnp.dot(
            w_ref[lag * TAPS + tap], moved[pl.ds(tap * channels, channels), :],
            preferred_element_type=jnp.float32,
        )
        for tap in range(TAPS)
    )


def conv_own_kernel(act_ref, shift_ref, w_ref, part_ref, moved0, moved1):
    spread(act_ref[0], shift_ref, moved0)
    spread(act_ref[1], shift_ref, moved1)
    part_ref[0] = tap_dot(w_ref, 2, moved0)
    part_ref[1] = tap_dot(w_ref, 1, moved0) + tap_dot(w_ref, 2, moved1)


def conv_halo_kernel(halo_ref, shift_ref, w_ref, part_ref, latent_ref, out_ref, moved0, moved1):
    spread(halo_ref[0], shift_ref, moved0)
    spread(halo_ref[1], shift_ref, moved1)
    first = part_ref[0] + tap_dot(w_ref, 0, moved0) + tap_dot(w_ref, 1, moved1)
    second = part_ref[1] + tap_dot(w_ref, 0, moved1)
    out_ref[0] = (latent_ref[0].astype(jnp.float32) + first).astype(jnp.bfloat16)
    out_ref[1] = (latent_ref[1].astype(jnp.float32) + second).astype(jnp.bfloat16)


def routes(count):
    own, hop1, swap1, hop2, swap2 = [], [], [], [], []
    for s in range(count):
        r, first, last = s % 4, s < 4, s + 4 >= count
        if r == 0:
            own.append((s, s + 1))
            hop1.append((s, s + 2))
            if not last:
                hop2.append((s, s + 4))
            if not first:
                swap2.append((s, s + 1))
        elif r == 1:
            if not last:
                hop1.append((s, s + 4))
            hop2.append((s, s + 2))
            if not first:
                swap1.append((s, s - 1))
                swap2.append((s, s - 1))
        elif r == 2:
            own.append((s, s + 1))
            if not last:
                hop1.append((s, s - 2))
            swap1.append((s, s + 1))
        else:
            if not last:
                hop1.append((s, s + 4))
            if not first:
                swap1.append((s, s - 1))
                hop2.append((s, s - 2))
            swap2.append((s, s - 1))
    return own, hop1, swap1, hop2, swap2


def shards(queries, keys, values, lookback, proj_weight, features, norm_gain, conv_weight):
    count = lax.axis_size("span")
    me = lax.axis_index("span")
    second = lax.rem(me, 4) == 1
    second, keys, values = lax.optimization_barrier((second, keys, values))
    own, hop1, swap1, hop2, swap2 = routes(count)
    move = functools.partial(lax.ppermute, axis_name="span")

    rows, width = queries.shape
    heads = width // HEAD_DIM
    frames, channels, pixels = features.shape

    block = jax.ShapeDtypeStruct((rows, width), jnp.float32)
    picture = jax.ShapeDtypeStruct(features.shape, jnp.bfloat16)

    k_r1 = move(keys, perm=hop1)
    k_s0 = move(keys, perm=own)
    v_r1 = move(values, perm=hop1)
    v_s0 = move(values, perm=own)

    tokens = frames * pixels // (PATCH * PATCH)
    place_matrix, shift_matrix, w_near = pl.pallas_call(
        one_hot_kernel,
        out_shape=(
            jax.ShapeDtypeStruct((PATCH * PATCH * tokens, frames * pixels), jnp.bfloat16),
            jax.ShapeDtypeStruct((pixels, TAPS * pixels), jnp.bfloat16),
            jax.ShapeDtypeStruct(proj_weight.shape, jnp.bfloat16),
        ),
        in_specs=[pl.BlockSpec(memory_space=pl.ANY)],
        out_specs=(VMEM,) * 3,
        scratch_shapes=[pltpu.SemaphoreType.DMA],
        compiler_params=params(),
        name="one_hot",
    )(proj_weight)
    k_r1, place_matrix, shift_matrix, w_near = lax.optimization_barrier(
        (k_r1, place_matrix, shift_matrix, w_near)
    )

    k_r2 = move(jnp.where(second, keys, k_r1), perm=hop2)
    k_s1 = move(k_r1, perm=swap1)
    v_hop = jnp.where(second, values, v_r1)
    v_r2 = move(v_hop, perm=hop2)
    v_s1 = move(v_r1, perm=swap1)

    mixed, top, total = pl.pallas_call(
        early_kernel,
        out_shape=(block,) * 3,
        in_specs=[SMEM] + [VMEM] * 7,
        out_specs=(VMEM,) * 3,
        compiler_params=params(),
        name="early",
        cost_estimate=pl.CostEstimate(
            flops=8 * rows * rows * width,
            bytes_accessed=9 * rows * width * 2,
            transcendentals=2 * heads * rows * rows,
        ),
    )(
        lookback, queries, keys, k_r1, k_s0, values, v_r1, v_s0,
    )

    k_s2 = move(k_r2, perm=swap2)
    weights, base, inverse = pl.pallas_call(
        late_kernel,
        out_shape=(
            jax.ShapeDtypeStruct((heads, rows, 3 * rows), jnp.bfloat16), block, block,
        ),
        in_specs=[SMEM] + [VMEM] * 7,
        out_specs=(VMEM,) * 3,
        compiler_params=params(),
        name="late",
        cost_estimate=pl.CostEstimate(
            flops=6 * rows * rows * width,
            bytes_accessed=9 * rows * width * 2,
            transcendentals=3 * heads * rows * rows,
        ),
    )(lookback, queries, k_s1, k_r2, k_s2, mixed, top, total)

    v_r2, _ = lax.optimization_barrier((v_r2, mixed))
    v_s2 = move(v_r2, perm=swap2)
    patch_width = proj_weight.shape[1]
    attended, latent, activated = pl.pallas_call(
        latent_kernel,
        out_shape=(jax.ShapeDtypeStruct((rows, width), jnp.bfloat16), picture, picture),
        in_specs=[VMEM] * 10,
        out_specs=(pl.BlockSpec(memory_space=pl.ANY), VMEM, VMEM),
        scratch_shapes=[
            pltpu.VMEM((rows, width), jnp.bfloat16),
            pltpu.VMEM((patch_width, rows), jnp.float32),
            pltpu.SemaphoreType.DMA,
        ],
        compiler_params=params(),
        name="latent",
        cost_estimate=pl.CostEstimate(
            flops=2 * rows * width * (2 * rows + patch_width),
            bytes_accessed=10 * rows * width * 2 + width * patch_width * 2,
            transcendentals=features.size,
        ),
    )(
        weights, base, inverse, v_s1, v_r2, v_s2, w_near, place_matrix, features,
        norm_gain.reshape(1, channels),
    )

    halo = move(activated, perm=[(s, s + 1) for s in range(count - 1)])

    moved = [pltpu.VMEM((TAPS * channels, pixels), jnp.bfloat16)] * 2
    conv_cost = pl.CostEstimate(
        flops=2 * channels * TAPS * channels * pixels * 3,
        bytes_accessed=conv_weight.size * 2 + shift_matrix.size * 2,
        transcendentals=0,
    )
    part = pl.pallas_call(
        conv_own_kernel,
        out_shape=jax.ShapeDtypeStruct(features.shape, jnp.float32),
        in_specs=[VMEM] * 3,
        out_specs=VMEM,
        scratch_shapes=moved,
        compiler_params=params(),
        name="conv_own",
        cost_estimate=conv_cost,
    )(activated, shift_matrix, conv_weight)
    decoded = pl.pallas_call(
        conv_halo_kernel,
        out_shape=jax.ShapeDtypeStruct(features.shape, jnp.bfloat16),
        in_specs=[VMEM] * 5,
        out_specs=VMEM,
        scratch_shapes=moved,
        compiler_params=params(),
        name="conv_halo",
        cost_estimate=conv_cost,
    )(halo, shift_matrix, conv_weight, part, latent)
    return (attended, decoded)


def solution(mesh):
    placed = (
        P(("groups", "span"), None),
        P(("groups", "span"), None),
        P(("groups", "span"), None),
        P(("groups", "span")),
        P(),
        P(("groups", "span"), None, None),
        P(),
        P(),
    )
    return jax.shard_map(
        shards,
        mesh=mesh,
        in_specs=placed,
        out_specs=(P(("groups", "span"), None), P(("groups", "span"), None, None)),
        check_vma=False,
    )
```

```python
import functools

import jax
import jax.numpy as jnp
import numpy as np
from jax import lax
from jax.experimental import pallas as pl
from jax.experimental.pallas import tpu as pltpu
from jax.sharding import PartitionSpec as P

HEAD_DIM = 128
LOOKBACK = 3
SIDE = 16
PATCH = 2
TAPS = 9
EPS = 1e-06

VMEM = pl.BlockSpec(memory_space=pltpu.VMEM)
SMEM = pl.BlockSpec(memory_space=pltpu.SMEM)


def params():
    return pltpu.CompilerParams(vmem_limit_bytes=16 * 1024 * 1024)


def one_hot_kernel(w_far, place_ref, shift_ref, w_near, sem):
    copy = pltpu.make_async_copy(w_far, w_near, sem)
    copy.start()
    half = SIDE // PATCH
    patches = half * half
    pixels = SIDE * SIDE
    tokens = place_ref.shape[0] // (PATCH * PATCH)
    column = lax.broadcasted_iota(jnp.int32, (tokens, place_ref.shape[1]), 1)
    pixel = column % pixels
    row, col = pixel // SIDE, pixel % SIDE
    token = column // pixels * patches + row // PATCH * half + col // PATCH
    corner = row % PATCH * PATCH + col % PATCH
    hit = lax.broadcasted_iota(jnp.int32, token.shape, 0) == token
    for k in range(PATCH * PATCH):
        place_ref[pl.ds(k * tokens, tokens), :] = jnp.where(
            hit & (corner == k), 1.0, 0.0
        ).astype(jnp.bfloat16)
    source = lax.broadcasted_iota(jnp.int32, (pixels, pixels), 0)
    target = lax.broadcasted_iota(jnp.int32, (pixels, pixels), 1)
    for b in range(3):
        for e in range(3):
            r, c = target // SIDE + b - 1, target % SIDE + e - 1
            inside = (r >= 0) & (r < SIDE) & (c >= 0) & (c < SIDE)
            tap = 3 * b + e
            shift_ref[:, tap * pixels : (tap + 1) * pixels] = jnp.where(
                inside & (source == r * SIDE + c), 1.0, 0.0
            ).astype(jnp.bfloat16)
    copy.wait()


UNSEEN = LOOKBACK + 1
DISTANCES = ((0, UNSEEN, 3, 2, 1), (0, 1, UNSEEN, 2, 3), (0, 2, 3, UNSEEN, 1), (0, 1, 3, 2, UNSEEN))
RATE = float(np.log2(np.e) * HEAD_DIM**-0.5)


def biases(lookback):
    place = lax.rem(lax.axis_index("span"), 4)
    out = []
    for ways in zip(*DISTANCES):
        distance = ways[0]
        for k, way in enumerate(ways[1:], 1):
            distance = jnp.where(place == k, way, distance)
        out.append(jnp.where(distance <= lookback[0], 0.0, -jnp.inf).astype(jnp.float32))
    return out


def head(h):
    return pl.ds(pl.multiple_of(h * HEAD_DIM, HEAD_DIM), HEAD_DIM)


def staged(heads, *stages):
    held = {}
    for step in range(heads + len(stages) - 1):
        for i, stage in enumerate(stages):
            h = step - i
            if 0 <= h < heads:
                held[h] = stage(h, held.get(h))


GROUP = 4


def grouped(heads, *stages):
    def body(g, carry):
        staged(GROUP, *[lambda i, held, s=stage: s(g * GROUP + i, held) for stage in stages])
        return carry

    lax.fori_loop(0, heads // GROUP, body, 0)


def scores_of(q_ref, blocks, biases, h):
    keys = jnp.concatenate(blocks, axis=0)
    s = lax.dot_general(
        q_ref[:, head(h)], keys, (((1,), (1,)), ((), ())), preferred_element_type=jnp.float32
    )
    rows = blocks[0].shape[0]
    parts = [s[:, i * rows : (i + 1) * rows] for i in range(len(blocks))]
    return [part if bias is None else part + bias for part, bias in zip(parts, biases)]


def top_of(parts):
    return jnp.max(functools.reduce(jnp.maximum, parts), axis=1, keepdims=True)


def early_kernel(
    lookback, q_ref, k0, k_hop, k_own, k2, v0, v_hop, v_own, v2, mixed_ref, top_ref, total_ref
):
    rows = q_ref.shape[0]
    bias = biases(lookback)
    hopped = lax.rem(lax.axis_index("span"), 2) == 0
    ones = jnp.ones((3 * rows, HEAD_DIM), jnp.bfloat16)

    def score(h, _):
        k1 = jnp.where(hopped, k_hop[:, head(h)], k_own[:, head(h)])
        keys = (k0[:, head(h)], k1, k2[:, head(h)])
        return scores_of(q_ref, keys, (None, bias[1], bias[2]), h)

    def soften(h, parts):
        top = top_of(parts)
        top_ref[:, head(h)] = jnp.broadcast_to(top, (rows, HEAD_DIM))
        probs = [jnp.exp2((part - top) * RATE).astype(jnp.bfloat16) for part in parts]
        return jnp.concatenate(probs, axis=1)

    def blend(h, probs):
        v1 = jnp.where(hopped, v_hop[:, head(h)], v_own[:, head(h)])
        values = jnp.concatenate([v0[:, head(h)], v1, v2[:, head(h)]], axis=0)
        both = jnp.dot(
            probs, jnp.concatenate([values, ones], axis=1), preferred_element_type=jnp.float32
        )
        mixed_ref[:, head(h)] = both[:, :HEAD_DIM]
        total_ref[:, head(h)] = both[:, HEAD_DIM:]

    grouped(q_ref.shape[1] // HEAD_DIM, score, soften, blend)


def late_kernel(
    lookback, q_ref, k1, k2, mixed_ref, top_ref, total_ref, p_ref, base_ref, inverse_ref
):
    rows = q_ref.shape[0]
    ones = jnp.ones((2 * rows, HEAD_DIM), jnp.bfloat16)
    bias = biases(lookback)

    def score(h, _):
        return scores_of(q_ref, (k1[:, head(h)], k2[:, head(h)]), (bias[3], bias[4]), h)

    def soften(h, parts):
        before = top_ref[:, head(h)]
        top = jnp.maximum(before, top_of(parts))
        probs = [jnp.exp2((part - top) * RATE).astype(jnp.bfloat16) for part in parts]
        probs = jnp.concatenate(probs, axis=1)
        p_ref[h] = probs
        return probs, jnp.exp2((before - top) * RATE)

    def settle(h, held):
        probs, shrink = held
        total = jnp.dot(probs, ones, preferred_element_type=jnp.float32)
        inverse = 1.0 / (total + total_ref[:, head(h)] * shrink)
        inverse_ref[:, head(h)] = inverse
        base_ref[:, head(h)] = mixed_ref[:, head(h)] * (shrink * inverse)

    grouped(q_ref.shape[1] // HEAD_DIM, score, soften, settle)


def latent_kernel(
    p_ref, base_ref, inverse_ref, v1, v2, w_ref, place_ref, features_ref, gain_ref,
    out_ref, latent_ref, act_ref, mine, sums, turned, sem,
):
    frames, channels, pixels = features_ref.shape

    groups = mine.shape[1] // (GROUP * HEAD_DIM)

    def blend(h, _):
        values = jnp.concatenate([v1[:, head(h)], v2[:, head(h)]], axis=0)
        return jnp.dot(p_ref[h], values, preferred_element_type=jnp.float32)

    def settle(h, late):
        late = base_ref[:, head(h)] + late * inverse_ref[:, head(h)]
        mine[:, head(h)] = late.astype(jnp.bfloat16)

    def attend(g):
        staged(
            GROUP, lambda i, _: blend(g * GROUP + i, _), lambda i, x: settle(g * GROUP + i, x)
        )

    def project(g):
        span = GROUP * HEAD_DIM
        cols = pl.ds(pl.multiple_of(g * span, span), span)
        return jnp.dot(mine[:, cols], w_ref[cols, :], preferred_element_type=jnp.float32)

    attend(0)
    sums[...] = jnp.zeros_like(sums)

    def body(g, carry):
        attend(g)
        sums[...] += project(g - 1)
        return carry

    lax.fori_loop(1, groups, body, 0)
    copy = pltpu.make_async_copy(mine, out_ref, sem)
    copy.start()
    projected = sums[...] + project(groups - 1)
    turned[...] = projected.T
    parts = [turned[pl.ds(k, channels, stride=4), :] for k in range(4)]
    mixed = jnp.concatenate(parts, axis=1)
    high = mixed.astype(jnp.bfloat16)
    low = (mixed - high.astype(jnp.float32)).astype(jnp.bfloat16)
    placed = jnp.dot(high, place_ref[...], preferred_element_type=jnp.float32)
    placed += jnp.dot(low, place_ref[...], preferred_element_type=jnp.float32)
    gain = jnp.broadcast_to(gain_ref[...], (8, channels)).T[:, :1]
    for f in range(frames):
        latent = features_ref[f].astype(jnp.float32) + placed[:, f * pixels : (f + 1) * pixels]
        latent = latent.astype(jnp.bfloat16)
        latent_ref[f] = latent
        data = latent.astype(jnp.float32)
        mean_square = jnp.mean(data * data, axis=0, keepdims=True)
        normed = data * lax.rsqrt(mean_square + EPS) * gain
        act_ref[f] = (normed / (1.0 + jnp.exp(-normed))).astype(jnp.bfloat16)
    copy.wait()


def over_taps(use):
    def body(b, carry):
        for e in range(3):
            use(3 * b + e)
        return carry

    lax.fori_loop(0, 3, body, 0)


def tap_rows(tap, channels):
    return pl.ds(pl.multiple_of(tap * channels, channels), channels)


def spread(frames_ref, shift_ref, moved):
    frames, channels, pixels = frames_ref.shape

    def use(tap):
        for f in range(frames):
            moved[f, tap_rows(tap, channels), :] = jnp.dot(
                frames_ref[f], shift_ref[:, tap_rows(tap, pixels)],
                preferred_element_type=jnp.float32,
            ).astype(jnp.bfloat16)

    over_taps(use)


def tap_dot(w_ref, lag, tap, moved, f):
    weights = w_ref[lag * TAPS + tap]
    rows = tap_rows(tap, weights.shape[1])
    return jnp.dot(weights, moved[f, rows, :], preferred_element_type=jnp.float32)


def conv_own_kernel(act_ref, shift_ref, w_ref, part_ref, moved):
    spread(act_ref, shift_ref, moved)
    part_ref[...] = jnp.zeros_like(part_ref)

    def use(tap):
        part_ref[0] += tap_dot(w_ref, 2, tap, moved, 0)
        part_ref[1] += tap_dot(w_ref, 1, tap, moved, 0) + tap_dot(w_ref, 2, tap, moved, 1)

    over_taps(use)


def conv_halo_kernel(halo_ref, shift_ref, w_ref, part_ref, latent_ref, out_ref, moved, sums):
    spread(halo_ref, shift_ref, moved)
    sums[...] = part_ref[...] + latent_ref[...].astype(jnp.float32)

    def use(tap):
        sums[0] += tap_dot(w_ref, 0, tap, moved, 0) + tap_dot(w_ref, 1, tap, moved, 1)
        sums[1] += tap_dot(w_ref, 0, tap, moved, 1)

    over_taps(use)
    out_ref[...] = sums[...].astype(jnp.bfloat16)


def routes(count):
    own, hop1, swap1, hop2, swap2 = [], [], [], [], []
    for s in range(count):
        r, first, last = s % 4, s < 4, s + 4 >= count
        if r == 0:
            own.append((s, s + 1))
            hop1.append((s, s + 2))
            if not last:
                hop2.append((s, s + 4))
            if not first:
                swap2.append((s, s + 1))
        elif r == 1:
            if not last:
                hop1.append((s, s + 4))
            hop2.append((s, s + 2))
            if not first:
                swap1.append((s, s - 1))
                swap2.append((s, s - 1))
        elif r == 2:
            own.append((s, s + 1))
            if not last:
                hop1.append((s, s - 2))
            swap1.append((s, s + 1))
        else:
            if not last:
                hop1.append((s, s + 4))
            if not first:
                swap1.append((s, s - 1))
                hop2.append((s, s - 2))
            swap2.append((s, s - 1))
    return own, hop1, swap1, hop2, swap2


def shards(queries, keys, values, lookback, proj_weight, features, norm_gain, conv_weight):
    count = lax.axis_size("span")
    me = lax.axis_index("span")
    second = lax.rem(me, 4) == 1
    second, keys, values = lax.optimization_barrier((second, keys, values))
    own, hop1, swap1, hop2, swap2 = routes(count)
    move = functools.partial(lax.ppermute, axis_name="span")

    rows, width = queries.shape
    heads = width // HEAD_DIM
    frames, channels, pixels = features.shape

    block = jax.ShapeDtypeStruct((rows, width), jnp.float32)
    picture = jax.ShapeDtypeStruct(features.shape, jnp.bfloat16)

    k_r1 = move(keys, perm=hop1)
    k_s0 = move(keys, perm=own)
    v_r1 = move(values, perm=hop1)
    v_s0 = move(values, perm=own)

    tokens = frames * pixels // (PATCH * PATCH)
    place_matrix, shift_matrix, w_near = pl.pallas_call(
        one_hot_kernel,
        out_shape=(
            jax.ShapeDtypeStruct((PATCH * PATCH * tokens, frames * pixels), jnp.bfloat16),
            jax.ShapeDtypeStruct((pixels, TAPS * pixels), jnp.bfloat16),
            jax.ShapeDtypeStruct(proj_weight.shape, jnp.bfloat16),
        ),
        in_specs=[pl.BlockSpec(memory_space=pl.ANY)],
        out_specs=(VMEM,) * 3,
        scratch_shapes=[pltpu.SemaphoreType.DMA],
        compiler_params=params(),
        name="one_hot",
    )(proj_weight)
    k_r1, place_matrix, shift_matrix, w_near = lax.optimization_barrier(
        (k_r1, place_matrix, shift_matrix, w_near)
    )

    k_r2 = move(jnp.where(second, keys, k_r1), perm=hop2)
    k_s1 = move(k_r1, perm=swap1)
    v_hop = jnp.where(second, values, v_r1)
    v_r2 = move(v_hop, perm=hop2)
    v_s1 = move(v_r1, perm=swap1)

    mixed, top, total = pl.pallas_call(
        early_kernel,
        out_shape=(block,) * 3,
        in_specs=[SMEM] + [VMEM] * 9,
        out_specs=(VMEM,) * 3,
        compiler_params=params(),
        name="early",
        cost_estimate=pl.CostEstimate(
            flops=12 * rows * rows * width,
            bytes_accessed=9 * rows * width * 2,
            transcendentals=3 * heads * rows * rows,
        ),
    )(
        lookback, queries, keys, k_r1, k_s0, k_s1, values, v_r1, v_s0, v_s1,
    )

    k_s2 = move(k_r2, perm=swap2)
    weights, base, inverse = pl.pallas_call(
        late_kernel,
        out_shape=(
            jax.ShapeDtypeStruct((heads, rows, 2 * rows), jnp.bfloat16), block, block,
        ),
        in_specs=[SMEM] + [VMEM] * 6,
        out_specs=(VMEM,) * 3,
        compiler_params=params(),
        name="late",
        cost_estimate=pl.CostEstimate(
            flops=4 * rows * rows * width,
            bytes_accessed=9 * rows * width * 2,
            transcendentals=2 * heads * rows * rows,
        ),
    )(lookback, queries, k_r2, k_s2, mixed, top, total)

    v_r2, _ = lax.optimization_barrier((v_r2, mixed))
    v_s2 = move(v_r2, perm=swap2)
    patch_width = proj_weight.shape[1]
    attended, latent, activated = pl.pallas_call(
        latent_kernel,
        out_shape=(jax.ShapeDtypeStruct((rows, width), jnp.bfloat16), picture, picture),
        in_specs=[VMEM] * 9,
        out_specs=(pl.BlockSpec(memory_space=pl.ANY), VMEM, VMEM),
        scratch_shapes=[
            pltpu.VMEM((rows, width), jnp.bfloat16),
            pltpu.VMEM((rows, patch_width), jnp.float32),
            pltpu.VMEM((patch_width, rows), jnp.float32),
            pltpu.SemaphoreType.DMA,
        ],
        compiler_params=params(),
        name="latent",
        cost_estimate=pl.CostEstimate(
            flops=2 * rows * width * (2 * rows + patch_width),
            bytes_accessed=10 * rows * width * 2 + width * patch_width * 2,
            transcendentals=features.size,
        ),
    )(
        weights, base, inverse, v_r2, v_s2, w_near, place_matrix, features,
        norm_gain.reshape(1, channels),
    )

    halo = move(activated, perm=[(s, s + 1) for s in range(count - 1)])

    moved = [pltpu.VMEM((frames, TAPS * channels, pixels), jnp.bfloat16)]
    conv_cost = pl.CostEstimate(
        flops=2 * channels * TAPS * channels * pixels * 3,
        bytes_accessed=conv_weight.size * 2 + shift_matrix.size * 2,
        transcendentals=0,
    )
    part = pl.pallas_call(
        conv_own_kernel,
        out_shape=jax.ShapeDtypeStruct(features.shape, jnp.float32),
        in_specs=[VMEM] * 3,
        out_specs=VMEM,
        scratch_shapes=moved,
        compiler_params=params(),
        name="conv_own",
        cost_estimate=conv_cost,
    )(activated, shift_matrix, conv_weight)
    decoded = pl.pallas_call(
        conv_halo_kernel,
        out_shape=jax.ShapeDtypeStruct(features.shape, jnp.bfloat16),
        in_specs=[VMEM] * 5,
        out_specs=VMEM,
        scratch_shapes=moved + [pltpu.VMEM(features.shape, jnp.float32)],
        compiler_params=params(),
        name="conv_halo",
        cost_estimate=conv_cost,
    )(halo, shift_matrix, conv_weight, part, latent)
    return (attended, decoded)


def solution(mesh):
    placed = (
        P(("groups", "span"), None),
        P(("groups", "span"), None),
        P(("groups", "span"), None),
        P(("groups", "span")),
        P(),
        P(("groups", "span"), None, None),
        P(),
        P(),
    )
    return jax.shard_map(
        shards,
        mesh=mesh,
        in_specs=placed,
        out_specs=(P(("groups", "span"), None), P(("groups", "span"), None, None)),
        check_vma=False,
    )
```

```python
import functools

import jax
import jax.numpy as jnp
import numpy as np
from jax import lax
from jax.experimental import pallas as pl
from jax.experimental.pallas import tpu as pltpu
from jax.sharding import PartitionSpec as P

HEAD_DIM = 128
LOOKBACK = 3
SIDE = 16
PATCH = 2
TAPS = 9
EPS = 1e-06

VMEM = pl.BlockSpec(memory_space=pltpu.VMEM)
SMEM = pl.BlockSpec(memory_space=pltpu.SMEM)


def params():
    return pltpu.CompilerParams(vmem_limit_bytes=16 * 1024 * 1024)


def one_hot_kernel(w_far, place_ref, shift_ref, w_near, sem):
    copy = pltpu.make_async_copy(w_far, w_near, sem)
    copy.start()
    half = SIDE // PATCH
    patches = half * half
    pixels = SIDE * SIDE
    tokens = place_ref.shape[0] // (PATCH * PATCH)
    column = lax.broadcasted_iota(jnp.int32, (tokens, place_ref.shape[1]), 1)
    pixel = column % pixels
    row, col = pixel // SIDE, pixel % SIDE
    token = column // pixels * patches + row // PATCH * half + col // PATCH
    corner = row % PATCH * PATCH + col % PATCH
    hit = lax.broadcasted_iota(jnp.int32, token.shape, 0) == token
    for k in range(PATCH * PATCH):
        place_ref[pl.ds(k * tokens, tokens), :] = jnp.where(
            hit & (corner == k), 1.0, 0.0
        ).astype(jnp.bfloat16)
    source = lax.broadcasted_iota(jnp.int32, (pixels, pixels), 0)
    target = lax.broadcasted_iota(jnp.int32, (pixels, pixels), 1)
    for k, e in enumerate((-1, 1)):
        col = target % SIDE + e
        shift_ref[:, k * pixels : (k + 1) * pixels] = jnp.where(
            (col >= 0) & (col < SIDE) & (source == target + e), 1.0, 0.0
        ).astype(jnp.bfloat16)
    copy.wait()


UNSEEN = LOOKBACK + 1
DISTANCES = ((0, UNSEEN, 3, 2, 1), (0, 1, UNSEEN, 2, 3), (0, 2, 3, UNSEEN, 1), (0, 1, 3, 2, UNSEEN))
RATE = float(np.log2(np.e) * HEAD_DIM**-0.5)


def biases(lookback):
    place = lax.rem(lax.axis_index("span"), 4)
    out = []
    for ways in zip(*DISTANCES):
        distance = ways[0]
        for k, way in enumerate(ways[1:], 1):
            distance = jnp.where(place == k, way, distance)
        out.append(jnp.where(distance <= lookback[0], 0.0, -jnp.inf).astype(jnp.float32))
    return out


def head(h):
    return slice(h * HEAD_DIM, (h + 1) * HEAD_DIM)


def staged(heads, *stages):
    held = {}
    for step in range(heads + len(stages) - 1):
        for i, stage in enumerate(stages):
            h = step - i
            if 0 <= h < heads:
                held[h] = stage(h, held.get(h))


def scores_of(q_ref, blocks, biases, h):
    keys = jnp.concatenate(blocks, axis=0)
    s = lax.dot_general(
        q_ref[:, head(h)], keys, (((1,), (1,)), ((), ())), preferred_element_type=jnp.float32
    )
    rows = blocks[0].shape[0]
    parts = [s[:, i * rows : (i + 1) * rows] for i in range(len(blocks))]
    return [part if bias is None else part + bias for part, bias in zip(parts, biases)]


def top_of(parts):
    return jnp.max(functools.reduce(jnp.maximum, parts), axis=1, keepdims=True)


def early_kernel(
    lookback, q_ref, k0, k_hop, k_own, k2, v0, v_hop, v_own, v2, mixed_ref, top_ref, total_ref
):
    rows = q_ref.shape[0]
    bias = biases(lookback)
    hopped = lax.rem(lax.axis_index("span"), 2) == 0
    ones = jnp.ones((3 * rows, HEAD_DIM), jnp.bfloat16)

    def score(h, _):
        k1 = jnp.where(hopped, k_hop[:, head(h)], k_own[:, head(h)])
        keys = (k0[:, head(h)], k1, k2[:, head(h)])
        return scores_of(q_ref, keys, (None, bias[1], bias[2]), h)

    def soften(h, parts):
        top = top_of(parts)
        top_ref[:, head(h)] = jnp.broadcast_to(top, (rows, HEAD_DIM))
        probs = [jnp.exp2((part - top) * RATE).astype(jnp.bfloat16) for part in parts]
        return jnp.concatenate(probs, axis=1)

    def blend(h, probs):
        v1 = jnp.where(hopped, v_hop[:, head(h)], v_own[:, head(h)])
        values = jnp.concatenate([v0[:, head(h)], v1, v2[:, head(h)]], axis=0)
        both = jnp.dot(
            probs, jnp.concatenate([values, ones], axis=1), preferred_element_type=jnp.float32
        )
        mixed_ref[:, head(h)] = both[:, :HEAD_DIM]
        total_ref[:, head(h)] = both[:, HEAD_DIM:]

    staged(q_ref.shape[1] // HEAD_DIM, score, soften, blend)


def late_kernel(
    lookback, q_ref, k1, k2, mixed_ref, top_ref, total_ref, p_ref, base_ref, inverse_ref
):
    rows = q_ref.shape[0]
    ones = jnp.ones((2 * rows, HEAD_DIM), jnp.bfloat16)
    bias = biases(lookback)

    def score(h, _):
        return scores_of(q_ref, (k1[:, head(h)], k2[:, head(h)]), (bias[3], bias[4]), h)

    def soften(h, parts):
        before = top_ref[:, head(h)]
        top = jnp.maximum(before, top_of(parts))
        probs = [jnp.exp2((part - top) * RATE).astype(jnp.bfloat16) for part in parts]
        probs = jnp.concatenate(probs, axis=1)
        p_ref[h] = probs
        return probs, jnp.exp2((before - top) * RATE)

    def settle(h, held):
        probs, shrink = held
        total = jnp.dot(probs, ones, preferred_element_type=jnp.float32)
        inverse = 1.0 / (total + total_ref[:, head(h)] * shrink)
        inverse_ref[:, head(h)] = inverse
        base_ref[:, head(h)] = mixed_ref[:, head(h)] * (shrink * inverse)

    staged(q_ref.shape[1] // HEAD_DIM, score, soften, settle)


def latent_kernel(
    p_ref, base_ref, inverse_ref, v1, v2, w_ref, place_ref, features_ref, gain_ref,
    out_ref, latent_ref, act_ref, mine, turned, sem,
):
    frames, channels, pixels = features_ref.shape

    heads = mine.shape[1] // HEAD_DIM
    projected = 0.0
    for part in (range(heads // 2), range(heads // 2, heads)):

        def blend(i, _):
            h = part[i]
            values = jnp.concatenate([v1[:, head(h)], v2[:, head(h)]], axis=0)
            return jnp.dot(p_ref[h], values, preferred_element_type=jnp.float32)

        def settle(i, late):
            h = part[i]
            late = base_ref[:, head(h)] + late * inverse_ref[:, head(h)]
            mine[:, head(h)] = late.astype(jnp.bfloat16)

        staged(len(part), blend, settle)
        cols = slice(part[0] * HEAD_DIM, (part[-1] + 1) * HEAD_DIM)
        projected += jnp.dot(mine[:, cols], w_ref[cols, :], preferred_element_type=jnp.float32)
    copy = pltpu.make_async_copy(mine, out_ref, sem)
    copy.start()
    turned[...] = projected.T
    parts = [turned[pl.ds(k, channels, stride=4), :] for k in range(4)]
    mixed = jnp.concatenate(parts, axis=1)
    high = mixed.astype(jnp.bfloat16)
    low = (mixed - high.astype(jnp.float32)).astype(jnp.bfloat16)
    placed = jnp.dot(high, place_ref[...], preferred_element_type=jnp.float32)
    placed += jnp.dot(low, place_ref[...], preferred_element_type=jnp.float32)
    gain = jnp.broadcast_to(gain_ref[...], (8, channels)).T[:, :1]
    for f in range(frames):
        latent = features_ref[f].astype(jnp.float32) + placed[:, f * pixels : (f + 1) * pixels]
        latent = latent.astype(jnp.bfloat16)
        latent_ref[f] = latent
        data = latent.astype(jnp.float32)
        mean_square = jnp.mean(data * data, axis=0, keepdims=True)
        normed = data * lax.rsqrt(mean_square + EPS) * gain
        act_ref[f] = (normed / (1.0 + jnp.exp(-normed))).astype(jnp.bfloat16)
    copy.wait()


def spread(act, shift_ref, moved):
    channels, pixels = act.shape
    lane = lax.broadcasted_iota(jnp.int32, act.shape, 1)
    for e in range(3):
        if e == 1:
            middle = act.astype(jnp.float32)
        else:
            side = shift_ref[:, e // 2 * pixels : (e // 2 + 1) * pixels]
            middle = jnp.dot(act, side, preferred_element_type=jnp.float32)
        above = jnp.where(lane >= SIDE, pltpu.roll(middle, SIDE, 1), 0.0)
        below = jnp.where(lane < pixels - SIDE, pltpu.roll(middle, pixels - SIDE, 1), 0.0)
        for b, part in enumerate((above, middle, below)):
            moved[pl.ds((3 * b + e) * channels, channels), :] = part.astype(jnp.bfloat16)


def tap_dot(w_ref, lag, moved):
    channels = w_ref.shape[2]
    return sum(
        jnp.dot(
            w_ref[lag * TAPS + tap], moved[pl.ds(tap * channels, channels), :],
            preferred_element_type=jnp.float32,
        )
        for tap in range(TAPS)
    )


def conv_own_kernel(act_ref, shift_ref, w_ref, part_ref, moved0, moved1):
    spread(act_ref[0], shift_ref, moved0)
    spread(act_ref[1], shift_ref, moved1)
    part_ref[0] = tap_dot(w_ref, 2, moved0)
    part_ref[1] = tap_dot(w_ref, 1, moved0) + tap_dot(w_ref, 2, moved1)


def conv_halo_kernel(halo_ref, shift_ref, w_ref, part_ref, latent_ref, out_ref, moved0, moved1):
    spread(halo_ref[0], shift_ref, moved0)
    spread(halo_ref[1], shift_ref, moved1)
    first = part_ref[0] + tap_dot(w_ref, 0, moved0) + tap_dot(w_ref, 1, moved1)
    second = part_ref[1] + tap_dot(w_ref, 0, moved1)
    out_ref[0] = (latent_ref[0].astype(jnp.float32) + first).astype(jnp.bfloat16)
    out_ref[1] = (latent_ref[1].astype(jnp.float32) + second).astype(jnp.bfloat16)


def routes(count):
    own, hop1, swap1, hop2, swap2 = [], [], [], [], []
    for s in range(count):
        r, first, last = s % 4, s < 4, s + 4 >= count
        if r == 0:
            own.append((s, s + 1))
            hop1.append((s, s + 2))
            if not last:
                hop2.append((s, s + 4))
            if not first:
                swap2.append((s, s + 1))
        elif r == 1:
            if not last:
                hop1.append((s, s + 4))
            hop2.append((s, s + 2))
            if not first:
                swap1.append((s, s - 1))
                swap2.append((s, s - 1))
        elif r == 2:
            own.append((s, s + 1))
            if not last:
                hop1.append((s, s - 2))
            swap1.append((s, s + 1))
        else:
            if not last:
                hop1.append((s, s + 4))
            if not first:
                swap1.append((s, s - 1))
                hop2.append((s, s - 2))
            swap2.append((s, s - 1))
    return own, hop1, swap1, hop2, swap2


def shards(queries, keys, values, lookback, proj_weight, features, norm_gain, conv_weight):
    count = lax.axis_size("span")
    me = lax.axis_index("span")
    second = lax.rem(me, 4) == 1
    second, keys, values = lax.optimization_barrier((second, keys, values))
    own, hop1, swap1, hop2, swap2 = routes(count)
    move = functools.partial(lax.ppermute, axis_name="span")

    rows, width = queries.shape
    heads = width // HEAD_DIM
    frames, channels, pixels = features.shape

    block = jax.ShapeDtypeStruct((rows, width), jnp.float32)
    picture = jax.ShapeDtypeStruct(features.shape, jnp.bfloat16)

    k_r1 = move(keys, perm=hop1)
    k_s0 = move(keys, perm=own)
    v_r1 = move(values, perm=hop1)
    v_s0 = move(values, perm=own)

    tokens = frames * pixels // (PATCH * PATCH)
    place_matrix, shift_matrix, w_near = pl.pallas_call(
        one_hot_kernel,
        out_shape=(
            jax.ShapeDtypeStruct((PATCH * PATCH * tokens, frames * pixels), jnp.bfloat16),
            jax.ShapeDtypeStruct((pixels, 2 * pixels), jnp.bfloat16),
            jax.ShapeDtypeStruct(proj_weight.shape, jnp.bfloat16),
        ),
        in_specs=[pl.BlockSpec(memory_space=pl.ANY)],
        out_specs=(VMEM,) * 3,
        scratch_shapes=[pltpu.SemaphoreType.DMA],
        compiler_params=params(),
        name="one_hot",
    )(proj_weight)
    k_r1, place_matrix, shift_matrix, w_near = lax.optimization_barrier(
        (k_r1, place_matrix, shift_matrix, w_near)
    )

    k_r2 = move(jnp.where(second, keys, k_r1), perm=hop2)
    k_s1 = move(k_r1, perm=swap1)
    v_hop = jnp.where(second, values, v_r1)
    v_r2 = move(v_hop, perm=hop2)
    v_s1 = move(v_r1, perm=swap1)

    mixed, top, total = pl.pallas_call(
        early_kernel,
        out_shape=(block,) * 3,
        in_specs=[SMEM] + [VMEM] * 9,
        out_specs=(VMEM,) * 3,
        compiler_params=params(),
        name="early",
        cost_estimate=pl.CostEstimate(
            flops=12 * rows * rows * width,
            bytes_accessed=9 * rows * width * 2,
            transcendentals=3 * heads * rows * rows,
        ),
    )(
        lookback, queries, keys, k_r1, k_s0, k_s1, values, v_r1, v_s0, v_s1,
    )

    k_s2 = move(k_r2, perm=swap2)
    weights, base, inverse = pl.pallas_call(
        late_kernel,
        out_shape=(
            jax.ShapeDtypeStruct((heads, rows, 2 * rows), jnp.bfloat16), block, block,
        ),
        in_specs=[SMEM] + [VMEM] * 6,
        out_specs=(VMEM,) * 3,
        compiler_params=params(),
        name="late",
        cost_estimate=pl.CostEstimate(
            flops=4 * rows * rows * width,
            bytes_accessed=9 * rows * width * 2,
            transcendentals=2 * heads * rows * rows,
        ),
    )(lookback, queries, k_r2, k_s2, mixed, top, total)

    v_r2, _ = lax.optimization_barrier((v_r2, mixed))
    v_s2 = move(v_r2, perm=swap2)
    patch_width = proj_weight.shape[1]
    attended, latent, activated = pl.pallas_call(
        latent_kernel,
        out_shape=(jax.ShapeDtypeStruct((rows, width), jnp.bfloat16), picture, picture),
        in_specs=[VMEM] * 9,
        out_specs=(pl.BlockSpec(memory_space=pl.ANY), VMEM, VMEM),
        scratch_shapes=[
            pltpu.VMEM((rows, width), jnp.bfloat16),
            pltpu.VMEM((patch_width, rows), jnp.float32),
            pltpu.SemaphoreType.DMA,
        ],
        compiler_params=params(),
        name="latent",
        cost_estimate=pl.CostEstimate(
            flops=2 * rows * width * (2 * rows + patch_width),
            bytes_accessed=10 * rows * width * 2 + width * patch_width * 2,
            transcendentals=features.size,
        ),
    )(
        weights, base, inverse, v_r2, v_s2, w_near, place_matrix, features,
        norm_gain.reshape(1, channels),
    )

    halo = move(activated, perm=[(s, s + 1) for s in range(count - 1)])

    moved = [pltpu.VMEM((TAPS * channels, pixels), jnp.bfloat16)] * 2
    conv_cost = pl.CostEstimate(
        flops=2 * channels * TAPS * channels * pixels * 3,
        bytes_accessed=conv_weight.size * 2 + shift_matrix.size * 2,
        transcendentals=0,
    )
    part = pl.pallas_call(
        conv_own_kernel,
        out_shape=jax.ShapeDtypeStruct(features.shape, jnp.float32),
        in_specs=[VMEM] * 3,
        out_specs=VMEM,
        scratch_shapes=moved,
        compiler_params=params(),
        name="conv_own",
        cost_estimate=conv_cost,
    )(activated, shift_matrix, conv_weight)
    decoded = pl.pallas_call(
        conv_halo_kernel,
        out_shape=jax.ShapeDtypeStruct(features.shape, jnp.bfloat16),
        in_specs=[VMEM] * 5,
        out_specs=VMEM,
        scratch_shapes=moved,
        compiler_params=params(),
        name="conv_halo",
        cost_estimate=conv_cost,
    )(halo, shift_matrix, conv_weight, part, latent)
    return (attended, decoded)


def solution(mesh):
    placed = (
        P(("groups", "span"), None),
        P(("groups", "span"), None),
        P(("groups", "span"), None),
        P(("groups", "span")),
        P(),
        P(("groups", "span"), None, None),
        P(),
        P(),
    )
    return jax.shard_map(
        shards,
        mesh=mesh,
        in_specs=placed,
        out_specs=(P(("groups", "span"), None), P(("groups", "span"), None, None)),
        check_vma=False,
    )
```

```python
import functools

import jax
import jax.numpy as jnp
import numpy as np
from jax import lax
from jax.experimental import pallas as pl
from jax.experimental.pallas import tpu as pltpu
from jax.sharding import PartitionSpec as P

HEAD_DIM = 128
LOOKBACK = 3
SIDE = 16
PATCH = 2
TAPS = 9
EPS = 1e-06

VMEM = pl.BlockSpec(memory_space=pltpu.VMEM)
SMEM = pl.BlockSpec(memory_space=pltpu.SMEM)


def params():
    return pltpu.CompilerParams(vmem_limit_bytes=16 * 1024 * 1024)


def one_hot_kernel(w_far, place_ref, shift_ref, w_near, sem):
    copy = pltpu.make_async_copy(w_far, w_near, sem)
    copy.start()
    half = SIDE // PATCH
    patches = half * half
    pixels = SIDE * SIDE
    tokens = place_ref.shape[0] // (PATCH * PATCH)
    column = lax.broadcasted_iota(jnp.int32, (tokens, place_ref.shape[1]), 1)
    pixel = column % pixels
    row, col = pixel // SIDE, pixel % SIDE
    token = column // pixels * patches + row // PATCH * half + col // PATCH
    corner = row % PATCH * PATCH + col % PATCH
    hit = lax.broadcasted_iota(jnp.int32, token.shape, 0) == token
    for k in range(PATCH * PATCH):
        place_ref[pl.ds(k * tokens, tokens), :] = jnp.where(
            hit & (corner == k), 1.0, 0.0
        ).astype(jnp.bfloat16)
    source = lax.broadcasted_iota(jnp.int32, (pixels, pixels), 0)
    target = lax.broadcasted_iota(jnp.int32, (pixels, pixels), 1)
    for k, e in enumerate((-1, 1)):
        col = target % SIDE + e
        shift_ref[:, k * pixels : (k + 1) * pixels] = jnp.where(
            (col >= 0) & (col < SIDE) & (source == target + e), 1.0, 0.0
        ).astype(jnp.bfloat16)
    copy.wait()


UNSEEN = LOOKBACK + 1
DISTANCES = ((0, UNSEEN, 3, 2, 1), (0, 1, UNSEEN, 2, 3), (0, 2, 3, UNSEEN, 1), (0, 1, 3, 2, UNSEEN))
RATE = float(np.log2(np.e) * HEAD_DIM**-0.5)


def biases(lookback):
    place = lax.rem(lax.axis_index("span"), 4)
    out = []
    for ways in zip(*DISTANCES):
        distance = ways[0]
        for k, way in enumerate(ways[1:], 1):
            distance = jnp.where(place == k, way, distance)
        out.append(jnp.where(distance <= lookback[0], 0.0, -jnp.inf).astype(jnp.float32))
    return out


def head(h):
    return slice(h * HEAD_DIM, (h + 1) * HEAD_DIM)


def staged(heads, *stages):
    held = {}
    for step in range(heads + len(stages) - 1):
        for i, stage in enumerate(stages):
            h = step - i
            if 0 <= h < heads:
                held[h] = stage(h, held.get(h))


def scores_of(q_ref, blocks, biases, h):
    keys = jnp.concatenate(blocks, axis=0)
    s = lax.dot_general(
        q_ref[:, head(h)], keys, (((1,), (1,)), ((), ())), preferred_element_type=jnp.float32
    )
    rows = blocks[0].shape[0]
    parts = [s[:, i * rows : (i + 1) * rows] for i in range(len(blocks))]
    return [part if bias is None else part + bias for part, bias in zip(parts, biases)]


def top_of(parts):
    return jnp.max(functools.reduce(jnp.maximum, parts), axis=1, keepdims=True)


def early_kernel(
    lookback, q_ref, k0, k_hop, k_own, k2, v0, v_hop, v_own, v2, mixed_ref, top_ref, total_ref
):
    rows = q_ref.shape[0]
    bias = biases(lookback)
    hopped = lax.rem(lax.axis_index("span"), 2) == 0
    ones = jnp.ones((3 * rows, HEAD_DIM), jnp.bfloat16)

    def score(h, _):
        k1 = jnp.where(hopped, k_hop[:, head(h)], k_own[:, head(h)])
        keys = (k0[:, head(h)], k1, k2[:, head(h)])
        return scores_of(q_ref, keys, (None, bias[1], bias[2]), h)

    def soften(h, parts):
        top = top_of(parts)
        top_ref[:, head(h)] = jnp.broadcast_to(top, (rows, HEAD_DIM))
        probs = [jnp.exp2((part - top) * RATE).astype(jnp.bfloat16) for part in parts]
        return jnp.concatenate(probs, axis=1)

    def blend(h, probs):
        v1 = jnp.where(hopped, v_hop[:, head(h)], v_own[:, head(h)])
        values = jnp.concatenate([v0[:, head(h)], v1, v2[:, head(h)]], axis=0)
        both = jnp.dot(
            probs, jnp.concatenate([values, ones], axis=1), preferred_element_type=jnp.float32
        )
        mixed_ref[:, head(h)] = both[:, :HEAD_DIM]
        total_ref[:, head(h)] = both[:, HEAD_DIM:]

    staged(q_ref.shape[1] // HEAD_DIM, score, soften, blend)


def late_kernel(
    lookback, q_ref, k1, k2, mixed_ref, top_ref, total_ref, p_ref, base_ref, inverse_ref
):
    rows = q_ref.shape[0]
    ones = jnp.ones((2 * rows, HEAD_DIM), jnp.bfloat16)
    bias = biases(lookback)

    def score(h, _):
        return scores_of(q_ref, (k1[:, head(h)], k2[:, head(h)]), (bias[3], bias[4]), h)

    def soften(h, parts):
        before = top_ref[:, head(h)]
        top = jnp.maximum(before, top_of(parts))
        probs = [jnp.exp2((part - top) * RATE).astype(jnp.bfloat16) for part in parts]
        probs = jnp.concatenate(probs, axis=1)
        p_ref[h] = probs
        return probs, jnp.exp2((before - top) * RATE)

    def settle(h, held):
        probs, shrink = held
        total = jnp.dot(probs, ones, preferred_element_type=jnp.float32)
        inverse = 1.0 / (total + total_ref[:, head(h)] * shrink)
        inverse_ref[:, head(h)] = inverse
        base_ref[:, head(h)] = mixed_ref[:, head(h)] * (shrink * inverse)

    staged(q_ref.shape[1] // HEAD_DIM, score, soften, settle)


def latent_kernel(
    p_ref, base_ref, inverse_ref, v1, v2, w_ref, place_ref, features_ref, gain_ref,
    out_ref, latent_ref, act_ref, mine, turned, sem,
):
    frames, channels, pixels = features_ref.shape

    heads = mine.shape[1] // HEAD_DIM
    group = 4

    def blend(g, _):
        late = []
        for h in range(g * group, (g + 1) * group):
            values = jnp.concatenate([v1[:, head(h)], v2[:, head(h)]], axis=0)
            late.append(jnp.dot(p_ref[h], values, preferred_element_type=jnp.float32))
        return late

    def settle(g, late):
        for h, part in zip(range(g * group, (g + 1) * group), late):
            part = base_ref[:, head(h)] + part * inverse_ref[:, head(h)]
            mine[:, head(h)] = part.astype(jnp.bfloat16)

    def project(g, _):
        cols = slice(g * group * HEAD_DIM, (g + 1) * group * HEAD_DIM)
        part = jnp.dot(mine[:, cols], w_ref[cols, :], preferred_element_type=jnp.float32)
        products.append(part if not products else products.pop() + part)

    products = []
    staged(heads // group, blend, settle, project)
    copy = pltpu.make_async_copy(mine, out_ref, sem)
    copy.start()
    projected = products[0]
    turned[...] = projected.T
    parts = [turned[pl.ds(k, channels, stride=4), :] for k in range(4)]
    mixed = jnp.concatenate(parts, axis=1)
    high = mixed.astype(jnp.bfloat16)
    low = (mixed - high.astype(jnp.float32)).astype(jnp.bfloat16)
    placed = jnp.dot(high, place_ref[...], preferred_element_type=jnp.float32)
    placed += jnp.dot(low, place_ref[...], preferred_element_type=jnp.float32)
    gain = jnp.broadcast_to(gain_ref[...], (8, channels)).T[:, :1]
    for f in range(frames):
        latent = features_ref[f].astype(jnp.float32) + placed[:, f * pixels : (f + 1) * pixels]
        latent = latent.astype(jnp.bfloat16)
        latent_ref[f] = latent
        data = latent.astype(jnp.float32)
        mean_square = jnp.mean(data * data, axis=0, keepdims=True)
        normed = data * lax.rsqrt(mean_square + EPS) * gain
        act_ref[f] = (normed / (1.0 + jnp.exp(-normed))).astype(jnp.bfloat16)
    copy.wait()


def spread(act, shift_ref, moved):
    channels, pixels = act.shape
    lane = lax.broadcasted_iota(jnp.int32, act.shape, 1)
    for e in range(3):
        if e == 1:
            middle = act.astype(jnp.float32)
        else:
            side = shift_ref[:, e // 2 * pixels : (e // 2 + 1) * pixels]
            middle = jnp.dot(act, side, preferred_element_type=jnp.float32)
        above = jnp.where(lane >= SIDE, pltpu.roll(middle, SIDE, 1), 0.0)
        below = jnp.where(lane < pixels - SIDE, pltpu.roll(middle, pixels - SIDE, 1), 0.0)
        for b, part in enumerate((above, middle, below)):
            moved[pl.ds((3 * b + e) * channels, channels), :] = part.astype(jnp.bfloat16)


def tap_dot(w_ref, lag, moved):
    channels = w_ref.shape[2]
    return sum(
        jnp.dot(
            w_ref[lag * TAPS + tap], moved[pl.ds(tap * channels, channels), :],
            preferred_element_type=jnp.float32,
        )
        for tap in range(TAPS)
    )


def conv_own_kernel(act_ref, shift_ref, w_ref, part_ref, moved0, moved1):
    spread(act_ref[0], shift_ref, moved0)
    spread(act_ref[1], shift_ref, moved1)
    part_ref[0] = tap_dot(w_ref, 2, moved0)
    part_ref[1] = tap_dot(w_ref, 1, moved0) + tap_dot(w_ref, 2, moved1)


def conv_halo_kernel(halo_ref, shift_ref, w_ref, part_ref, latent_ref, out_ref, moved0, moved1):
    spread(halo_ref[0], shift_ref, moved0)
    spread(halo_ref[1], shift_ref, moved1)
    first = part_ref[0] + tap_dot(w_ref, 0, moved0) + tap_dot(w_ref, 1, moved1)
    second = part_ref[1] + tap_dot(w_ref, 0, moved1)
    out_ref[0] = (latent_ref[0].astype(jnp.float32) + first).astype(jnp.bfloat16)
    out_ref[1] = (latent_ref[1].astype(jnp.float32) + second).astype(jnp.bfloat16)


def routes(count):
    own, hop1, swap1, hop2, swap2 = [], [], [], [], []
    for s in range(count):
        r, first, last = s % 4, s < 4, s + 4 >= count
        if r == 0:
            own.append((s, s + 1))
            hop1.append((s, s + 2))
            if not last:
                hop2.append((s, s + 4))
            if not first:
                swap2.append((s, s + 1))
        elif r == 1:
            if not last:
                hop1.append((s, s + 4))
            hop2.append((s, s + 2))
            if not first:
                swap1.append((s, s - 1))
                swap2.append((s, s - 1))
        elif r == 2:
            own.append((s, s + 1))
            if not last:
                hop1.append((s, s - 2))
            swap1.append((s, s + 1))
        else:
            if not last:
                hop1.append((s, s + 4))
            if not first:
                swap1.append((s, s - 1))
                hop2.append((s, s - 2))
            swap2.append((s, s - 1))
    return own, hop1, swap1, hop2, swap2


def shards(queries, keys, values, lookback, proj_weight, features, norm_gain, conv_weight):
    count = lax.axis_size("span")
    me = lax.axis_index("span")
    second = lax.rem(me, 4) == 1
    second, keys, values = lax.optimization_barrier((second, keys, values))
    own, hop1, swap1, hop2, swap2 = routes(count)
    move = functools.partial(lax.ppermute, axis_name="span")

    rows, width = queries.shape
    heads = width // HEAD_DIM
    frames, channels, pixels = features.shape

    block = jax.ShapeDtypeStruct((rows, width), jnp.float32)
    picture = jax.ShapeDtypeStruct(features.shape, jnp.bfloat16)

    k_r1 = move(keys, perm=hop1)
    k_s0 = move(keys, perm=own)
    v_r1 = move(values, perm=hop1)
    v_s0 = move(values, perm=own)

    tokens = frames * pixels // (PATCH * PATCH)
    place_matrix, shift_matrix, w_near = pl.pallas_call(
        one_hot_kernel,
        out_shape=(
            jax.ShapeDtypeStruct((PATCH * PATCH * tokens, frames * pixels), jnp.bfloat16),
            jax.ShapeDtypeStruct((pixels, 2 * pixels), jnp.bfloat16),
            jax.ShapeDtypeStruct(proj_weight.shape, jnp.bfloat16),
        ),
        in_specs=[pl.BlockSpec(memory_space=pl.ANY)],
        out_specs=(VMEM,) * 3,
        scratch_shapes=[pltpu.SemaphoreType.DMA],
        compiler_params=params(),
        name="one_hot",
    )(proj_weight)
    k_r1, place_matrix, shift_matrix, w_near = lax.optimization_barrier(
        (k_r1, place_matrix, shift_matrix, w_near)
    )

    k_r2 = move(jnp.where(second, keys, k_r1), perm=hop2)
    k_s1 = move(k_r1, perm=swap1)
    v_hop = jnp.where(second, values, v_r1)
    v_r2 = move(v_hop, perm=hop2)
    v_s1 = move(v_r1, perm=swap1)

    mixed, top, total = pl.pallas_call(
        early_kernel,
        out_shape=(block,) * 3,
        in_specs=[SMEM] + [VMEM] * 9,
        out_specs=(VMEM,) * 3,
        compiler_params=params(),
        name="early",
        cost_estimate=pl.CostEstimate(
            flops=12 * rows * rows * width,
            bytes_accessed=9 * rows * width * 2,
            transcendentals=3 * heads * rows * rows,
        ),
    )(
        lookback, queries, keys, k_r1, k_s0, k_s1, values, v_r1, v_s0, v_s1,
    )

    k_s2 = move(k_r2, perm=swap2)
    weights, base, inverse = pl.pallas_call(
        late_kernel,
        out_shape=(
            jax.ShapeDtypeStruct((heads, rows, 2 * rows), jnp.bfloat16), block, block,
        ),
        in_specs=[SMEM] + [VMEM] * 6,
        out_specs=(VMEM,) * 3,
        compiler_params=params(),
        name="late",
        cost_estimate=pl.CostEstimate(
            flops=4 * rows * rows * width,
            bytes_accessed=9 * rows * width * 2,
            transcendentals=2 * heads * rows * rows,
        ),
    )(lookback, queries, k_r2, k_s2, mixed, top, total)

    v_r2, _ = lax.optimization_barrier((v_r2, mixed))
    v_s2 = move(v_r2, perm=swap2)
    patch_width = proj_weight.shape[1]
    attended, latent, activated = pl.pallas_call(
        latent_kernel,
        out_shape=(jax.ShapeDtypeStruct((rows, width), jnp.bfloat16), picture, picture),
        in_specs=[VMEM] * 9,
        out_specs=(pl.BlockSpec(memory_space=pl.ANY), VMEM, VMEM),
        scratch_shapes=[
            pltpu.VMEM((rows, width), jnp.bfloat16),
            pltpu.VMEM((patch_width, rows), jnp.float32),
            pltpu.SemaphoreType.DMA,
        ],
        compiler_params=params(),
        name="latent",
        cost_estimate=pl.CostEstimate(
            flops=2 * rows * width * (2 * rows + patch_width),
            bytes_accessed=10 * rows * width * 2 + width * patch_width * 2,
            transcendentals=features.size,
        ),
    )(
        weights, base, inverse, v_r2, v_s2, w_near, place_matrix, features,
        norm_gain.reshape(1, channels),
    )

    halo = move(activated, perm=[(s, s + 1) for s in range(count - 1)])

    moved = [pltpu.VMEM((TAPS * channels, pixels), jnp.bfloat16)] * 2
    conv_cost = pl.CostEstimate(
        flops=2 * channels * TAPS * channels * pixels * 3,
        bytes_accessed=conv_weight.size * 2 + shift_matrix.size * 2,
        transcendentals=0,
    )
    part = pl.pallas_call(
        conv_own_kernel,
        out_shape=jax.ShapeDtypeStruct(features.shape, jnp.float32),
        in_specs=[VMEM] * 3,
        out_specs=VMEM,
        scratch_shapes=moved,
        compiler_params=params(),
        name="conv_own",
        cost_estimate=conv_cost,
    )(activated, shift_matrix, conv_weight)
    decoded = pl.pallas_call(
        conv_halo_kernel,
        out_shape=jax.ShapeDtypeStruct(features.shape, jnp.bfloat16),
        in_specs=[VMEM] * 5,
        out_specs=VMEM,
        scratch_shapes=moved,
        compiler_params=params(),
        name="conv_halo",
        cost_estimate=conv_cost,
    )(halo, shift_matrix, conv_weight, part, latent)
    return (attended, decoded)


def solution(mesh):
    placed = (
        P(("groups", "span"), None),
        P(("groups", "span"), None),
        P(("groups", "span"), None),
        P(("groups", "span")),
        P(),
        P(("groups", "span"), None, None),
        P(),
        P(),
    )
    return jax.shard_map(
        shards,
        mesh=mesh,
        in_specs=placed,
        out_specs=(P(("groups", "span"), None), P(("groups", "span"), None, None)),
        check_vma=False,
    )
```

```python
import functools

import jax
import jax.numpy as jnp
import numpy as np
from jax import lax
from jax.experimental import pallas as pl
from jax.experimental.pallas import tpu as pltpu
from jax.sharding import PartitionSpec as P

HEAD_DIM = 128
LOOKBACK = 3
SIDE = 16
PATCH = 2
TAPS = 9
EPS = 1e-06

VMEM = pl.BlockSpec(memory_space=pltpu.VMEM)
SMEM = pl.BlockSpec(memory_space=pltpu.SMEM)


def params():
    return pltpu.CompilerParams(vmem_limit_bytes=16 * 1024 * 1024)


def one_hot_kernel(w_far, place_ref, shift_ref, w_near, sem):
    copy = pltpu.make_async_copy(w_far, w_near, sem)
    copy.start()
    half = SIDE // PATCH
    patches = half * half
    pixels = SIDE * SIDE
    tokens = place_ref.shape[0] // (PATCH * PATCH)
    column = lax.broadcasted_iota(jnp.int32, (tokens, place_ref.shape[1]), 1)
    pixel = column % pixels
    row, col = pixel // SIDE, pixel % SIDE
    token = column // pixels * patches + row // PATCH * half + col // PATCH
    corner = row % PATCH * PATCH + col % PATCH
    hit = lax.broadcasted_iota(jnp.int32, token.shape, 0) == token
    for k in range(PATCH * PATCH):
        place_ref[pl.ds(k * tokens, tokens), :] = jnp.where(
            hit & (corner == k), 1.0, 0.0
        ).astype(jnp.bfloat16)
    source = lax.broadcasted_iota(jnp.int32, (pixels, pixels), 0)
    target = lax.broadcasted_iota(jnp.int32, (pixels, pixels), 1)
    for k, e in enumerate((-1, 1)):
        col = target % SIDE + e
        shift_ref[:, k * pixels : (k + 1) * pixels] = jnp.where(
            (col >= 0) & (col < SIDE) & (source == target + e), 1.0, 0.0
        ).astype(jnp.bfloat16)
    copy.wait()


UNSEEN = LOOKBACK + 1
DISTANCES = ((0, UNSEEN, 3, 2, 1), (0, 1, UNSEEN, 2, 3), (0, 2, 3, UNSEEN, 1), (0, 1, 3, 2, UNSEEN))
RATE = float(np.log2(np.e) * HEAD_DIM**-0.5)


def biases(lookback):
    place = lax.rem(lax.axis_index("span"), 4)
    out = []
    for ways in zip(*DISTANCES):
        distance = ways[0]
        for k, way in enumerate(ways[1:], 1):
            distance = jnp.where(place == k, way, distance)
        out.append(jnp.where(distance <= lookback[0], 0.0, -jnp.inf).astype(jnp.float32))
    return out


def head(h):
    return slice(h * HEAD_DIM, (h + 1) * HEAD_DIM)


def staged(heads, *stages):
    held = {}
    for step in range(heads + len(stages) - 1):
        for i, stage in enumerate(stages):
            h = step - i
            if 0 <= h < heads:
                held[h] = stage(h, held.get(h))


def scores_of(q_ref, blocks, biases, h):
    keys = jnp.concatenate(blocks, axis=0)
    s = lax.dot_general(
        q_ref[:, head(h)], keys, (((1,), (1,)), ((), ())), preferred_element_type=jnp.float32
    )
    rows = blocks[0].shape[0]
    parts = [s[:, i * rows : (i + 1) * rows] for i in range(len(blocks))]
    return [part if bias is None else part + bias for part, bias in zip(parts, biases)]


def top_of(parts):
    return jnp.max(functools.reduce(jnp.maximum, parts), axis=1, keepdims=True)


def early_kernel(
    lookback, q_ref, k0, k_hop, k_own, k2, v0, v_hop, v_own, v2, mixed_ref, top_ref, total_ref
):
    rows = q_ref.shape[0]
    bias = biases(lookback)
    hopped = lax.rem(lax.axis_index("span"), 2) == 0
    ones = jnp.ones((3 * rows, HEAD_DIM), jnp.bfloat16)

    def score(h, _):
        k1 = jnp.where(hopped, k_hop[:, head(h)], k_own[:, head(h)])
        keys = (k0[:, head(h)], k1, k2[:, head(h)])
        return scores_of(q_ref, keys, (None, bias[1], bias[2]), h)

    def soften(h, parts):
        top = top_of(parts)
        top_ref[:, head(h)] = jnp.broadcast_to(top, (rows, HEAD_DIM))
        probs = [jnp.exp2((part - top) * RATE).astype(jnp.bfloat16) for part in parts]
        return jnp.concatenate(probs, axis=1)

    def blend(h, probs):
        v1 = jnp.where(hopped, v_hop[:, head(h)], v_own[:, head(h)])
        values = jnp.concatenate([v0[:, head(h)], v1, v2[:, head(h)]], axis=0)
        both = jnp.dot(
            probs, jnp.concatenate([values, ones], axis=1), preferred_element_type=jnp.float32
        )
        mixed_ref[:, head(h)] = both[:, :HEAD_DIM]
        total_ref[:, head(h)] = both[:, HEAD_DIM:]

    staged(q_ref.shape[1] // HEAD_DIM, score, soften, blend)


def late_kernel(
    lookback, q_ref, k1, k2, mixed_ref, top_ref, total_ref, p_ref, base_ref, inverse_ref
):
    rows = q_ref.shape[0]
    ones = jnp.ones((2 * rows, HEAD_DIM), jnp.bfloat16)
    bias = biases(lookback)

    def score(h, _):
        return scores_of(q_ref, (k1[:, head(h)], k2[:, head(h)]), (bias[3], bias[4]), h)

    def soften(h, parts):
        before = top_ref[:, head(h)]
        top = jnp.maximum(before, top_of(parts))
        probs = [jnp.exp2((part - top) * RATE).astype(jnp.bfloat16) for part in parts]
        probs = jnp.concatenate(probs, axis=1)
        p_ref[h] = probs
        return probs, jnp.exp2((before - top) * RATE)

    def settle(h, held):
        probs, shrink = held
        total = jnp.dot(probs, ones, preferred_element_type=jnp.float32)
        inverse = 1.0 / (total + total_ref[:, head(h)] * shrink)
        inverse_ref[:, head(h)] = inverse
        base_ref[:, head(h)] = mixed_ref[:, head(h)] * (shrink * inverse)

    staged(q_ref.shape[1] // HEAD_DIM, score, soften, settle)


def latent_kernel(
    p_ref, base_ref, inverse_ref, v1, v2, w_ref, place_ref, features_ref, gain_ref,
    out_ref, latent_ref, act_ref, mine, turned, sem,
):
    frames, channels, pixels = features_ref.shape

    heads = mine.shape[1] // HEAD_DIM
    group = 4

    def blend(g, _):
        late = []
        for h in range(g * group, (g + 1) * group):
            values = jnp.concatenate([v1[:, head(h)], v2[:, head(h)]], axis=0)
            late.append(jnp.dot(p_ref[h], values, preferred_element_type=jnp.float32))
        return late

    def settle(g, late):
        for h, part in zip(range(g * group, (g + 1) * group), late):
            part = base_ref[:, head(h)] + part * inverse_ref[:, head(h)]
            mine[:, head(h)] = part.astype(jnp.bfloat16)

    def project(g, _):
        cols = slice(g * group * HEAD_DIM, (g + 1) * group * HEAD_DIM)
        part = jnp.dot(mine[:, cols], w_ref[cols, :], preferred_element_type=jnp.float32)
        products.append(part if not products else products.pop() + part)

    products = []
    staged(heads // group, blend, settle, project)
    copy = pltpu.make_async_copy(mine, out_ref, sem)
    copy.start()
    projected = products[0]
    turned[...] = projected.T
    parts = [turned[pl.ds(k, channels, stride=4), :] for k in range(4)]
    mixed = jnp.concatenate(parts, axis=1)
    high = mixed.astype(jnp.bfloat16)
    low = (mixed - high.astype(jnp.float32)).astype(jnp.bfloat16)
    placed = jnp.dot(high, place_ref[...], preferred_element_type=jnp.float32)
    placed += jnp.dot(low, place_ref[...], preferred_element_type=jnp.float32)
    gain = jnp.broadcast_to(gain_ref[...], (8, channels)).T[:, :1]
    for f in range(frames):
        latent = features_ref[f].astype(jnp.float32) + placed[:, f * pixels : (f + 1) * pixels]
        latent = latent.astype(jnp.bfloat16)
        latent_ref[f] = latent
        data = latent.astype(jnp.float32)
        mean_square = jnp.mean(data * data, axis=0, keepdims=True)
        normed = data * lax.rsqrt(mean_square + EPS) * gain
        act_ref[f] = (normed / (1.0 + jnp.exp(-normed))).astype(jnp.bfloat16)
    copy.wait()


def spread(act, shift_ref, moved):
    channels, pixels = act.shape
    lane = lax.broadcasted_iota(jnp.int32, act.shape, 1)
    for e in range(3):
        if e == 1:
            middle = act.astype(jnp.float32)
        else:
            side = shift_ref[:, e // 2 * pixels : (e // 2 + 1) * pixels]
            middle = jnp.dot(act, side, preferred_element_type=jnp.float32)
        above = jnp.where(lane >= SIDE, pltpu.roll(middle, SIDE, 1), 0.0)
        below = jnp.where(lane < pixels - SIDE, pltpu.roll(middle, pixels - SIDE, 1), 0.0)
        for b, part in enumerate((above, middle, below)):
            moved[pl.ds((3 * b + e) * channels, channels), :] = part.astype(jnp.bfloat16)


def tap_dot(w_ref, lag, moved):
    channels = w_ref.shape[2]
    return sum(
        jnp.dot(
            w_ref[lag * TAPS + tap], moved[pl.ds(tap * channels, channels), :],
            preferred_element_type=jnp.float32,
        )
        for tap in range(TAPS)
    )


def conv_own_kernel(act_ref, shift_ref, w_ref, part_ref, wide_ref, moved0, moved1):
    channels = w_ref.shape[2]
    spread(act_ref[0], shift_ref, moved0)
    spread(act_ref[1], shift_ref, moved1)
    part_ref[0] = tap_dot(w_ref, 2, moved0)
    part_ref[1] = tap_dot(w_ref, 1, moved0) + tap_dot(w_ref, 2, moved1)
    for lag in range(2):
        for tap in range(TAPS):
            wide_ref[lag, :, tap * channels : (tap + 1) * channels] = w_ref[lag * TAPS + tap]


def conv_halo_kernel(
    halo_ref, shift_ref, wide_ref, part_ref, latent_ref, out_ref, moved0, moved1
):
    spread(halo_ref[0], shift_ref, moved0)
    spread(halo_ref[1], shift_ref, moved1)

    def meet(lag, moved):
        return jnp.dot(wide_ref[lag], moved[...], preferred_element_type=jnp.float32)

    first = part_ref[0] + meet(0, moved0) + meet(1, moved1)
    second = part_ref[1] + meet(0, moved1)
    out_ref[0] = (latent_ref[0].astype(jnp.float32) + first).astype(jnp.bfloat16)
    out_ref[1] = (latent_ref[1].astype(jnp.float32) + second).astype(jnp.bfloat16)


def routes(count):
    own, hop1, swap1, hop2, swap2 = [], [], [], [], []
    for s in range(count):
        r, first, last = s % 4, s < 4, s + 4 >= count
        if r == 0:
            own.append((s, s + 1))
            hop1.append((s, s + 2))
            if not last:
                hop2.append((s, s + 4))
            if not first:
                swap2.append((s, s + 1))
        elif r == 1:
            if not last:
                hop1.append((s, s + 4))
            hop2.append((s, s + 2))
            if not first:
                swap1.append((s, s - 1))
                swap2.append((s, s - 1))
        elif r == 2:
            own.append((s, s + 1))
            if not last:
                hop1.append((s, s - 2))
            swap1.append((s, s + 1))
        else:
            if not last:
                hop1.append((s, s + 4))
            if not first:
                swap1.append((s, s - 1))
                hop2.append((s, s - 2))
            swap2.append((s, s - 1))
    return own, hop1, swap1, hop2, swap2


def shards(queries, keys, values, lookback, proj_weight, features, norm_gain, conv_weight):
    count = lax.axis_size("span")
    me = lax.axis_index("span")
    second = lax.rem(me, 4) == 1
    second, keys, values = lax.optimization_barrier((second, keys, values))
    own, hop1, swap1, hop2, swap2 = routes(count)
    move = functools.partial(lax.ppermute, axis_name="span")

    rows, width = queries.shape
    heads = width // HEAD_DIM
    frames, channels, pixels = features.shape

    block = jax.ShapeDtypeStruct((rows, width), jnp.float32)
    picture = jax.ShapeDtypeStruct(features.shape, jnp.bfloat16)

    k_r1 = move(keys, perm=hop1)
    k_s0 = move(keys, perm=own)
    v_r1 = move(values, perm=hop1)
    v_s0 = move(values, perm=own)

    tokens = frames * pixels // (PATCH * PATCH)
    place_matrix, shift_matrix, w_near = pl.pallas_call(
        one_hot_kernel,
        out_shape=(
            jax.ShapeDtypeStruct((PATCH * PATCH * tokens, frames * pixels), jnp.bfloat16),
            jax.ShapeDtypeStruct((pixels, 2 * pixels), jnp.bfloat16),
            jax.ShapeDtypeStruct(proj_weight.shape, jnp.bfloat16),
        ),
        in_specs=[pl.BlockSpec(memory_space=pl.ANY)],
        out_specs=(VMEM,) * 3,
        scratch_shapes=[pltpu.SemaphoreType.DMA],
        compiler_params=params(),
        name="one_hot",
    )(proj_weight)
    k_r1, place_matrix, shift_matrix, w_near = lax.optimization_barrier(
        (k_r1, place_matrix, shift_matrix, w_near)
    )

    k_r2 = move(jnp.where(second, keys, k_r1), perm=hop2)
    k_s1 = move(k_r1, perm=swap1)
    v_hop = jnp.where(second, values, v_r1)
    v_r2 = move(v_hop, perm=hop2)
    v_s1 = move(v_r1, perm=swap1)

    mixed, top, total = pl.pallas_call(
        early_kernel,
        out_shape=(block,) * 3,
        in_specs=[SMEM] + [VMEM] * 9,
        out_specs=(VMEM,) * 3,
        compiler_params=params(),
        name="early",
        cost_estimate=pl.CostEstimate(
            flops=12 * rows * rows * width,
            bytes_accessed=9 * rows * width * 2,
            transcendentals=3 * heads * rows * rows,
        ),
    )(
        lookback, queries, keys, k_r1, k_s0, k_s1, values, v_r1, v_s0, v_s1,
    )

    k_s2 = move(k_r2, perm=swap2)
    weights, base, inverse = pl.pallas_call(
        late_kernel,
        out_shape=(
            jax.ShapeDtypeStruct((heads, rows, 2 * rows), jnp.bfloat16), block, block,
        ),
        in_specs=[SMEM] + [VMEM] * 6,
        out_specs=(VMEM,) * 3,
        compiler_params=params(),
        name="late",
        cost_estimate=pl.CostEstimate(
            flops=4 * rows * rows * width,
            bytes_accessed=9 * rows * width * 2,
            transcendentals=2 * heads * rows * rows,
        ),
    )(lookback, queries, k_r2, k_s2, mixed, top, total)

    v_r2, _ = lax.optimization_barrier((v_r2, mixed))
    v_s2 = move(v_r2, perm=swap2)
    patch_width = proj_weight.shape[1]
    attended, latent, activated = pl.pallas_call(
        latent_kernel,
        out_shape=(jax.ShapeDtypeStruct((rows, width), jnp.bfloat16), picture, picture),
        in_specs=[VMEM] * 9,
        out_specs=(pl.BlockSpec(memory_space=pl.ANY), VMEM, VMEM),
        scratch_shapes=[
            pltpu.VMEM((rows, width), jnp.bfloat16),
            pltpu.VMEM((patch_width, rows), jnp.float32),
            pltpu.SemaphoreType.DMA,
        ],
        compiler_params=params(),
        name="latent",
        cost_estimate=pl.CostEstimate(
            flops=2 * rows * width * (2 * rows + patch_width),
            bytes_accessed=10 * rows * width * 2 + width * patch_width * 2,
            transcendentals=features.size,
        ),
    )(
        weights, base, inverse, v_r2, v_s2, w_near, place_matrix, features,
        norm_gain.reshape(1, channels),
    )

    halo = move(activated, perm=[(s, s + 1) for s in range(count - 1)])

    moved = [pltpu.VMEM((TAPS * channels, pixels), jnp.bfloat16)] * 2
    conv_cost = pl.CostEstimate(
        flops=2 * channels * TAPS * channels * pixels * 3,
        bytes_accessed=conv_weight.size * 2 + shift_matrix.size * 2,
        transcendentals=0,
    )
    part, wide = pl.pallas_call(
        conv_own_kernel,
        out_shape=(
            jax.ShapeDtypeStruct(features.shape, jnp.float32),
            jax.ShapeDtypeStruct((2, channels, TAPS * channels), jnp.bfloat16),
        ),
        in_specs=[VMEM] * 3,
        out_specs=(VMEM,) * 2,
        scratch_shapes=moved,
        compiler_params=params(),
        name="conv_own",
        cost_estimate=conv_cost,
    )(activated, shift_matrix, conv_weight)
    decoded = pl.pallas_call(
        conv_halo_kernel,
        out_shape=jax.ShapeDtypeStruct(features.shape, jnp.bfloat16),
        in_specs=[VMEM] * 5,
        out_specs=VMEM,
        scratch_shapes=moved,
        compiler_params=params(),
        name="conv_halo",
        cost_estimate=conv_cost,
    )(halo, shift_matrix, wide, part, latent)
    return (attended, decoded)


def solution(mesh):
    placed = (
        P(("groups", "span"), None),
        P(("groups", "span"), None),
        P(("groups", "span"), None),
        P(("groups", "span")),
        P(),
        P(("groups", "span"), None, None),
        P(),
        P(),
    )
    return jax.shard_map(
        shards,
        mesh=mesh,
        in_specs=placed,
        out_specs=(P(("groups", "span"), None), P(("groups", "span"), None, None)),
        check_vma=False,
    )
```

```python
import functools

import jax
import jax.numpy as jnp
import numpy as np
from jax import lax
from jax.experimental import pallas as pl
from jax.experimental.pallas import tpu as pltpu
from jax.sharding import PartitionSpec as P

HEAD_DIM = 128
LOOKBACK = 3
SIDE = 16
PATCH = 2
TAPS = 9
EPS = 1e-06

VMEM = pl.BlockSpec(memory_space=pltpu.VMEM)
SMEM = pl.BlockSpec(memory_space=pltpu.SMEM)


def params():
    return pltpu.CompilerParams(vmem_limit_bytes=16 * 1024 * 1024)


def one_hot_kernel(w_far, place_ref, shift_ref, w_near, sem):
    copy = pltpu.make_async_copy(w_far, w_near, sem)
    copy.start()
    half = SIDE // PATCH
    patches = half * half
    pixels = SIDE * SIDE
    tokens = place_ref.shape[0] // (PATCH * PATCH)
    column = lax.broadcasted_iota(jnp.int32, (tokens, place_ref.shape[1]), 1)
    pixel = column % pixels
    row, col = pixel // SIDE, pixel % SIDE
    token = column // pixels * patches + row // PATCH * half + col // PATCH
    corner = row % PATCH * PATCH + col % PATCH
    hit = lax.broadcasted_iota(jnp.int32, token.shape, 0) == token
    for k in range(PATCH * PATCH):
        place_ref[pl.ds(k * tokens, tokens), :] = jnp.where(
            hit & (corner == k), 1.0, 0.0
        ).astype(jnp.bfloat16)
    source = lax.broadcasted_iota(jnp.int32, (pixels, pixels), 0)
    target = lax.broadcasted_iota(jnp.int32, (pixels, pixels), 1)
    for k, e in enumerate((-1, 1)):
        col = target % SIDE + e
        shift_ref[:, k * pixels : (k + 1) * pixels] = jnp.where(
            (col >= 0) & (col < SIDE) & (source == target + e), 1.0, 0.0
        ).astype(jnp.bfloat16)
    copy.wait()


UNSEEN = LOOKBACK + 1
DISTANCES = ((0, UNSEEN, 3, 2, 1), (0, 1, UNSEEN, 2, 3), (0, 2, 3, UNSEEN, 1), (0, 1, 3, 2, UNSEEN))
RATE = float(np.log2(np.e) * HEAD_DIM**-0.5)


def biases(lookback):
    place = lax.rem(lax.axis_index("span"), 4)
    out = []
    for ways in zip(*DISTANCES):
        distance = ways[0]
        for k, way in enumerate(ways[1:], 1):
            distance = jnp.where(place == k, way, distance)
        out.append(jnp.where(distance <= lookback[0], 0.0, -jnp.inf).astype(jnp.float32))
    return out


def head(h):
    return slice(h * HEAD_DIM, (h + 1) * HEAD_DIM)


def staged(heads, *stages):
    held = {}
    for step in range(heads + len(stages) - 1):
        for i, stage in enumerate(stages):
            h = step - i
            if 0 <= h < heads:
                held[h] = stage(h, held.get(h))


def scores_of(q_ref, blocks, biases, h):
    keys = jnp.concatenate(blocks, axis=0)
    s = lax.dot_general(
        q_ref[:, head(h)], keys, (((1,), (1,)), ((), ())), preferred_element_type=jnp.float32
    )
    rows = blocks[0].shape[0]
    parts = [s[:, i * rows : (i + 1) * rows] for i in range(len(blocks))]
    return [part if bias is None else part + bias for part, bias in zip(parts, biases)]


def top_of(parts):
    return jnp.max(functools.reduce(jnp.maximum, parts), axis=1, keepdims=True)


def early_kernel(
    lookback, q_ref, k0, k_hop, k_own, k2, v0, v_hop, v_own, v2, mixed_ref, top_ref, total_ref
):
    rows = q_ref.shape[0]
    bias = biases(lookback)
    hopped = lax.rem(lax.axis_index("span"), 2) == 0
    ones = jnp.ones((3 * rows, HEAD_DIM), jnp.bfloat16)

    def score(h, _):
        k1 = jnp.where(hopped, k_hop[:, head(h)], k_own[:, head(h)])
        keys = (k0[:, head(h)], k1, k2[:, head(h)])
        return scores_of(q_ref, keys, (None, bias[1], bias[2]), h)

    def soften(h, parts):
        top = top_of(parts)
        top_ref[:, head(h)] = jnp.broadcast_to(top, (rows, HEAD_DIM))
        probs = [jnp.exp2((part - top) * RATE).astype(jnp.bfloat16) for part in parts]
        return jnp.concatenate(probs, axis=1)

    def blend(h, probs):
        v1 = jnp.where(hopped, v_hop[:, head(h)], v_own[:, head(h)])
        values = jnp.concatenate([v0[:, head(h)], v1, v2[:, head(h)]], axis=0)
        both = jnp.dot(
            probs, jnp.concatenate([values, ones], axis=1), preferred_element_type=jnp.float32
        )
        mixed_ref[:, head(h)] = both[:, :HEAD_DIM]
        total_ref[:, head(h)] = both[:, HEAD_DIM:]

    staged(q_ref.shape[1] // HEAD_DIM, score, soften, blend)


def late_kernel(
    lookback, q_ref, k1, k2, mixed_ref, top_ref, total_ref, p_ref, base_ref, inverse_ref
):
    rows = q_ref.shape[0]
    ones = jnp.ones((2 * rows, HEAD_DIM), jnp.bfloat16)
    bias = biases(lookback)

    def score(h, _):
        return scores_of(q_ref, (k1[:, head(h)], k2[:, head(h)]), (bias[3], bias[4]), h)

    def soften(h, parts):
        before = top_ref[:, head(h)]
        top = jnp.maximum(before, top_of(parts))
        probs = [jnp.exp2((part - top) * RATE).astype(jnp.bfloat16) for part in parts]
        probs = jnp.concatenate(probs, axis=1)
        p_ref[h] = probs
        return probs, jnp.exp2((before - top) * RATE)

    def settle(h, held):
        probs, shrink = held
        total = jnp.dot(probs, ones, preferred_element_type=jnp.float32)
        inverse = 1.0 / (total + total_ref[:, head(h)] * shrink)
        inverse_ref[:, head(h)] = inverse
        base_ref[:, head(h)] = mixed_ref[:, head(h)] * (shrink * inverse)

    staged(q_ref.shape[1] // HEAD_DIM, score, soften, settle)


def blend_late(heads, p_ref, base_ref, inverse_ref, v1, v2, out_ref):
    def blend(i, _):
        h = heads[i]
        values = jnp.concatenate([v1[:, head(h)], v2[:, head(h)]], axis=0)
        return jnp.dot(p_ref[h], values, preferred_element_type=jnp.float32)

    def settle(i, late):
        h = heads[i]
        late = base_ref[:, head(h)] + late * inverse_ref[:, head(h)]
        out_ref[:, head(i)] = late.astype(jnp.bfloat16)

    staged(len(heads), blend, settle)


def first_half_kernel(p_ref, base_ref, inverse_ref, v1, v2, w_ref, out_ref, projected_ref):
    width = out_ref.shape[1]
    heads = range(width // HEAD_DIM)
    blend_late(heads, p_ref, base_ref, inverse_ref, v1, v2, out_ref)
    projected_ref[...] = jnp.dot(
        out_ref[...], w_ref[:width, :], preferred_element_type=jnp.float32
    )


def latent_kernel(
    p_ref, base_ref, inverse_ref, v1, v2, w_ref, first_ref, begun_ref, place_ref, features_ref,
    gain_ref, out_ref, latent_ref, act_ref, mine, turned, sems,
):
    frames, channels, pixels = features_ref.shape
    before, width = first_ref.shape[1], mine.shape[1]
    copies = [
        pltpu.make_async_copy(first_ref, out_ref.at[:, pl.ds(0, before)], sems.at[0]),
        pltpu.make_async_copy(mine, out_ref.at[:, pl.ds(before, width)], sems.at[1]),
    ]
    copies[0].start()
    heads = range(before // HEAD_DIM, (before + width) // HEAD_DIM)
    blend_late(heads, p_ref, base_ref, inverse_ref, v1, v2, mine)
    copies[1].start()
    projected = begun_ref[...] + jnp.dot(
        mine[...], w_ref[before:, :], preferred_element_type=jnp.float32
    )
    turned[...] = projected.T
    parts = [turned[pl.ds(k, channels, stride=4), :] for k in range(4)]
    mixed = jnp.concatenate(parts, axis=1)
    high = mixed.astype(jnp.bfloat16)
    low = (mixed - high.astype(jnp.float32)).astype(jnp.bfloat16)
    placed = jnp.dot(high, place_ref[...], preferred_element_type=jnp.float32)
    placed += jnp.dot(low, place_ref[...], preferred_element_type=jnp.float32)
    gain = jnp.broadcast_to(gain_ref[...], (8, channels)).T[:, :1]
    for f in range(frames):
        latent = features_ref[f].astype(jnp.float32) + placed[:, f * pixels : (f + 1) * pixels]
        latent = latent.astype(jnp.bfloat16)
        latent_ref[f] = latent
        data = latent.astype(jnp.float32)
        mean_square = jnp.mean(data * data, axis=0, keepdims=True)
        normed = data * lax.rsqrt(mean_square + EPS) * gain
        act_ref[f] = (normed / (1.0 + jnp.exp(-normed))).astype(jnp.bfloat16)
    for copy in copies:
        copy.wait()


def spread(act, shift_ref, moved):
    channels, pixels = act.shape
    lane = lax.broadcasted_iota(jnp.int32, act.shape, 1)
    for e in range(3):
        if e == 1:
            middle = act.astype(jnp.float32)
        else:
            side = shift_ref[:, e // 2 * pixels : (e // 2 + 1) * pixels]
            middle = jnp.dot(act, side, preferred_element_type=jnp.float32)
        above = jnp.where(lane >= SIDE, pltpu.roll(middle, SIDE, 1), 0.0)
        below = jnp.where(lane < pixels - SIDE, pltpu.roll(middle, pixels - SIDE, 1), 0.0)
        for b, part in enumerate((above, middle, below)):
            moved[pl.ds((3 * b + e) * channels, channels), :] = part.astype(jnp.bfloat16)


def tap_dot(w_ref, lag, moved):
    channels = w_ref.shape[2]
    return sum(
        jnp.dot(
            w_ref[lag * TAPS + tap], moved[pl.ds(tap * channels, channels), :],
            preferred_element_type=jnp.float32,
        )
        for tap in range(TAPS)
    )


def conv_own_kernel(act_ref, shift_ref, w_ref, part_ref, wide_ref, moved0, moved1):
    channels = w_ref.shape[2]
    spread(act_ref[0], shift_ref, moved0)
    spread(act_ref[1], shift_ref, moved1)
    part_ref[0] = tap_dot(w_ref, 2, moved0)
    part_ref[1] = tap_dot(w_ref, 1, moved0) + tap_dot(w_ref, 2, moved1)
    for lag in range(2):
        for tap in range(TAPS):
            wide_ref[lag, :, tap * channels : (tap + 1) * channels] = w_ref[lag * TAPS + tap]


def conv_halo_kernel(
    halo_ref, shift_ref, wide_ref, part_ref, latent_ref, out_ref, moved0, moved1
):
    spread(halo_ref[0], shift_ref, moved0)
    spread(halo_ref[1], shift_ref, moved1)

    def meet(lag, moved):
        return jnp.dot(wide_ref[lag], moved[...], preferred_element_type=jnp.float32)

    first = part_ref[0] + meet(0, moved0) + meet(1, moved1)
    second = part_ref[1] + meet(0, moved1)
    out_ref[0] = (latent_ref[0].astype(jnp.float32) + first).astype(jnp.bfloat16)
    out_ref[1] = (latent_ref[1].astype(jnp.float32) + second).astype(jnp.bfloat16)


def routes(count):
    own, hop1, swap1, hop2, swap2 = [], [], [], [], []
    for s in range(count):
        r, first, last = s % 4, s < 4, s + 4 >= count
        if r == 0:
            own.append((s, s + 1))
            hop1.append((s, s + 2))
            if not last:
                hop2.append((s, s + 4))
            if not first:
                swap2.append((s, s + 1))
        elif r == 1:
            if not last:
                hop1.append((s, s + 4))
            hop2.append((s, s + 2))
            if not first:
                swap1.append((s, s - 1))
                swap2.append((s, s - 1))
        elif r == 2:
            own.append((s, s + 1))
            if not last:
                hop1.append((s, s - 2))
            swap1.append((s, s + 1))
        else:
            if not last:
                hop1.append((s, s + 4))
            if not first:
                swap1.append((s, s - 1))
                hop2.append((s, s - 2))
            swap2.append((s, s - 1))
    return own, hop1, swap1, hop2, swap2


def shards(queries, keys, values, lookback, proj_weight, features, norm_gain, conv_weight):
    count = lax.axis_size("span")
    me = lax.axis_index("span")
    second = lax.rem(me, 4) == 1
    second, keys, values = lax.optimization_barrier((second, keys, values))
    own, hop1, swap1, hop2, swap2 = routes(count)
    move = functools.partial(lax.ppermute, axis_name="span")

    rows, width = queries.shape
    heads = width // HEAD_DIM
    frames, channels, pixels = features.shape

    block = jax.ShapeDtypeStruct((rows, width), jnp.float32)
    picture = jax.ShapeDtypeStruct(features.shape, jnp.bfloat16)

    k_r1 = move(keys, perm=hop1)
    k_s0 = move(keys, perm=own)
    v_r1 = move(values, perm=hop1)
    v_s0 = move(values, perm=own)

    tokens = frames * pixels // (PATCH * PATCH)
    place_matrix, shift_matrix, w_near = pl.pallas_call(
        one_hot_kernel,
        out_shape=(
            jax.ShapeDtypeStruct((PATCH * PATCH * tokens, frames * pixels), jnp.bfloat16),
            jax.ShapeDtypeStruct((pixels, 2 * pixels), jnp.bfloat16),
            jax.ShapeDtypeStruct(proj_weight.shape, jnp.bfloat16),
        ),
        in_specs=[pl.BlockSpec(memory_space=pl.ANY)],
        out_specs=(VMEM,) * 3,
        scratch_shapes=[pltpu.SemaphoreType.DMA],
        compiler_params=params(),
        name="one_hot",
    )(proj_weight)
    k_r1, place_matrix, shift_matrix, w_near = lax.optimization_barrier(
        (k_r1, place_matrix, shift_matrix, w_near)
    )

    k_r2 = move(jnp.where(second, keys, k_r1), perm=hop2)
    k_s1 = move(k_r1, perm=swap1)
    v_hop = jnp.where(second, values, v_r1)
    v_r2 = move(v_hop, perm=hop2)
    v_s1 = move(v_r1, perm=swap1)

    mixed, top, total = pl.pallas_call(
        early_kernel,
        out_shape=(block,) * 3,
        in_specs=[SMEM] + [VMEM] * 9,
        out_specs=(VMEM,) * 3,
        compiler_params=params(),
        name="early",
        cost_estimate=pl.CostEstimate(
            flops=12 * rows * rows * width,
            bytes_accessed=9 * rows * width * 2,
            transcendentals=3 * heads * rows * rows,
        ),
    )(
        lookback, queries, keys, k_r1, k_s0, k_s1, values, v_r1, v_s0, v_s1,
    )

    k_s2 = move(k_r2, perm=swap2)
    weights, base, inverse = pl.pallas_call(
        late_kernel,
        out_shape=(
            jax.ShapeDtypeStruct((heads, rows, 2 * rows), jnp.bfloat16), block, block,
        ),
        in_specs=[SMEM] + [VMEM] * 6,
        out_specs=(VMEM,) * 3,
        compiler_params=params(),
        name="late",
        cost_estimate=pl.CostEstimate(
            flops=4 * rows * rows * width,
            bytes_accessed=9 * rows * width * 2,
            transcendentals=2 * heads * rows * rows,
        ),
    )(lookback, queries, k_r2, k_s2, mixed, top, total)

    v_r2, _ = lax.optimization_barrier((v_r2, mixed))
    v_s2 = move(v_r2, perm=swap2)
    patch_width = proj_weight.shape[1]
    half = heads // 2 * HEAD_DIM
    first, begun = pl.pallas_call(
        first_half_kernel,
        out_shape=(
            jax.ShapeDtypeStruct((rows, half), jnp.bfloat16),
            jax.ShapeDtypeStruct((rows, patch_width), jnp.float32),
        ),
        in_specs=[VMEM] * 6,
        out_specs=(VMEM,) * 2,
        compiler_params=params(),
        name="first_half",
        cost_estimate=pl.CostEstimate(
            flops=2 * rows * half * (2 * rows + patch_width),
            bytes_accessed=6 * rows * width + half * patch_width * 2,
            transcendentals=0,
        ),
    )(weights, base, inverse, v_r2, v_s2, w_near)

    attended, latent, activated = pl.pallas_call(
        latent_kernel,
        out_shape=(jax.ShapeDtypeStruct((rows, width), jnp.bfloat16), picture, picture),
        in_specs=[VMEM] * 11,
        out_specs=(pl.BlockSpec(memory_space=pl.ANY), VMEM, VMEM),
        scratch_shapes=[
            pltpu.VMEM((rows, width - half), jnp.bfloat16),
            pltpu.VMEM((patch_width, rows), jnp.float32),
            pltpu.SemaphoreType.DMA((2,)),
        ],
        compiler_params=params(),
        name="latent",
        cost_estimate=pl.CostEstimate(
            flops=2 * rows * (width - half) * (2 * rows + patch_width),
            bytes_accessed=10 * rows * width + (width - half) * patch_width * 2,
            transcendentals=features.size,
        ),
    )(
        weights, base, inverse, v_r2, v_s2, w_near, first, begun,
        place_matrix, features, norm_gain.reshape(1, channels),
    )

    halo = move(activated, perm=[(s, s + 1) for s in range(count - 1)])

    moved = [pltpu.VMEM((TAPS * channels, pixels), jnp.bfloat16)] * 2
    conv_cost = pl.CostEstimate(
        flops=2 * channels * TAPS * channels * pixels * 3,
        bytes_accessed=conv_weight.size * 2 + shift_matrix.size * 2,
        transcendentals=0,
    )
    part, wide = pl.pallas_call(
        conv_own_kernel,
        out_shape=(
            jax.ShapeDtypeStruct(features.shape, jnp.float32),
            jax.ShapeDtypeStruct((2, channels, TAPS * channels), jnp.bfloat16),
        ),
        in_specs=[VMEM] * 3,
        out_specs=(VMEM,) * 2,
        scratch_shapes=moved,
        compiler_params=params(),
        name="conv_own",
        cost_estimate=conv_cost,
    )(activated, shift_matrix, conv_weight)
    decoded = pl.pallas_call(
        conv_halo_kernel,
        out_shape=jax.ShapeDtypeStruct(features.shape, jnp.bfloat16),
        in_specs=[VMEM] * 5,
        out_specs=VMEM,
        scratch_shapes=moved,
        compiler_params=params(),
        name="conv_halo",
        cost_estimate=conv_cost,
    )(halo, shift_matrix, wide, part, latent)
    return (attended, decoded)


def solution(mesh):
    placed = (
        P(("groups", "span"), None),
        P(("groups", "span"), None),
        P(("groups", "span"), None),
        P(("groups", "span")),
        P(),
        P(("groups", "span"), None, None),
        P(),
        P(),
    )
    return jax.shard_map(
        shards,
        mesh=mesh,
        in_specs=placed,
        out_specs=(P(("groups", "span"), None), P(("groups", "span"), None, None)),
        check_vma=False,
    )
```

```python
import functools

import jax
import jax.numpy as jnp
import numpy as np
from jax import lax
from jax.experimental import pallas as pl
from jax.experimental.pallas import tpu as pltpu
from jax.sharding import PartitionSpec as P

HEAD_DIM = 128
LOOKBACK = 3
SIDE = 16
PATCH = 2
TAPS = 9
EPS = 1e-06

VMEM = pl.BlockSpec(memory_space=pltpu.VMEM)
SMEM = pl.BlockSpec(memory_space=pltpu.SMEM)


def params():
    return pltpu.CompilerParams(vmem_limit_bytes=16 * 1024 * 1024)


def one_hot_kernel(w_far, place_ref, shift_ref, w_near, sem):
    copy = pltpu.make_async_copy(w_far, w_near, sem)
    copy.start()
    half = SIDE // PATCH
    patches = half * half
    pixels = SIDE * SIDE
    tokens = place_ref.shape[0] // (PATCH * PATCH)
    column = lax.broadcasted_iota(jnp.int32, (tokens, place_ref.shape[1]), 1)
    pixel = column % pixels
    row, col = pixel // SIDE, pixel % SIDE
    token = column // pixels * patches + row // PATCH * half + col // PATCH
    corner = row % PATCH * PATCH + col % PATCH
    hit = lax.broadcasted_iota(jnp.int32, token.shape, 0) == token
    for k in range(PATCH * PATCH):
        place_ref[pl.ds(k * tokens, tokens), :] = jnp.where(
            hit & (corner == k), 1.0, 0.0
        ).astype(jnp.bfloat16)
    source = lax.broadcasted_iota(jnp.int32, (pixels, pixels), 0)
    target = lax.broadcasted_iota(jnp.int32, (pixels, pixels), 1)
    for k, e in enumerate((-1, 1)):
        col = target % SIDE + e
        shift_ref[:, k * pixels : (k + 1) * pixels] = jnp.where(
            (col >= 0) & (col < SIDE) & (source == target + e), 1.0, 0.0
        ).astype(jnp.bfloat16)
    copy.wait()


UNSEEN = LOOKBACK + 1
DISTANCES = ((0, UNSEEN, 3, 2, 1), (0, 1, UNSEEN, 2, 3), (0, 2, 3, UNSEEN, 1), (0, 1, 3, 2, UNSEEN))
RATE = float(np.log2(np.e) * HEAD_DIM**-0.5)


def biases(lookback):
    place = lax.rem(lax.axis_index("span"), 4)
    out = []
    for ways in zip(*DISTANCES):
        distance = ways[0]
        for k, way in enumerate(ways[1:], 1):
            distance = jnp.where(place == k, way, distance)
        out.append(jnp.where(distance <= lookback[0], 0.0, -jnp.inf).astype(jnp.float32))
    return out


def head(h):
    return slice(h * HEAD_DIM, (h + 1) * HEAD_DIM)


def staged(heads, *stages):
    held = {}
    for step in range(heads + len(stages) - 1):
        for i, stage in enumerate(stages):
            h = step - i
            if 0 <= h < heads:
                held[h] = stage(h, held.get(h))


def scores_of(q_ref, blocks, biases, h):
    keys = jnp.concatenate(blocks, axis=0)
    s = lax.dot_general(
        q_ref[:, head(h)], keys, (((1,), (1,)), ((), ())), preferred_element_type=jnp.float32
    )
    rows = blocks[0].shape[0]
    parts = [s[:, i * rows : (i + 1) * rows] for i in range(len(blocks))]
    return [part if bias is None else part + bias for part, bias in zip(parts, biases)]


def top_of(parts):
    return jnp.max(functools.reduce(jnp.maximum, parts), axis=1, keepdims=True)


def early_kernel(
    lookback, q_ref, k0, k_hop, k_own, k2, v0, v_hop, v_own, v2, mixed_ref, top_ref, total_ref
):
    rows = q_ref.shape[0]
    bias = biases(lookback)
    hopped = lax.rem(lax.axis_index("span"), 2) == 0
    ones = jnp.ones((3 * rows, HEAD_DIM), jnp.bfloat16)

    def score(h, _):
        k1 = jnp.where(hopped, k_hop[:, head(h)], k_own[:, head(h)])
        keys = (k0[:, head(h)], k1, k2[:, head(h)])
        return scores_of(q_ref, keys, (None, bias[1], bias[2]), h)

    def soften(h, parts):
        top = top_of(parts)
        top_ref[:, head(h)] = jnp.broadcast_to(top, (rows, HEAD_DIM))
        probs = [jnp.exp2((part - top) * RATE).astype(jnp.bfloat16) for part in parts]
        return jnp.concatenate(probs, axis=1)

    def blend(h, probs):
        v1 = jnp.where(hopped, v_hop[:, head(h)], v_own[:, head(h)])
        values = jnp.concatenate([v0[:, head(h)], v1, v2[:, head(h)]], axis=0)
        both = jnp.dot(
            probs, jnp.concatenate([values, ones], axis=1), preferred_element_type=jnp.float32
        )
        mixed_ref[:, head(h)] = both[:, :HEAD_DIM]
        total_ref[:, head(h)] = both[:, HEAD_DIM:]

    staged(q_ref.shape[1] // HEAD_DIM, score, soften, blend)


def late_kernel(
    lookback, q_ref, k1, k2, mixed_ref, top_ref, total_ref, p_ref, base_ref, inverse_ref
):
    rows = q_ref.shape[0]
    ones = jnp.ones((2 * rows, HEAD_DIM), jnp.bfloat16)
    bias = biases(lookback)

    def score(h, _):
        return scores_of(q_ref, (k1[:, head(h)], k2[:, head(h)]), (bias[3], bias[4]), h)

    def soften(h, parts):
        before = top_ref[:, head(h)]
        top = jnp.maximum(before, top_of(parts))
        probs = [jnp.exp2((part - top) * RATE).astype(jnp.bfloat16) for part in parts]
        probs = jnp.concatenate(probs, axis=1)
        p_ref[h] = probs
        return probs, jnp.exp2((before - top) * RATE)

    def settle(h, held):
        probs, shrink = held
        total = jnp.dot(probs, ones, preferred_element_type=jnp.float32)
        inverse = 1.0 / (total + total_ref[:, head(h)] * shrink)
        inverse_ref[:, head(h)] = inverse
        base_ref[:, head(h)] = mixed_ref[:, head(h)] * (shrink * inverse)

    staged(q_ref.shape[1] // HEAD_DIM, score, soften, settle)


def blend_late(heads, p_ref, base_ref, inverse_ref, v1, v2, out_ref):
    def blend(i, _):
        h = heads[i]
        values = jnp.concatenate([v1[:, head(h)], v2[:, head(h)]], axis=0)
        return jnp.dot(p_ref[h], values, preferred_element_type=jnp.float32)

    def settle(i, late):
        h = heads[i]
        late = base_ref[:, head(h)] + late * inverse_ref[:, head(h)]
        out_ref[:, head(i)] = late.astype(jnp.bfloat16)

    staged(len(heads), blend, settle)


def first_half_kernel(p_ref, base_ref, inverse_ref, v1, v2, w_ref, out_ref, projected_ref):
    width = out_ref.shape[1]
    heads = range(width // HEAD_DIM)
    blend_late(heads, p_ref, base_ref, inverse_ref, v1, v2, out_ref)
    projected_ref[...] = jnp.dot(
        out_ref[...], w_ref[:width, :], preferred_element_type=jnp.float32
    )


def second_half_kernel(
    p_ref, base_ref, inverse_ref, v1, v2, w_ref, begun_ref, out_ref, turned_ref
):
    width = base_ref.shape[1]
    before = width - out_ref.shape[1]
    heads = range(before // HEAD_DIM, width // HEAD_DIM)
    blend_late(heads, p_ref, base_ref, inverse_ref, v1, v2, out_ref)
    projected = begun_ref[...] + jnp.dot(
        out_ref[...], w_ref[before:, :], preferred_element_type=jnp.float32
    )
    turned_ref[...] = projected.T


def latent_kernel(
    first_ref, second_ref, turned, place_ref, features_ref, gain_ref,
    out_ref, latent_ref, act_ref, sems,
):
    frames, channels, pixels = features_ref.shape
    before, width = first_ref.shape[1], second_ref.shape[1]
    copies = [
        pltpu.make_async_copy(first_ref, out_ref.at[:, pl.ds(0, before)], sems.at[0]),
        pltpu.make_async_copy(second_ref, out_ref.at[:, pl.ds(before, width)], sems.at[1]),
    ]
    for copy in copies:
        copy.start()
    parts = [turned[pl.ds(k, channels, stride=4), :] for k in range(4)]
    mixed = jnp.concatenate(parts, axis=1)
    high = mixed.astype(jnp.bfloat16)
    low = (mixed - high.astype(jnp.float32)).astype(jnp.bfloat16)
    placed = jnp.dot(high, place_ref[...], preferred_element_type=jnp.float32)
    placed += jnp.dot(low, place_ref[...], preferred_element_type=jnp.float32)
    gain = jnp.broadcast_to(gain_ref[...], (8, channels)).T[:, :1]
    for f in range(frames):
        latent = features_ref[f].astype(jnp.float32) + placed[:, f * pixels : (f + 1) * pixels]
        latent = latent.astype(jnp.bfloat16)
        latent_ref[f] = latent
        data = latent.astype(jnp.float32)
        mean_square = jnp.mean(data * data, axis=0, keepdims=True)
        normed = data * lax.rsqrt(mean_square + EPS) * gain
        act_ref[f] = (normed / (1.0 + jnp.exp(-normed))).astype(jnp.bfloat16)
    for copy in copies:
        copy.wait()


def spread(act, shift_ref, moved):
    channels, pixels = act.shape
    lane = lax.broadcasted_iota(jnp.int32, act.shape, 1)
    for e in range(3):
        if e == 1:
            middle = act.astype(jnp.float32)
        else:
            side = shift_ref[:, e // 2 * pixels : (e // 2 + 1) * pixels]
            middle = jnp.dot(act, side, preferred_element_type=jnp.float32)
        above = jnp.where(lane >= SIDE, pltpu.roll(middle, SIDE, 1), 0.0)
        below = jnp.where(lane < pixels - SIDE, pltpu.roll(middle, pixels - SIDE, 1), 0.0)
        for b, part in enumerate((above, middle, below)):
            moved[pl.ds((3 * b + e) * channels, channels), :] = part.astype(jnp.bfloat16)


def tap_dot(w_ref, lag, moved):
    channels = w_ref.shape[2]
    return sum(
        jnp.dot(
            w_ref[lag * TAPS + tap], moved[pl.ds(tap * channels, channels), :],
            preferred_element_type=jnp.float32,
        )
        for tap in range(TAPS)
    )


def conv_own_kernel(act_ref, shift_ref, w_ref, part_ref, wide_ref, moved0, moved1):
    channels = w_ref.shape[2]
    spread(act_ref[0], shift_ref, moved0)
    spread(act_ref[1], shift_ref, moved1)
    part_ref[0] = tap_dot(w_ref, 2, moved0)
    part_ref[1] = tap_dot(w_ref, 1, moved0) + tap_dot(w_ref, 2, moved1)
    for lag in range(2):
        for tap in range(TAPS):
            wide_ref[lag, :, tap * channels : (tap + 1) * channels] = w_ref[lag * TAPS + tap]


def halo_shift_kernel(halo_ref, shift_ref, moved0, moved1):
    spread(halo_ref[0], shift_ref, moved0)
    spread(halo_ref[1], shift_ref, moved1)


def conv_halo_kernel(moved0, moved1, wide_ref, part_ref, latent_ref, out_ref):
    def meet(lag, moved):
        return jnp.dot(wide_ref[lag], moved[...], preferred_element_type=jnp.float32)

    first = part_ref[0] + meet(0, moved0) + meet(1, moved1)
    second = part_ref[1] + meet(0, moved1)
    out_ref[0] = (latent_ref[0].astype(jnp.float32) + first).astype(jnp.bfloat16)
    out_ref[1] = (latent_ref[1].astype(jnp.float32) + second).astype(jnp.bfloat16)


def routes(count):
    own, hop1, swap1, hop2, swap2 = [], [], [], [], []
    for s in range(count):
        r, first, last = s % 4, s < 4, s + 4 >= count
        if r == 0:
            own.append((s, s + 1))
            hop1.append((s, s + 2))
            if not last:
                hop2.append((s, s + 4))
            if not first:
                swap2.append((s, s + 1))
        elif r == 1:
            if not last:
                hop1.append((s, s + 4))
            hop2.append((s, s + 2))
            if not first:
                swap1.append((s, s - 1))
                swap2.append((s, s - 1))
        elif r == 2:
            own.append((s, s + 1))
            if not last:
                hop1.append((s, s - 2))
            swap1.append((s, s + 1))
        else:
            if not last:
                hop1.append((s, s + 4))
            if not first:
                swap1.append((s, s - 1))
                hop2.append((s, s - 2))
            swap2.append((s, s - 1))
    return own, hop1, swap1, hop2, swap2


def shards(queries, keys, values, lookback, proj_weight, features, norm_gain, conv_weight):
    count = lax.axis_size("span")
    me = lax.axis_index("span")
    second = lax.rem(me, 4) == 1
    second, keys, values = lax.optimization_barrier((second, keys, values))
    own, hop1, swap1, hop2, swap2 = routes(count)
    move = functools.partial(lax.ppermute, axis_name="span")

    rows, width = queries.shape
    heads = width // HEAD_DIM
    frames, channels, pixels = features.shape

    block = jax.ShapeDtypeStruct((rows, width), jnp.float32)
    picture = jax.ShapeDtypeStruct(features.shape, jnp.bfloat16)

    k_r1 = move(keys, perm=hop1)
    k_s0 = move(keys, perm=own)
    v_r1 = move(values, perm=hop1)
    v_s0 = move(values, perm=own)

    tokens = frames * pixels // (PATCH * PATCH)
    place_matrix, shift_matrix, w_near = pl.pallas_call(
        one_hot_kernel,
        out_shape=(
            jax.ShapeDtypeStruct((PATCH * PATCH * tokens, frames * pixels), jnp.bfloat16),
            jax.ShapeDtypeStruct((pixels, 2 * pixels), jnp.bfloat16),
            jax.ShapeDtypeStruct(proj_weight.shape, jnp.bfloat16),
        ),
        in_specs=[pl.BlockSpec(memory_space=pl.ANY)],
        out_specs=(VMEM,) * 3,
        scratch_shapes=[pltpu.SemaphoreType.DMA],
        compiler_params=params(),
        name="one_hot",
    )(proj_weight)
    k_r1, place_matrix, shift_matrix, w_near = lax.optimization_barrier(
        (k_r1, place_matrix, shift_matrix, w_near)
    )

    k_r2 = move(jnp.where(second, keys, k_r1), perm=hop2)
    k_s1 = move(k_r1, perm=swap1)
    v_hop = jnp.where(second, values, v_r1)
    v_r2 = move(v_hop, perm=hop2)
    v_s1 = move(v_r1, perm=swap1)

    mixed, top, total = pl.pallas_call(
        early_kernel,
        out_shape=(block,) * 3,
        in_specs=[SMEM] + [VMEM] * 9,
        out_specs=(VMEM,) * 3,
        compiler_params=params(),
        name="early",
        cost_estimate=pl.CostEstimate(
            flops=12 * rows * rows * width,
            bytes_accessed=9 * rows * width * 2,
            transcendentals=3 * heads * rows * rows,
        ),
    )(
        lookback, queries, keys, k_r1, k_s0, k_s1, values, v_r1, v_s0, v_s1,
    )

    k_s2 = move(k_r2, perm=swap2)
    weights, base, inverse = pl.pallas_call(
        late_kernel,
        out_shape=(
            jax.ShapeDtypeStruct((heads, rows, 2 * rows), jnp.bfloat16), block, block,
        ),
        in_specs=[SMEM] + [VMEM] * 6,
        out_specs=(VMEM,) * 3,
        compiler_params=params(),
        name="late",
        cost_estimate=pl.CostEstimate(
            flops=4 * rows * rows * width,
            bytes_accessed=9 * rows * width * 2,
            transcendentals=2 * heads * rows * rows,
        ),
    )(lookback, queries, k_r2, k_s2, mixed, top, total)

    v_r2, _ = lax.optimization_barrier((v_r2, mixed))
    v_s2 = move(v_r2, perm=swap2)
    patch_width = proj_weight.shape[1]
    half = heads // 2 * HEAD_DIM
    first, begun = pl.pallas_call(
        first_half_kernel,
        out_shape=(
            jax.ShapeDtypeStruct((rows, half), jnp.bfloat16),
            jax.ShapeDtypeStruct((rows, patch_width), jnp.float32),
        ),
        in_specs=[VMEM] * 6,
        out_specs=(VMEM,) * 2,
        compiler_params=params(),
        name="first_half",
        cost_estimate=pl.CostEstimate(
            flops=2 * rows * half * (2 * rows + patch_width),
            bytes_accessed=6 * rows * width + half * patch_width * 2,
            transcendentals=0,
        ),
    )(weights, base, inverse, v_r2, v_s2, w_near)

    second_half, turned = pl.pallas_call(
        second_half_kernel,
        out_shape=(
            jax.ShapeDtypeStruct((rows, width - half), jnp.bfloat16),
            jax.ShapeDtypeStruct((patch_width, rows), jnp.float32),
        ),
        in_specs=[VMEM] * 7,
        out_specs=(VMEM,) * 2,
        compiler_params=params(),
        name="second_half",
        cost_estimate=pl.CostEstimate(
            flops=2 * rows * (width - half) * (2 * rows + patch_width),
            bytes_accessed=6 * rows * width + (width - half) * patch_width * 2,
            transcendentals=0,
        ),
    )(weights, base, inverse, v_r2, v_s2, w_near, begun)

    attended, latent, activated = pl.pallas_call(
        latent_kernel,
        out_shape=(jax.ShapeDtypeStruct((rows, width), jnp.bfloat16), picture, picture),
        in_specs=[VMEM] * 6,
        out_specs=(pl.BlockSpec(memory_space=pl.ANY), VMEM, VMEM),
        scratch_shapes=[pltpu.SemaphoreType.DMA((2,))],
        compiler_params=params(),
        name="latent",
        cost_estimate=pl.CostEstimate(
            flops=4 * channels * place_matrix.size,
            bytes_accessed=4 * rows * width + 6 * features.size,
            transcendentals=features.size,
        ),
    )(first, second_half, turned, place_matrix, features, norm_gain.reshape(1, channels))

    halo = move(activated, perm=[(s, s + 1) for s in range(count - 1)])

    moved = [pltpu.VMEM((TAPS * channels, pixels), jnp.bfloat16)] * 2
    conv_cost = pl.CostEstimate(
        flops=2 * channels * TAPS * channels * pixels * 3,
        bytes_accessed=conv_weight.size * 2 + shift_matrix.size * 2,
        transcendentals=0,
    )
    part, wide = pl.pallas_call(
        conv_own_kernel,
        out_shape=(
            jax.ShapeDtypeStruct(features.shape, jnp.float32),
            jax.ShapeDtypeStruct((2, channels, TAPS * channels), jnp.bfloat16),
        ),
        in_specs=[VMEM] * 3,
        out_specs=(VMEM,) * 2,
        scratch_shapes=moved,
        compiler_params=params(),
        name="conv_own",
        cost_estimate=conv_cost,
    )(activated, shift_matrix, conv_weight)
    shifted = pl.pallas_call(
        halo_shift_kernel,
        out_shape=(jax.ShapeDtypeStruct((TAPS * channels, pixels), jnp.bfloat16),) * 2,
        in_specs=[VMEM] * 2,
        out_specs=(VMEM,) * 2,
        compiler_params=params(),
        name="halo_shift",
        cost_estimate=pl.CostEstimate(
            flops=8 * channels * pixels * pixels,
            bytes_accessed=4 * TAPS * channels * pixels,
            transcendentals=0,
        ),
    )(halo, shift_matrix)
    decoded = pl.pallas_call(
        conv_halo_kernel,
        out_shape=jax.ShapeDtypeStruct(features.shape, jnp.bfloat16),
        in_specs=[VMEM] * 5,
        out_specs=VMEM,
        compiler_params=params(),
        name="conv_halo",
        cost_estimate=conv_cost,
    )(*shifted, wide, part, latent)
    return (attended, decoded)


def solution(mesh):
    placed = (
        P(("groups", "span"), None),
        P(("groups", "span"), None),
        P(("groups", "span"), None),
        P(("groups", "span")),
        P(),
        P(("groups", "span"), None, None),
        P(),
        P(),
    )
    return jax.shard_map(
        shards,
        mesh=mesh,
        in_specs=placed,
        out_specs=(P(("groups", "span"), None), P(("groups", "span"), None, None)),
        check_vma=False,
    )
```

```python
import functools

import jax
import jax.numpy as jnp
import numpy as np
from jax import lax
from jax.experimental import pallas as pl
from jax.experimental.pallas import tpu as pltpu
from jax.sharding import PartitionSpec as P

HEAD_DIM = 128
LOOKBACK = 3
SIDE = 16
PATCH = 2
TAPS = 9
EPS = 1e-06

VMEM = pl.BlockSpec(memory_space=pltpu.VMEM)
SMEM = pl.BlockSpec(memory_space=pltpu.SMEM)


def params():
    return pltpu.CompilerParams(vmem_limit_bytes=16 * 1024 * 1024)


def one_hot_kernel(w_far, place_ref, shift_ref, w_near, sem):
    copy = pltpu.make_async_copy(w_far, w_near, sem)
    copy.start()
    half = SIDE // PATCH
    patches = half * half
    pixels = SIDE * SIDE
    tokens = place_ref.shape[0] // (PATCH * PATCH)
    column = lax.broadcasted_iota(jnp.int32, (tokens, place_ref.shape[1]), 1)
    pixel = column % pixels
    row, col = pixel // SIDE, pixel % SIDE
    token = column // pixels * patches + row // PATCH * half + col // PATCH
    corner = row % PATCH * PATCH + col % PATCH
    hit = lax.broadcasted_iota(jnp.int32, token.shape, 0) == token
    for k in range(PATCH * PATCH):
        place_ref[pl.ds(k * tokens, tokens), :] = jnp.where(
            hit & (corner == k), 1.0, 0.0
        ).astype(jnp.bfloat16)
    source = lax.broadcasted_iota(jnp.int32, (pixels, pixels), 0)
    target = lax.broadcasted_iota(jnp.int32, (pixels, pixels), 1)
    for k, e in enumerate((-1, 1)):
        col = target % SIDE + e
        shift_ref[:, k * pixels : (k + 1) * pixels] = jnp.where(
            (col >= 0) & (col < SIDE) & (source == target + e), 1.0, 0.0
        ).astype(jnp.bfloat16)
    copy.wait()


UNSEEN = LOOKBACK + 1
DISTANCES = ((0, UNSEEN, 3, 2, 1), (0, 1, UNSEEN, 2, 3), (0, 2, 3, UNSEEN, 1), (0, 1, 3, 2, UNSEEN))
RATE = float(np.log2(np.e) * HEAD_DIM**-0.5)


def biases(lookback):
    place = lax.rem(lax.axis_index("span"), 4)
    out = []
    for ways in zip(*DISTANCES):
        distance = ways[0]
        for k, way in enumerate(ways[1:], 1):
            distance = jnp.where(place == k, way, distance)
        out.append(jnp.where(distance <= lookback[0], 0.0, -jnp.inf).astype(jnp.float32))
    return out


def head(h):
    return slice(h * HEAD_DIM, (h + 1) * HEAD_DIM)


def staged(heads, *stages):
    held = {}
    for step in range(heads + len(stages) - 1):
        for i, stage in enumerate(stages):
            h = step - i
            if 0 <= h < heads:
                held[h] = stage(h, held.get(h))


def scores_of(q_ref, blocks, biases, h):
    keys = jnp.concatenate(blocks, axis=0)
    s = lax.dot_general(
        q_ref[:, head(h)], keys, (((1,), (1,)), ((), ())), preferred_element_type=jnp.float32
    )
    rows = blocks[0].shape[0]
    parts = [s[:, i * rows : (i + 1) * rows] for i in range(len(blocks))]
    return [part if bias is None else part + bias for part, bias in zip(parts, biases)]


def top_of(parts):
    return jnp.max(functools.reduce(jnp.maximum, parts), axis=1, keepdims=True)


def early_kernel(
    lookback, q_ref, k0, k_hop, k_own, k2, v0, v_hop, v_own, v2, mixed_ref, top_ref, total_ref
):
    rows = q_ref.shape[0]
    bias = biases(lookback)
    hopped = lax.rem(lax.axis_index("span"), 2) == 0
    ones = jnp.ones((3 * rows, HEAD_DIM), jnp.bfloat16)

    def score(h, _):
        k1 = jnp.where(hopped, k_hop[:, head(h)], k_own[:, head(h)])
        keys = (k0[:, head(h)], k1, k2[:, head(h)])
        return scores_of(q_ref, keys, (None, bias[1], bias[2]), h)

    def soften(h, parts):
        top = top_of(parts)
        top_ref[:, head(h)] = jnp.broadcast_to(top, (rows, HEAD_DIM))
        probs = [jnp.exp2((part - top) * RATE).astype(jnp.bfloat16) for part in parts]
        return jnp.concatenate(probs, axis=1)

    def blend(h, probs):
        v1 = jnp.where(hopped, v_hop[:, head(h)], v_own[:, head(h)])
        values = jnp.concatenate([v0[:, head(h)], v1, v2[:, head(h)]], axis=0)
        both = jnp.dot(
            probs, jnp.concatenate([values, ones], axis=1), preferred_element_type=jnp.float32
        )
        mixed_ref[:, head(h)] = both[:, :HEAD_DIM]
        total_ref[:, head(h)] = both[:, HEAD_DIM:]

    staged(q_ref.shape[1] // HEAD_DIM, score, soften, blend)


def late_kernel(
    lookback, q_ref, k1, k2, mixed_ref, top_ref, total_ref, p_ref, base_ref, inverse_ref
):
    rows = q_ref.shape[0]
    ones = jnp.ones((2 * rows, HEAD_DIM), jnp.bfloat16)
    bias = biases(lookback)

    def score(h, _):
        return scores_of(q_ref, (k1[:, head(h)], k2[:, head(h)]), (bias[3], bias[4]), h)

    def soften(h, parts):
        before = top_ref[:, head(h)]
        top = jnp.maximum(before, top_of(parts))
        probs = [jnp.exp2((part - top) * RATE).astype(jnp.bfloat16) for part in parts]
        probs = jnp.concatenate(probs, axis=1)
        p_ref[h] = probs
        return probs, jnp.exp2((before - top) * RATE)

    def settle(h, held):
        probs, shrink = held
        total = jnp.dot(probs, ones, preferred_element_type=jnp.float32)
        inverse = 1.0 / (total + total_ref[:, head(h)] * shrink)
        inverse_ref[:, head(h)] = inverse
        base_ref[:, head(h)] = mixed_ref[:, head(h)] * (shrink * inverse)

    staged(q_ref.shape[1] // HEAD_DIM, score, soften, settle)


def blend_late(heads, p_ref, base_ref, inverse_ref, v1, v2, out_ref):
    def blend(i, _):
        h = heads[i]
        values = jnp.concatenate([v1[:, head(h)], v2[:, head(h)]], axis=0)
        return jnp.dot(p_ref[h], values, preferred_element_type=jnp.float32)

    def settle(i, late):
        h = heads[i]
        late = base_ref[:, head(h)] + late * inverse_ref[:, head(h)]
        out_ref[:, head(i)] = late.astype(jnp.bfloat16)

    staged(len(heads), blend, settle)


def first_half_kernel(p_ref, base_ref, inverse_ref, v1, v2, w_ref, out_ref, projected_ref):
    width = out_ref.shape[1]
    heads = range(width // HEAD_DIM)
    blend_late(heads, p_ref, base_ref, inverse_ref, v1, v2, out_ref)
    projected_ref[...] = jnp.dot(
        out_ref[...], w_ref[:width, :], preferred_element_type=jnp.float32
    )


def latent_kernel(
    p_ref, base_ref, inverse_ref, v1, v2, w_ref, first_ref, begun_ref, place_ref, features_ref,
    gain_ref, out_ref, latent_ref, act_ref, mine, turned, sems,
):
    frames, channels, pixels = features_ref.shape
    before, width = first_ref.shape[1], mine.shape[1]
    copies = [
        pltpu.make_async_copy(first_ref, out_ref.at[:, pl.ds(0, before)], sems.at[0]),
        pltpu.make_async_copy(mine, out_ref.at[:, pl.ds(before, width)], sems.at[1]),
    ]
    copies[0].start()
    heads = range(before // HEAD_DIM, (before + width) // HEAD_DIM)
    blend_late(heads, p_ref, base_ref, inverse_ref, v1, v2, mine)
    copies[1].start()
    projected = begun_ref[...] + jnp.dot(
        mine[...], w_ref[before:, :], preferred_element_type=jnp.float32
    )
    turned[...] = projected.T
    parts = [turned[pl.ds(k, channels, stride=4), :] for k in range(4)]
    mixed = jnp.concatenate(parts, axis=1)
    high = mixed.astype(jnp.bfloat16)
    low = (mixed - high.astype(jnp.float32)).astype(jnp.bfloat16)
    place = place_ref[...]
    placed = jnp.dot(
        jnp.concatenate([high, low], axis=1), jnp.concatenate([place, place], axis=0),
        preferred_element_type=jnp.float32,
    )
    gain = jnp.broadcast_to(gain_ref[...], (8, channels)).T[:, :1]
    for f in range(frames):
        latent = features_ref[f].astype(jnp.float32) + placed[:, f * pixels : (f + 1) * pixels]
        latent = latent.astype(jnp.bfloat16)
        latent_ref[f] = latent
        data = latent.astype(jnp.float32)
        mean_square = jnp.mean(data * data, axis=0, keepdims=True)
        normed = data * lax.rsqrt(mean_square + EPS) * gain
        act_ref[f] = (normed / (1.0 + jnp.exp(-normed))).astype(jnp.bfloat16)
    for copy in copies:
        copy.wait()


def spread(act, shift_ref, moved):
    channels, pixels = act.shape
    lane = lax.broadcasted_iota(jnp.int32, act.shape, 1)
    for e in range(3):
        if e == 1:
            middle = act.astype(jnp.float32)
        else:
            side = shift_ref[:, e // 2 * pixels : (e // 2 + 1) * pixels]
            middle = jnp.dot(act, side, preferred_element_type=jnp.float32)
        above = jnp.where(lane >= SIDE, pltpu.roll(middle, SIDE, 1), 0.0)
        below = jnp.where(lane < pixels - SIDE, pltpu.roll(middle, pixels - SIDE, 1), 0.0)
        for b, part in enumerate((above, middle, below)):
            moved[pl.ds((3 * b + e) * channels, channels), :] = part.astype(jnp.bfloat16)


def tap_dot(w_ref, lag, moved):
    channels = w_ref.shape[2]
    return sum(
        jnp.dot(
            w_ref[lag * TAPS + tap], moved[pl.ds(tap * channels, channels), :],
            preferred_element_type=jnp.float32,
        )
        for tap in range(TAPS)
    )


def conv_own_kernel(act_ref, shift_ref, w_ref, part_ref, wide_ref, moved0, moved1):
    channels = w_ref.shape[2]
    spread(act_ref[0], shift_ref, moved0)
    spread(act_ref[1], shift_ref, moved1)
    part_ref[0] = tap_dot(w_ref, 2, moved0)
    part_ref[1] = tap_dot(w_ref, 1, moved0) + tap_dot(w_ref, 2, moved1)
    for lag in range(2):
        for tap in range(TAPS):
            wide_ref[lag, :, tap * channels : (tap + 1) * channels] = w_ref[lag * TAPS + tap]


def conv_halo_kernel(
    halo_ref, shift_ref, wide_ref, part_ref, latent_ref, out_ref, moved0, moved1
):
    spread(halo_ref[0], shift_ref, moved0)
    spread(halo_ref[1], shift_ref, moved1)

    def meet(lag, moved):
        return jnp.dot(wide_ref[lag], moved[...], preferred_element_type=jnp.float32)

    first = part_ref[0] + meet(0, moved0) + meet(1, moved1)
    second = part_ref[1] + meet(0, moved1)
    out_ref[0] = (latent_ref[0].astype(jnp.float32) + first).astype(jnp.bfloat16)
    out_ref[1] = (latent_ref[1].astype(jnp.float32) + second).astype(jnp.bfloat16)


def routes(count):
    own, hop1, swap1, hop2, swap2 = [], [], [], [], []
    for s in range(count):
        r, first, last = s % 4, s < 4, s + 4 >= count
        if r == 0:
            own.append((s, s + 1))
            hop1.append((s, s + 2))
            if not last:
                hop2.append((s, s + 4))
            if not first:
                swap2.append((s, s + 1))
        elif r == 1:
            if not last:
                hop1.append((s, s + 4))
            hop2.append((s, s + 2))
            if not first:
                swap1.append((s, s - 1))
                swap2.append((s, s - 1))
        elif r == 2:
            own.append((s, s + 1))
            if not last:
                hop1.append((s, s - 2))
            swap1.append((s, s + 1))
        else:
            if not last:
                hop1.append((s, s + 4))
            if not first:
                swap1.append((s, s - 1))
                hop2.append((s, s - 2))
            swap2.append((s, s - 1))
    return own, hop1, swap1, hop2, swap2


def shards(queries, keys, values, lookback, proj_weight, features, norm_gain, conv_weight):
    count = lax.axis_size("span")
    me = lax.axis_index("span")
    second = lax.rem(me, 4) == 1
    second, keys, values = lax.optimization_barrier((second, keys, values))
    own, hop1, swap1, hop2, swap2 = routes(count)
    move = functools.partial(lax.ppermute, axis_name="span")

    rows, width = queries.shape
    heads = width // HEAD_DIM
    frames, channels, pixels = features.shape

    block = jax.ShapeDtypeStruct((rows, width), jnp.float32)
    picture = jax.ShapeDtypeStruct(features.shape, jnp.bfloat16)

    k_r1 = move(keys, perm=hop1)
    k_s0 = move(keys, perm=own)
    v_r1 = move(values, perm=hop1)
    v_s0 = move(values, perm=own)

    tokens = frames * pixels // (PATCH * PATCH)
    place_matrix, shift_matrix, w_near = pl.pallas_call(
        one_hot_kernel,
        out_shape=(
            jax.ShapeDtypeStruct((PATCH * PATCH * tokens, frames * pixels), jnp.bfloat16),
            jax.ShapeDtypeStruct((pixels, 2 * pixels), jnp.bfloat16),
            jax.ShapeDtypeStruct(proj_weight.shape, jnp.bfloat16),
        ),
        in_specs=[pl.BlockSpec(memory_space=pl.ANY)],
        out_specs=(VMEM,) * 3,
        scratch_shapes=[pltpu.SemaphoreType.DMA],
        compiler_params=params(),
        name="one_hot",
    )(proj_weight)
    k_r1, place_matrix, shift_matrix, w_near = lax.optimization_barrier(
        (k_r1, place_matrix, shift_matrix, w_near)
    )

    k_r2 = move(jnp.where(second, keys, k_r1), perm=hop2)
    k_s1 = move(k_r1, perm=swap1)
    v_hop = jnp.where(second, values, v_r1)
    v_r2 = move(v_hop, perm=hop2)
    v_s1 = move(v_r1, perm=swap1)

    mixed, top, total = pl.pallas_call(
        early_kernel,
        out_shape=(block,) * 3,
        in_specs=[SMEM] + [VMEM] * 9,
        out_specs=(VMEM,) * 3,
        compiler_params=params(),
        name="early",
        cost_estimate=pl.CostEstimate(
            flops=12 * rows * rows * width,
            bytes_accessed=9 * rows * width * 2,
            transcendentals=3 * heads * rows * rows,
        ),
    )(
        lookback, queries, keys, k_r1, k_s0, k_s1, values, v_r1, v_s0, v_s1,
    )

    k_s2 = move(k_r2, perm=swap2)
    weights, base, inverse = pl.pallas_call(
        late_kernel,
        out_shape=(
            jax.ShapeDtypeStruct((heads, rows, 2 * rows), jnp.bfloat16), block, block,
        ),
        in_specs=[SMEM] + [VMEM] * 6,
        out_specs=(VMEM,) * 3,
        compiler_params=params(),
        name="late",
        cost_estimate=pl.CostEstimate(
            flops=4 * rows * rows * width,
            bytes_accessed=9 * rows * width * 2,
            transcendentals=2 * heads * rows * rows,
        ),
    )(lookback, queries, k_r2, k_s2, mixed, top, total)

    v_r2, _ = lax.optimization_barrier((v_r2, mixed))
    v_s2 = move(v_r2, perm=swap2)
    patch_width = proj_weight.shape[1]
    half = heads // 2 * HEAD_DIM
    first, begun = pl.pallas_call(
        first_half_kernel,
        out_shape=(
            jax.ShapeDtypeStruct((rows, half), jnp.bfloat16),
            jax.ShapeDtypeStruct((rows, patch_width), jnp.float32),
        ),
        in_specs=[VMEM] * 6,
        out_specs=(VMEM,) * 2,
        compiler_params=params(),
        name="first_half",
        cost_estimate=pl.CostEstimate(
            flops=2 * rows * half * (2 * rows + patch_width),
            bytes_accessed=6 * rows * width + half * patch_width * 2,
            transcendentals=0,
        ),
    )(weights, base, inverse, v_r2, v_s2, w_near)

    attended, latent, activated = pl.pallas_call(
        latent_kernel,
        out_shape=(jax.ShapeDtypeStruct((rows, width), jnp.bfloat16), picture, picture),
        in_specs=[VMEM] * 11,
        out_specs=(pl.BlockSpec(memory_space=pl.ANY), VMEM, VMEM),
        scratch_shapes=[
            pltpu.VMEM((rows, width - half), jnp.bfloat16),
            pltpu.VMEM((patch_width, rows), jnp.float32),
            pltpu.SemaphoreType.DMA((2,)),
        ],
        compiler_params=params(),
        name="latent",
        cost_estimate=pl.CostEstimate(
            flops=2 * rows * (width - half) * (2 * rows + patch_width),
            bytes_accessed=10 * rows * width + (width - half) * patch_width * 2,
            transcendentals=features.size,
        ),
    )(
        weights, base, inverse, v_r2, v_s2, w_near, first, begun,
        place_matrix, features, norm_gain.reshape(1, channels),
    )

    halo = move(activated, perm=[(s, s + 1) for s in range(count - 1)])

    moved = [pltpu.VMEM((TAPS * channels, pixels), jnp.bfloat16)] * 2
    conv_cost = pl.CostEstimate(
        flops=2 * channels * TAPS * channels * pixels * 3,
        bytes_accessed=conv_weight.size * 2 + shift_matrix.size * 2,
        transcendentals=0,
    )
    part, wide = pl.pallas_call(
        conv_own_kernel,
        out_shape=(
            jax.ShapeDtypeStruct(features.shape, jnp.float32),
            jax.ShapeDtypeStruct((2, channels, TAPS * channels), jnp.bfloat16),
        ),
        in_specs=[VMEM] * 3,
        out_specs=(VMEM,) * 2,
        scratch_shapes=moved,
        compiler_params=params(),
        name="conv_own",
        cost_estimate=conv_cost,
    )(activated, shift_matrix, conv_weight)
    decoded = pl.pallas_call(
        conv_halo_kernel,
        out_shape=jax.ShapeDtypeStruct(features.shape, jnp.bfloat16),
        in_specs=[VMEM] * 5,
        out_specs=VMEM,
        scratch_shapes=moved,
        compiler_params=params(),
        name="conv_halo",
        cost_estimate=conv_cost,
    )(halo, shift_matrix, wide, part, latent)
    return (attended, decoded)


def solution(mesh):
    placed = (
        P(("groups", "span"), None),
        P(("groups", "span"), None),
        P(("groups", "span"), None),
        P(("groups", "span")),
        P(),
        P(("groups", "span"), None, None),
        P(),
        P(),
    )
    return jax.shard_map(
        shards,
        mesh=mesh,
        in_specs=placed,
        out_specs=(P(("groups", "span"), None), P(("groups", "span"), None, None)),
        check_vma=False,
    )
```

```python
import functools

import jax
import jax.numpy as jnp
import numpy as np
from jax import lax
from jax.experimental import pallas as pl
from jax.experimental.pallas import tpu as pltpu
from jax.sharding import PartitionSpec as P

HEAD_DIM = 128
LOOKBACK = 3
SIDE = 16
PATCH = 2
TAPS = 9
EPS = 1e-06

VMEM = pl.BlockSpec(memory_space=pltpu.VMEM)
SMEM = pl.BlockSpec(memory_space=pltpu.SMEM)


def params():
    return pltpu.CompilerParams(vmem_limit_bytes=16 * 1024 * 1024)


def one_hot_kernel(w_far, f_far, place_ref, shift_ref, w_near, f_near, sems):
    copies = [
        pltpu.make_async_copy(w_far, w_near, sems.at[0]),
        pltpu.make_async_copy(f_far, f_near, sems.at[1]),
    ]
    for copy in copies:
        copy.start()
    half = SIDE // PATCH
    patches = half * half
    pixels = SIDE * SIDE
    tokens = place_ref.shape[0] // (PATCH * PATCH)
    column = lax.broadcasted_iota(jnp.int32, (tokens, place_ref.shape[1]), 1)
    pixel = column % pixels
    row, col = pixel // SIDE, pixel % SIDE
    token = column // pixels * patches + row // PATCH * half + col // PATCH
    corner = row % PATCH * PATCH + col % PATCH
    hit = lax.broadcasted_iota(jnp.int32, token.shape, 0) == token
    for k in range(PATCH * PATCH):
        place_ref[pl.ds(k * tokens, tokens), :] = jnp.where(
            hit & (corner == k), 1.0, 0.0
        ).astype(jnp.bfloat16)
    source = lax.broadcasted_iota(jnp.int32, (pixels, pixels), 0)
    target = lax.broadcasted_iota(jnp.int32, (pixels, pixels), 1)
    for k, e in enumerate((-1, 1)):
        col = target % SIDE + e
        shift_ref[:, k * pixels : (k + 1) * pixels] = jnp.where(
            (col >= 0) & (col < SIDE) & (source == target + e), 1.0, 0.0
        ).astype(jnp.bfloat16)
    for copy in copies:
        copy.wait()


UNSEEN = LOOKBACK + 1
DISTANCES = ((0, UNSEEN, 3, 2, 1), (0, 1, UNSEEN, 2, 3), (0, 2, 3, UNSEEN, 1), (0, 1, 3, 2, UNSEEN))
RATE = float(np.log2(np.e) * HEAD_DIM**-0.5)


def biases(lookback):
    place = lax.rem(lax.axis_index("span"), 4)
    out = []
    for ways in zip(*DISTANCES):
        distance = ways[0]
        for k, way in enumerate(ways[1:], 1):
            distance = jnp.where(place == k, way, distance)
        out.append(jnp.where(distance <= lookback[0], 0.0, -jnp.inf).astype(jnp.float32))
    return out


def head(h):
    return slice(h * HEAD_DIM, (h + 1) * HEAD_DIM)


def staged(heads, *stages):
    held = {}
    for step in range(heads + len(stages) - 1):
        for i, stage in enumerate(stages):
            h = step - i
            if 0 <= h < heads:
                held[h] = stage(h, held.get(h))


def scores_of(q_ref, blocks, biases, h):
    keys = jnp.concatenate(blocks, axis=0)
    s = lax.dot_general(
        q_ref[:, head(h)], keys, (((1,), (1,)), ((), ())), preferred_element_type=jnp.float32
    )
    rows = blocks[0].shape[0]
    parts = [s[:, i * rows : (i + 1) * rows] for i in range(len(blocks))]
    return [part if bias is None else part + bias for part, bias in zip(parts, biases)]


def top_of(parts):
    return jnp.max(functools.reduce(jnp.maximum, parts), axis=1, keepdims=True)


def early_kernel(
    lookback, q_ref, k0, k_hop, k_own, k2, v0, v_hop, v_own, v2, mixed_ref, top_ref, total_ref
):
    rows = q_ref.shape[0]
    bias = biases(lookback)
    hopped = lax.rem(lax.axis_index("span"), 2) == 0
    ones = jnp.ones((3 * rows, HEAD_DIM), jnp.bfloat16)

    def score(h, _):
        k1 = jnp.where(hopped, k_hop[:, head(h)], k_own[:, head(h)])
        keys = (k0[:, head(h)], k1, k2[:, head(h)])
        return scores_of(q_ref, keys, (None, bias[1], bias[2]), h)

    def soften(h, parts):
        top = top_of(parts)
        top_ref[:, head(h)] = jnp.broadcast_to(top, (rows, HEAD_DIM))
        probs = [jnp.exp2((part - top) * RATE).astype(jnp.bfloat16) for part in parts]
        return jnp.concatenate(probs, axis=1)

    def blend(h, probs):
        v1 = jnp.where(hopped, v_hop[:, head(h)], v_own[:, head(h)])
        values = jnp.concatenate([v0[:, head(h)], v1, v2[:, head(h)]], axis=0)
        both = jnp.dot(
            probs, jnp.concatenate([values, ones], axis=1), preferred_element_type=jnp.float32
        )
        mixed_ref[:, head(h)] = both[:, :HEAD_DIM]
        total_ref[:, head(h)] = both[:, HEAD_DIM:]

    staged(q_ref.shape[1] // HEAD_DIM, score, soften, blend)


def late_kernel(
    lookback, q_ref, k1, k2, mixed_ref, top_ref, total_ref, p_ref, base_ref, inverse_ref
):
    rows = q_ref.shape[0]
    ones = jnp.ones((2 * rows, HEAD_DIM), jnp.bfloat16)
    bias = biases(lookback)

    def score(h, _):
        return scores_of(q_ref, (k1[:, head(h)], k2[:, head(h)]), (bias[3], bias[4]), h)

    def soften(h, parts):
        before = top_ref[:, head(h)]
        top = jnp.maximum(before, top_of(parts))
        probs = [jnp.exp2((part - top) * RATE).astype(jnp.bfloat16) for part in parts]
        probs = jnp.concatenate(probs, axis=1)
        p_ref[h] = probs
        return probs, jnp.exp2((before - top) * RATE)

    def settle(h, held):
        probs, shrink = held
        total = jnp.dot(probs, ones, preferred_element_type=jnp.float32)
        inverse = 1.0 / (total + total_ref[:, head(h)] * shrink)
        inverse_ref[:, head(h)] = inverse
        base_ref[:, head(h)] = mixed_ref[:, head(h)] * (shrink * inverse)

    staged(q_ref.shape[1] // HEAD_DIM, score, soften, settle)


def blend_late(heads, p_ref, base_ref, inverse_ref, v1, v2, out_ref):
    def blend(i, _):
        h = heads[i]
        values = jnp.concatenate([v1[:, head(h)], v2[:, head(h)]], axis=0)
        return jnp.dot(p_ref[h], values, preferred_element_type=jnp.float32)

    def settle(i, late):
        h = heads[i]
        late = base_ref[:, head(h)] + late * inverse_ref[:, head(h)]
        out_ref[:, head(i)] = late.astype(jnp.bfloat16)

    staged(len(heads), blend, settle)


def first_half_kernel(p_ref, base_ref, inverse_ref, v1, v2, w_ref, out_ref, projected_ref):
    width = out_ref.shape[1]
    heads = range(width // HEAD_DIM)
    blend_late(heads, p_ref, base_ref, inverse_ref, v1, v2, out_ref)
    projected_ref[...] = jnp.dot(
        out_ref[...], w_ref[:width, :], preferred_element_type=jnp.float32
    )


def latent_kernel(
    p_ref, base_ref, inverse_ref, v1, v2, w_ref, first_ref, begun_ref, place_ref, features_ref,
    gain_ref, out_ref, latent_ref, act_ref, mine, turned, sems,
):
    frames, channels, pixels = features_ref.shape
    before, width = first_ref.shape[1], mine.shape[1]
    copies = [
        pltpu.make_async_copy(first_ref, out_ref.at[:, pl.ds(0, before)], sems.at[0]),
        pltpu.make_async_copy(mine, out_ref.at[:, pl.ds(before, width)], sems.at[1]),
    ]
    copies[0].start()
    heads = range(before // HEAD_DIM, (before + width) // HEAD_DIM)
    blend_late(heads, p_ref, base_ref, inverse_ref, v1, v2, mine)
    copies[1].start()
    projected = begun_ref[...] + jnp.dot(
        mine[...], w_ref[before:, :], preferred_element_type=jnp.float32
    )
    turned[...] = projected.T
    parts = [turned[pl.ds(k, channels, stride=4), :] for k in range(4)]
    mixed = jnp.concatenate(parts, axis=1)
    high = mixed.astype(jnp.bfloat16)
    low = (mixed - high.astype(jnp.float32)).astype(jnp.bfloat16)
    placed = jnp.dot(high, place_ref[...], preferred_element_type=jnp.float32)
    placed += jnp.dot(low, place_ref[...], preferred_element_type=jnp.float32)
    gain = jnp.broadcast_to(gain_ref[...], (8, channels)).T[:, :1]
    for f in range(frames):
        latent = features_ref[f].astype(jnp.float32) + placed[:, f * pixels : (f + 1) * pixels]
        latent = latent.astype(jnp.bfloat16)
        latent_ref[f] = latent
        data = latent.astype(jnp.float32)
        mean_square = jnp.mean(data * data, axis=0, keepdims=True)
        normed = data * lax.rsqrt(mean_square + EPS) * gain
        act_ref[f] = (normed / (1.0 + jnp.exp(-normed))).astype(jnp.bfloat16)
    for copy in copies:
        copy.wait()


def spread(act, shift_ref, moved):
    channels, pixels = act.shape
    lane = lax.broadcasted_iota(jnp.int32, act.shape, 1)
    for e in range(3):
        if e == 1:
            middle = act.astype(jnp.float32)
        else:
            side = shift_ref[:, e // 2 * pixels : (e // 2 + 1) * pixels]
            middle = jnp.dot(act, side, preferred_element_type=jnp.float32)
        above = jnp.where(lane >= SIDE, pltpu.roll(middle, SIDE, 1), 0.0)
        below = jnp.where(lane < pixels - SIDE, pltpu.roll(middle, pixels - SIDE, 1), 0.0)
        for b, part in enumerate((above, middle, below)):
            moved[pl.ds((3 * b + e) * channels, channels), :] = part.astype(jnp.bfloat16)


def tap_dot(w_ref, lag, moved):
    channels = w_ref.shape[2]
    return sum(
        jnp.dot(
            w_ref[lag * TAPS + tap], moved[pl.ds(tap * channels, channels), :],
            preferred_element_type=jnp.float32,
        )
        for tap in range(TAPS)
    )


def conv_own_kernel(act_ref, shift_ref, w_ref, part_ref, wide_ref, moved0, moved1):
    channels = w_ref.shape[2]
    spread(act_ref[0], shift_ref, moved0)
    spread(act_ref[1], shift_ref, moved1)
    part_ref[0] = tap_dot(w_ref, 2, moved0)
    part_ref[1] = tap_dot(w_ref, 1, moved0) + tap_dot(w_ref, 2, moved1)
    for lag in range(2):
        for tap in range(TAPS):
            wide_ref[lag, :, tap * channels : (tap + 1) * channels] = w_ref[lag * TAPS + tap]


def conv_halo_kernel(
    halo_ref, shift_ref, wide_ref, part_ref, latent_ref, out_ref, moved0, moved1
):
    spread(halo_ref[0], shift_ref, moved0)
    spread(halo_ref[1], shift_ref, moved1)

    def meet(lag, moved):
        return jnp.dot(wide_ref[lag], moved[...], preferred_element_type=jnp.float32)

    first = part_ref[0] + meet(0, moved0) + meet(1, moved1)
    second = part_ref[1] + meet(0, moved1)
    out_ref[0] = (latent_ref[0].astype(jnp.float32) + first).astype(jnp.bfloat16)
    out_ref[1] = (latent_ref[1].astype(jnp.float32) + second).astype(jnp.bfloat16)


def routes(count):
    own, hop1, swap1, hop2, swap2 = [], [], [], [], []
    for s in range(count):
        r, first, last = s % 4, s < 4, s + 4 >= count
        if r == 0:
            own.append((s, s + 1))
            hop1.append((s, s + 2))
            if not last:
                hop2.append((s, s + 4))
            if not first:
                swap2.append((s, s + 1))
        elif r == 1:
            if not last:
                hop1.append((s, s + 4))
            hop2.append((s, s + 2))
            if not first:
                swap1.append((s, s - 1))
                swap2.append((s, s - 1))
        elif r == 2:
            own.append((s, s + 1))
            if not last:
                hop1.append((s, s - 2))
            swap1.append((s, s + 1))
        else:
            if not last:
                hop1.append((s, s + 4))
            if not first:
                swap1.append((s, s - 1))
                hop2.append((s, s - 2))
            swap2.append((s, s - 1))
    return own, hop1, swap1, hop2, swap2


def shards(queries, keys, values, lookback, proj_weight, features, norm_gain, conv_weight):
    count = lax.axis_size("span")
    me = lax.axis_index("span")
    second = lax.rem(me, 4) == 1
    second, keys, values = lax.optimization_barrier((second, keys, values))
    own, hop1, swap1, hop2, swap2 = routes(count)
    move = functools.partial(lax.ppermute, axis_name="span")

    rows, width = queries.shape
    heads = width // HEAD_DIM
    frames, channels, pixels = features.shape

    block = jax.ShapeDtypeStruct((rows, width), jnp.float32)
    picture = jax.ShapeDtypeStruct(features.shape, jnp.bfloat16)

    k_r1 = move(keys, perm=hop1)
    k_s0 = move(keys, perm=own)
    v_r1 = move(values, perm=hop1)
    v_s0 = move(values, perm=own)

    tokens = frames * pixels // (PATCH * PATCH)
    place_matrix, shift_matrix, w_near, f_near = pl.pallas_call(
        one_hot_kernel,
        out_shape=(
            jax.ShapeDtypeStruct((PATCH * PATCH * tokens, frames * pixels), jnp.bfloat16),
            jax.ShapeDtypeStruct((pixels, 2 * pixels), jnp.bfloat16),
            jax.ShapeDtypeStruct(proj_weight.shape, jnp.bfloat16),
            picture,
        ),
        in_specs=[pl.BlockSpec(memory_space=pl.ANY)] * 2,
        out_specs=(VMEM,) * 4,
        scratch_shapes=[pltpu.SemaphoreType.DMA((2,))],
        compiler_params=params(),
        name="one_hot",
    )(proj_weight, features)
    k_r1, place_matrix, shift_matrix, w_near, f_near = lax.optimization_barrier(
        (k_r1, place_matrix, shift_matrix, w_near, f_near)
    )

    k_r2 = move(jnp.where(second, keys, k_r1), perm=hop2)
    k_s1 = move(k_r1, perm=swap1)
    v_hop = jnp.where(second, values, v_r1)
    v_r2 = move(v_hop, perm=hop2)
    v_s1 = move(v_r1, perm=swap1)

    mixed, top, total = pl.pallas_call(
        early_kernel,
        out_shape=(block,) * 3,
        in_specs=[SMEM] + [VMEM] * 9,
        out_specs=(VMEM,) * 3,
        compiler_params=params(),
        name="early",
        cost_estimate=pl.CostEstimate(
            flops=12 * rows * rows * width,
            bytes_accessed=9 * rows * width * 2,
            transcendentals=3 * heads * rows * rows,
        ),
    )(
        lookback, queries, keys, k_r1, k_s0, k_s1, values, v_r1, v_s0, v_s1,
    )

    k_s2 = move(k_r2, perm=swap2)
    weights, base, inverse = pl.pallas_call(
        late_kernel,
        out_shape=(
            jax.ShapeDtypeStruct((heads, rows, 2 * rows), jnp.bfloat16), block, block,
        ),
        in_specs=[SMEM] + [VMEM] * 6,
        out_specs=(VMEM,) * 3,
        compiler_params=params(),
        name="late",
        cost_estimate=pl.CostEstimate(
            flops=4 * rows * rows * width,
            bytes_accessed=9 * rows * width * 2,
            transcendentals=2 * heads * rows * rows,
        ),
    )(lookback, queries, k_r2, k_s2, mixed, top, total)

    v_r2, _ = lax.optimization_barrier((v_r2, mixed))
    v_s2 = move(v_r2, perm=swap2)
    patch_width = proj_weight.shape[1]
    half = heads // 2 * HEAD_DIM
    first, begun = pl.pallas_call(
        first_half_kernel,
        out_shape=(
            jax.ShapeDtypeStruct((rows, half), jnp.bfloat16),
            jax.ShapeDtypeStruct((rows, patch_width), jnp.float32),
        ),
        in_specs=[VMEM] * 6,
        out_specs=(VMEM,) * 2,
        compiler_params=params(),
        name="first_half",
        cost_estimate=pl.CostEstimate(
            flops=2 * rows * half * (2 * rows + patch_width),
            bytes_accessed=6 * rows * width + half * patch_width * 2,
            transcendentals=0,
        ),
    )(weights, base, inverse, v_r2, v_s2, w_near)

    attended, latent, activated = pl.pallas_call(
        latent_kernel,
        out_shape=(jax.ShapeDtypeStruct((rows, width), jnp.bfloat16), picture, picture),
        in_specs=[VMEM] * 11,
        out_specs=(pl.BlockSpec(memory_space=pl.ANY), VMEM, VMEM),
        scratch_shapes=[
            pltpu.VMEM((rows, width - half), jnp.bfloat16),
            pltpu.VMEM((patch_width, rows), jnp.float32),
            pltpu.SemaphoreType.DMA((2,)),
        ],
        compiler_params=params(),
        name="latent",
        cost_estimate=pl.CostEstimate(
            flops=2 * rows * (width - half) * (2 * rows + patch_width),
            bytes_accessed=10 * rows * width + (width - half) * patch_width * 2,
            transcendentals=features.size,
        ),
    )(
        weights, base, inverse, v_r2, v_s2, w_near, first, begun,
        place_matrix, f_near, norm_gain.reshape(1, channels),
    )

    halo = move(activated, perm=[(s, s + 1) for s in range(count - 1)])

    moved = [pltpu.VMEM((TAPS * channels, pixels), jnp.bfloat16)] * 2
    conv_cost = pl.CostEstimate(
        flops=2 * channels * TAPS * channels * pixels * 3,
        bytes_accessed=conv_weight.size * 2 + shift_matrix.size * 2,
        transcendentals=0,
    )
    part, wide = pl.pallas_call(
        conv_own_kernel,
        out_shape=(
            jax.ShapeDtypeStruct(features.shape, jnp.float32),
            jax.ShapeDtypeStruct((2, channels, TAPS * channels), jnp.bfloat16),
        ),
        in_specs=[VMEM] * 3,
        out_specs=(VMEM,) * 2,
        scratch_shapes=moved,
        compiler_params=params(),
        name="conv_own",
        cost_estimate=conv_cost,
    )(activated, shift_matrix, conv_weight)
    decoded = pl.pallas_call(
        conv_halo_kernel,
        out_shape=jax.ShapeDtypeStruct(features.shape, jnp.bfloat16),
        in_specs=[VMEM] * 5,
        out_specs=VMEM,
        scratch_shapes=moved,
        compiler_params=params(),
        name="conv_halo",
        cost_estimate=conv_cost,
    )(halo, shift_matrix, wide, part, latent)
    return (attended, decoded)


def solution(mesh):
    placed = (
        P(("groups", "span"), None),
        P(("groups", "span"), None),
        P(("groups", "span"), None),
        P(("groups", "span")),
        P(),
        P(("groups", "span"), None, None),
        P(),
        P(),
    )
    return jax.shard_map(
        shards,
        mesh=mesh,
        in_specs=placed,
        out_specs=(P(("groups", "span"), None), P(("groups", "span"), None, None)),
        check_vma=False,
    )
```
